32 devices in a mesh: img: 16 (over z, x, core), band: 2 (over y).
Axes of the slice: x: 2, y: 2, z: 4, core: 2. Of those that a mesh axis runs over, the one named last changes fastest.
Arguments:
- latents: bfloat16 [32, 1024, 1152], P('img', 'band'), may hold values from -6 to 6
- cotangent: bfloat16 [32, 1024, 1152], P('img', 'band'), may hold values from -6 to 6
- labels: int32 [32], P('img'), may hold values from 0 to 999
- group_ids: int32 [32], P('img'), may hold values from 0 to 7
- group_logits: float32 [8], replicated, may hold values from -4 to 4
- row_pos: int32 [1024], P('band'), may hold values from 0 to 63
- col_pos: int32 [1024], P('band'), may hold values from 0 to 63
- time_weight: bfloat16 [256, 1152], replicated, may hold values from -0.375 to 0.375
- class_table: bfloat16 [1000, 1152], replicated, may hold values from -6 to 6
- ada_weight: bfloat16 [1152, 6912], replicated, may hold values from -0.1875 to 0.1875
- ada_bias: float32 [6912], replicated, may hold values from -3 to 3
- qkv_weight: bfloat16 [1152, 3456], replicated, may hold values from -0.1875 to 0.1875
- query_gain: float32 [72], replicated, may hold values from 0.1 to 1.9
- key_gain: float32 [72], replicated, may hold values from 0.1 to 1.9
- proj_weight: bfloat16 [1152, 1152], replicated, may hold values from -0.75 to 0.75
- gateup_weight: bfloat16 [1152, 6144], replicated, may hold values from -0.1875 to 0.1875
- down_weight: bfloat16 [3072, 1152], replicated, may hold values from -0.109375 to 0.109375
Outputs:
- result: bfloat16 [32, 1024, 1152], P('img', 'band')
- grad_latents: bfloat16 [32, 1024, 1152], P('img', 'band')
- grad_time: float32 [256, 1152], P('img', 'band')
- grad_class: float32 [1000, 1152], replicated
- grad_ada: float32 [1152, 6912], P('img', 'band')
- grad_ada_bias: float32 [6912], replicated
- grad_qkv: float32 [1152, 3456], P('img', 'band')
- grad_query_gain: float32 [72], replicated
- grad_key_gain: float32 [72], replicated
- grad_proj: float32 [1152, 1152], P('img', 'band')
- grad_gateup: float32 [1152, 6144], P('img', 'band')
- grad_down: float32 [3072, 1152], P('img', 'band')
The draws below stay inside these ranges and needn't reach their ends.
All inputs are finite; a program needn't handle non-finite values.
Results may differ from the reference program's by a relative error of at most 0.018.
Values may be sent and summed in bfloat16 or wider, within the bound.
A program may use at most 384 MiB of HBM per device.

```python
import math
import jax
import jax.numpy as jnp
import numpy as np
from jax import lax

D = 1152
HEADS = 16
HD = 72
FF = 3072
NCLASS = 1000
FREQ = 256
GRID = 32
GROUPS = 8
PATCHES = 1024
IMAGES = 32


def touch_ends(array, stream_key, smallest, high):
    spot = [jax.random.randint(jax.random.fold_in(stream_key, axis), (), 0, length) for axis, length in enumerate(array.shape)]
    main_axis = array.shape.index(max(array.shape))
    beside = spot[:main_axis] + [(spot[main_axis] + 1) % array.shape[main_axis]] + spot[main_axis + 1:]
    return array.at[tuple(spot)].set(smallest).at[tuple(beside)].set(high)


def block_levels(own_key, shape, split, smallest, high):
    def one(dim, shards_of):
        draws = jax.random.uniform(jax.random.fold_in(jax.random.fold_in(own_key, 6), dim), (shards_of,), jnp.float32, smallest / len(split), high / len(split))
        return jnp.repeat(jnp.exp(draws), shape[dim] // shards_of).reshape((-1,) + (1,) * (len(shape) - dim - 1))

    factor_of = one(*split[0])
    for cut in split[1:]:
        factor_of = factor_of * one(*cut)
    return factor_of


def rank_table(count, lean):
    loads = [(1 << 20) // math.isqrt(grade ** lean) + 1 for grade in range(1, count + 1)]
    spread = 1 + sum(loads) // (1 << 30)
    return np.cumsum(np.array([max(1, weight // spread) for weight in loads]))


def ranked(rng, extent, amount, slope):
    listing = rank_table(amount, slope)
    lot = jax.random.randint(jax.random.fold_in(rng, 1), extent, 0, int(listing[amount - 1]))
    standing = jnp.searchsorted(jnp.asarray(listing, jnp.int32), lot, side="right")
    return jax.random.permutation(jax.random.fold_in(rng, 2), amount)[standing].astype(jnp.int32)


def centred(rng, shape, deviation, most, split=(), kind=jnp.bfloat16):
    values = jax.random.normal(rng, shape, jnp.float32) * deviation
    if len(split) > 0:
        values = block_levels(rng, shape, split, -0.22, 0.18) * values
    return jnp.clip(values, min=-most, max=most).astype(kind)


def setup_inputs(seed: int = 0) -> dict:
    seeds = jax.random.split(jax.random.key(seed), 18)
    return {
        "latents": centred(seeds[0], (IMAGES, PATCHES, D), 1.0, 6.0, ((0, 16), (1, 2))),
        "cotangent": centred(seeds[1], (IMAGES, PATCHES, D), 1.0, 6.0, ((0, 16), (1, 2))),
        "labels": touch_ends(jax.random.randint(seeds[2], (IMAGES,), 0, NCLASS), jax.random.fold_in(seeds[2], 1), 0, NCLASS - 1).astype(jnp.int32),
        "group_ids": touch_ends(ranked(seeds[3], (IMAGES,), GROUPS, 2), jax.random.fold_in(seeds[3], 3), 0, GROUPS - 1).astype(jnp.int32),
        "group_logits": centred(seeds[4], (GROUPS,), 1.0, 4.0, (), jnp.float32),
        "row_pos": touch_ends(jax.random.randint(seeds[5], (PATCHES,), 0, 2 * GRID), jax.random.fold_in(seeds[5], 1), 0, (2 * GRID) - 1).astype(jnp.int32),
        "col_pos": touch_ends(jax.random.randint(seeds[6], (PATCHES,), 0, 2 * GRID), jax.random.fold_in(seeds[6], 1), 0, (2 * GRID) - 1).astype(jnp.int32),
        "time_weight": centred(seeds[7], (FREQ, D), FREQ ** -0.5, 0.375),
        "class_table": centred(seeds[8], (NCLASS, D), 1.0, 6.0),
        "ada_weight": centred(seeds[9], (D, 6 * D), D ** -0.5, 0.1875),
        "ada_bias": centred(seeds[10], (6 * D,), 0.5, 3.0, (), jnp.float32),
        "qkv_weight": centred(seeds[11], (D, 3 * D), D ** -0.5, 0.1875),
        "query_gain": jnp.clip(1.0 + 0.18 * jax.random.normal(seeds[12], (HD,), jnp.float32), 0.1, 1.9),
        "key_gain": jnp.clip(1.0 + 0.18 * jax.random.normal(seeds[13], (HD,), jnp.float32), 0.1, 1.9),
        "proj_weight": centred(seeds[14], (D, D), (D // 16) ** -0.5, 0.75),
        "gateup_weight": centred(seeds[15], (D, 2 * FF), D ** -0.5, 0.1875),
        "down_weight": centred(seeds[16], (FF, D), FF ** -0.5, 0.109375),
    }


highest = lax.Precision.HIGHEST
epsilon = 1e-06
per_step = 4

@jax.custom_vjp
def low(v):
    return lax.optimization_barrier(v.astype(jnp.bfloat16)).astype(jnp.float32)

@jax.custom_vjp
def low_back(v):
    return v

def low_keep(v):
    return (low(v), None)

def low_pass(kept, grad):
    return (grad,)

def back_keep(v):
    return (v, None)

def back_low(kept, grad):
    return (low(grad),)
low.defvjp(low_keep, low_pass)
low_back.defvjp(back_keep, back_low)

def unit_rms(values):
    return values * lax.rsqrt(lax.optimization_barrier(jnp.mean(values * values, axis=-1, keepdims=True)) + epsilon)

def rope_tables(row_pos, col_pos, quarter):
    frequency = jnp.exp(-math.log(10000.0) * jnp.arange(quarter, dtype=jnp.float32) / quarter)
    row_angle = row_pos.astype(jnp.float32)[:, None] * frequency[None, :]
    col_angle = col_pos.astype(jnp.float32)[:, None] * frequency[None, :]
    cosine = jnp.concatenate([jnp.cos(row_angle), jnp.cos(row_angle), jnp.cos(col_angle), jnp.cos(col_angle)], axis=-1)
    sine = jnp.concatenate([-jnp.sin(row_angle), jnp.sin(row_angle), -jnp.sin(col_angle), jnp.sin(col_angle)], axis=-1)
    return (cosine, sine)

def partner(values, quarter):
    return jnp.concatenate([values[..., quarter:2 * quarter], values[..., :quarter], values[..., 3 * quarter:], values[..., 2 * quarter:3 * quarter]], axis=-1)

def time_features(times, half):
    frequency = jnp.exp(-math.log(10000.0) * jnp.arange(half, dtype=jnp.float32) / half)
    angles = 1000.0 * times[:, None] * frequency[None, :]
    return jnp.concatenate([jnp.cos(angles), jnp.sin(angles)], axis=-1)

def reference(latents, cotangent, labels, group_ids, group_logits, row_pos, col_pos, time_weight, class_table, ada_weight, ada_bias, qkv_weight, query_gain, key_gain, proj_weight, gateup_weight, down_weight):
    quarter = HD // 4
    scaling = HD ** (-0.5)
    cosine, sine = rope_tables(row_pos, col_pos, quarter)
    cosine = cosine[None, :, None, :]
    sine = sine[None, :, None, :]
    group_hot = (group_ids[:, None] == jnp.arange(GROUPS, dtype=jnp.int32)[None, :]).astype(jnp.float32)
    times = jax.nn.sigmoid(jnp.dot(group_hot, group_logits.astype(jnp.float32), precision=highest))
    features = low(time_features(times, FREQ // 2))
    class_hot = (labels[:, None] == jnp.arange(NCLASS, dtype=jnp.int32)[None, :]).astype(jnp.float32)
    params = tuple((weight.astype(jnp.float32) for weight in (time_weight, class_table, ada_weight, ada_bias, qkv_weight, query_gain, key_gain, proj_weight, gateup_weight, down_weight)))
    source = latents.astype(jnp.float32)

    def turned(values):
        return values * cosine + partner(values, quarter) * sine

    def forward(weights, source):
        time_matrix, class_rows, ada_matrix, ada_shift, qkv_matrix, query_scale, key_scale, proj_matrix, gateup_matrix, down_matrix = weights
        before = jnp.dot(features, time_matrix, precision=highest) + jnp.dot(class_hot, class_rows, precision=highest)
        condition = low(jax.nn.silu(before))
        modulation = jnp.dot(condition, ada_matrix, precision=highest) + ada_shift

        def block(pair):
            portion, modes = pair
            pieces = [modes[:, None, member * D:(member + 1) * D] for member in range(6)]
            shift_one, scale_one, gate_one, shift_two, scale_two, gate_two = pieces
            entry_one = low(unit_rms(portion) * (1.0 + scale_one) + shift_one)
            projected = low_back(jnp.einsum('bpd,de->bpe', entry_one, qkv_matrix, precision=highest))
            shape = (portion.shape[0], PATCHES, HEADS, HD)
            query_raw = projected[..., :D].reshape(shape)
            key_raw = projected[..., D:2 * D].reshape(shape)
            value = low(projected[..., 2 * D:].reshape(shape))
            query = low(turned(unit_rms(query_raw) * query_scale))
            key = low(turned(unit_rms(key_raw) * key_scale))
            scores = low_back(jnp.einsum('bqhd,bkhd->bhqk', query, key, precision=highest) * scaling)
            probs = low(jax.nn.softmax(scores, axis=-1))
            mixed = jnp.einsum('bhqk,bkhd->bqhd', probs, value, precision=highest)
            mixed = low(low_back(mixed.reshape(portion.shape[0], PATCHES, D)))
            attended = low_back(jnp.einsum('bpd,de->bpe', mixed, proj_matrix, precision=highest))
            middle = portion + gate_one * attended
            entry_two = low(unit_rms(middle) * (1.0 + scale_two) + shift_two)
            gate_up = low_back(jnp.einsum('bpd,de->bpe', entry_two, gateup_matrix, precision=highest))
            hidden = low(jax.nn.silu(gate_up[..., :FF]) * gate_up[..., FF:])
            fed = low_back(jnp.einsum('bpf,fd->bpd', hidden, down_matrix, precision=highest))
            return middle + gate_two * fed
        stacked = source.reshape(IMAGES // per_step, per_step, PATCHES, D)
        modes = modulation.reshape(IMAGES // per_step, per_step, 6 * D)
        outputs = lax.map(jax.checkpoint(block), (stacked, modes))
        return outputs.reshape(IMAGES, PATCHES, D)
    output, pullback = jax.vjp(forward, params, source)
    grads, source_grad = pullback(cotangent.astype(jnp.float32))
    return (output.astype(jnp.bfloat16), source_grad.astype(jnp.bfloat16), grads[0], grads[1], grads[2], grads[3], grads[4], grads[5], grads[6], grads[7], grads[8], grads[9])
```

```python
import math

import jax
import jax.numpy as jnp
from jax import lax
from jax.experimental import pallas as pl
from jax.experimental.pallas import tpu as pltpu
from jax.sharding import PartitionSpec as P

HEADS = 16
HD = 72
FF = 3072
NCLASS = 1000
FREQ = 256
GROUPS = 8


highest = lax.Precision.HIGHEST
epsilon = 1e-06


def unit_rms(values):
    return values * lax.rsqrt(jnp.mean(values * values, axis=-1, keepdims=True) + epsilon)


def unit_rms_back(values, grads):
    factor = lax.rsqrt(jnp.mean(values * values, axis=-1, keepdims=True) + epsilon)
    normed = values * factor
    return factor * (grads - normed * jnp.mean(grads * normed, axis=-1, keepdims=True))


def rope_tables(row_pos, col_pos, quarter):
    frequency = jnp.exp(-math.log(10000.0) * jnp.arange(quarter, dtype=jnp.float32) / quarter)
    row_angle = row_pos.astype(jnp.float32)[:, None] * frequency[None, :]
    col_angle = col_pos.astype(jnp.float32)[:, None] * frequency[None, :]
    cosine = jnp.concatenate(
        [jnp.cos(row_angle), jnp.cos(row_angle), jnp.cos(col_angle), jnp.cos(col_angle)], axis=-1
    )
    sine = jnp.concatenate(
        [-jnp.sin(row_angle), jnp.sin(row_angle), -jnp.sin(col_angle), jnp.sin(col_angle)], axis=-1
    )
    return (cosine, sine)


def partner(values, quarter):
    return jnp.concatenate(
        [
            values[..., quarter : 2 * quarter],
            values[..., :quarter],
            values[..., 3 * quarter :],
            values[..., 2 * quarter : 3 * quarter],
        ],
        axis=-1,
    )


def time_features(times, half):
    frequency = jnp.exp(-math.log(10000.0) * jnp.arange(half, dtype=jnp.float32) / half)
    angles = 1000.0 * times[:, None] * frequency[None, :]
    return jnp.concatenate([jnp.cos(angles), jnp.sin(angles)], axis=-1)


def silu_slope(values):
    sigma = jax.nn.sigmoid(values)
    return sigma * (1.0 + values * (1.0 - sigma))


def per_device_banded(
    latents,
    cotangent,
    labels,
    group_ids,
    group_logits,
    row_pos,
    col_pos,
    time_weight,
    class_table,
    ada_weight,
    ada_bias,
    qkv_weight,
    query_gain,
    key_gain,
    proj_weight,
    gateup_weight,
    down_weight,
):
    images, rows, width = latents.shape
    quarter = HD // 4
    scaling = HD ** (-0.5)
    group_hot = (group_ids[:, None] == jnp.arange(GROUPS, dtype=jnp.int32)[None, :]).astype(
        jnp.float32
    )
    times = jax.nn.sigmoid(jnp.dot(group_hot, group_logits, precision=highest))
    features = time_features(times, FREQ // 2).astype(jnp.bfloat16)
    class_hot = (labels[:, None] == jnp.arange(NCLASS, dtype=jnp.int32)[None, :]).astype(
        jnp.bfloat16
    )
    before = jnp.dot(features, time_weight, preferred_element_type=jnp.float32) + jnp.dot(
        class_hot, class_table, preferred_element_type=jnp.float32
    )
    condition = jax.nn.silu(before).astype(jnp.bfloat16)
    modulation = jnp.dot(condition, ada_weight, preferred_element_type=jnp.float32) + ada_bias
    pieces = [modulation[:, None, member * width : (member + 1) * width] for member in range(6)]
    shift_one, scale_one, gate_one, shift_two, scale_two, gate_two = pieces
    cosine, sine = rope_tables(row_pos, col_pos, quarter)
    cosine = cosine[None, :, None, :]
    sine = sine[None, :, None, :]

    def turned(values):
        return values * cosine + partner(values, quarter) * sine

    def turned_back(grads):
        return grads * cosine + partner(grads * sine, quarter)

    source = latents.astype(jnp.float32)
    normed_one = unit_rms(source)
    entry_one = (normed_one * (1.0 + scale_one) + shift_one).astype(jnp.bfloat16)
    projected = jnp.einsum("bpd,de->bpe", entry_one, qkv_weight, preferred_element_type=jnp.float32)
    shape = (images, rows, HEADS, HD)
    query_raw = projected[..., :width].reshape(shape)
    key_raw = projected[..., width : 2 * width].reshape(shape)
    value_bf = projected[..., 2 * width :].reshape(shape).astype(jnp.bfloat16)
    query_unit = unit_rms(query_raw)
    key_unit = unit_rms(key_raw)
    query_bf = turned(query_unit * query_gain).astype(jnp.bfloat16)
    key_bf = turned(key_unit * key_gain).astype(jnp.bfloat16)
    peak = jnp.full((images, HEADS, rows), -1e30, jnp.float32)
    key_piece = lax.all_gather(key_bf, "band", axis=1, tiled=True)
    value_piece = lax.all_gather(value_bf, "band", axis=1, tiled=True)
    scores = (
        jnp.einsum("bqhd,bkhd->bhqk", query_bf, key_piece, preferred_element_type=jnp.float32)
        * scaling
    )
    new_peak = jnp.maximum(peak, jnp.max(scores, axis=-1))
    weights = jnp.exp(scores - new_peak[..., None])
    total = jnp.sum(weights, axis=-1)
    update = jnp.einsum(
        "bhqk,bkhd->bqhd",
        weights.astype(jnp.bfloat16),
        value_piece,
        preferred_element_type=jnp.float32,
    )
    accum = update
    peak, total, accum = (new_peak, total, accum)
    mixed = accum / jnp.transpose(total, (0, 2, 1))[..., None]
    log_total = peak + jnp.log(total)
    mixed_bf = mixed.reshape(images, rows, width).astype(jnp.bfloat16)
    attended = jnp.einsum("bpd,de->bpe", mixed_bf, proj_weight, preferred_element_type=jnp.float32)
    middle = source + gate_one * attended
    normed_two = unit_rms(middle)
    entry_two = (normed_two * (1.0 + scale_two) + shift_two).astype(jnp.bfloat16)
    gate_up = jnp.einsum(
        "bpd,de->bpe", entry_two, gateup_weight, preferred_element_type=jnp.float32
    )
    gate_part = gate_up[..., :FF]
    up_part = gate_up[..., FF:]
    hidden = (jax.nn.silu(gate_part) * up_part).astype(jnp.bfloat16)
    fed = jnp.einsum("bpf,fd->bpd", hidden, down_weight, preferred_element_type=jnp.float32)
    result = (middle + gate_two * fed).astype(jnp.bfloat16)
    upstream = cotangent.astype(jnp.float32)
    fed_grad = (upstream * gate_two).astype(jnp.bfloat16)
    grad_gate_two = jnp.sum(upstream * fed, axis=1)
    grad_down = jnp.einsum("bpf,bpd->fd", hidden, fed_grad, preferred_element_type=jnp.float32)
    hidden_grad = jnp.einsum(
        "bpd,fd->bpf", fed_grad, down_weight, preferred_element_type=jnp.float32
    )
    gate_grad = hidden_grad * up_part * silu_slope(gate_part)
    up_grad = hidden_grad * jax.nn.silu(gate_part)
    gate_up_grad = jnp.concatenate([gate_grad, up_grad], axis=-1).astype(jnp.bfloat16)
    grad_gateup = jnp.einsum(
        "bpd,bpe->de", entry_two, gate_up_grad, preferred_element_type=jnp.float32
    )
    entry_two_grad = jnp.einsum(
        "bpe,de->bpd", gate_up_grad, gateup_weight, preferred_element_type=jnp.float32
    )
    grad_scale_two = jnp.sum(entry_two_grad * normed_two, axis=1)
    grad_shift_two = jnp.sum(entry_two_grad, axis=1)
    middle_grad = upstream + unit_rms_back(middle, entry_two_grad * (1.0 + scale_two))
    grad_gate_one = jnp.sum(middle_grad * attended, axis=1)
    attended_grad = (middle_grad * gate_one).astype(jnp.bfloat16)
    grad_proj = jnp.einsum(
        "bpd,bpe->de", mixed_bf, attended_grad, preferred_element_type=jnp.float32
    )
    mixed_grad = jnp.einsum(
        "bpe,de->bpd", attended_grad, proj_weight, preferred_element_type=jnp.float32
    )
    mixed_grad_bf = mixed_grad.reshape(shape).astype(jnp.bfloat16)
    offsets = jnp.transpose(jnp.sum(mixed_grad_bf.astype(jnp.float32) * mixed, axis=-1), (0, 2, 1))
    key_piece = lax.all_gather(key_bf, "band", axis=1, tiled=True)
    value_piece = lax.all_gather(value_bf, "band", axis=1, tiled=True)
    scores = (
        jnp.einsum("bqhd,bkhd->bhqk", query_bf, key_piece, preferred_element_type=jnp.float32)
        * scaling
    )
    probs = jnp.exp(scores - log_total[..., None])
    prob_grad = jnp.einsum(
        "bqhd,bkhd->bhqk", mixed_grad_bf, value_piece, preferred_element_type=jnp.float32
    )
    score_grad = (probs * (prob_grad - offsets[..., None])).astype(jnp.bfloat16)
    query_grad = (
        jnp.einsum("bhqk,bkhd->bqhd", score_grad, key_piece, preferred_element_type=jnp.float32)
        * scaling
    )
    key_term = (
        jnp.einsum("bhqk,bqhd->bkhd", score_grad, query_bf, preferred_element_type=jnp.float32)
        * scaling
    )
    value_term = jnp.einsum(
        "bhqk,bqhd->bkhd",
        probs.astype(jnp.bfloat16),
        mixed_grad_bf,
        preferred_element_type=jnp.float32,
    )
    key_grads = key_term
    value_grads = value_term
    query_grad, key_grads, value_grads = (query_grad, key_grads, value_grads)
    key_local, value_local = (
        lax.psum_scatter(
            key_grads.astype(jnp.bfloat16), "band", scatter_dimension=1, tiled=True
        ).astype(jnp.float32),
        lax.psum_scatter(
            value_grads.astype(jnp.bfloat16), "band", scatter_dimension=1, tiled=True
        ).astype(jnp.float32),
    )
    query_turned = turned_back(query_grad)
    key_turned = turned_back(key_local)
    local_query_gain = jnp.sum(query_turned * query_unit, axis=(0, 1, 2))
    local_key_gain = jnp.sum(key_turned * key_unit, axis=(0, 1, 2))
    query_raw_grad = unit_rms_back(query_raw, query_turned * query_gain)
    key_raw_grad = unit_rms_back(key_raw, key_turned * key_gain)
    flat = (images, rows, width)
    projected_grad = jnp.concatenate(
        [query_raw_grad.reshape(flat), key_raw_grad.reshape(flat), value_local.reshape(flat)],
        axis=-1,
    ).astype(jnp.bfloat16)
    grad_qkv = jnp.einsum(
        "bpd,bpe->de", entry_one, projected_grad, preferred_element_type=jnp.float32
    )
    entry_one_grad = jnp.einsum(
        "bpe,de->bpd", projected_grad, qkv_weight, preferred_element_type=jnp.float32
    )
    grad_scale_one = jnp.sum(entry_one_grad * normed_one, axis=1)
    grad_shift_one = jnp.sum(entry_one_grad, axis=1)
    source_grad = middle_grad + unit_rms_back(source, entry_one_grad * (1.0 + scale_one))
    grad_latents = source_grad.astype(jnp.bfloat16)
    band_partial = jnp.concatenate(
        [
            grad_shift_one,
            grad_scale_one,
            grad_gate_one,
            grad_shift_two,
            grad_scale_two,
            grad_gate_two,
        ],
        axis=-1,
    )
    modulation_grad, band_query_gain, band_key_gain = (
        lax.psum(band_partial.astype(jnp.bfloat16), "band").astype(jnp.float32),
        lax.psum(local_query_gain[None, :].astype(jnp.bfloat16), "band").astype(jnp.float32),
        lax.psum(local_key_gain[None, :].astype(jnp.bfloat16), "band").astype(jnp.float32),
    )
    condition_grad = jnp.dot(modulation_grad, ada_weight.astype(jnp.float32).T, precision=highest)
    before_grad = condition_grad * silu_slope(before)
    condition_all, features_all, modulation_all, before_all, query_gain_rows, key_gain_rows = (
        lax.all_gather(
            condition.astype(jnp.float32).astype(jnp.bfloat16), "img", axis=0, tiled=True
        ).astype(jnp.float32),
        lax.all_gather(
            features.astype(jnp.float32).astype(jnp.bfloat16), "img", axis=0, tiled=True
        ).astype(jnp.float32),
        lax.all_gather(modulation_grad.astype(jnp.bfloat16), "img", axis=0, tiled=True).astype(
            modulation_grad.dtype
        ),
        lax.all_gather(before_grad.astype(jnp.bfloat16), "img", axis=0, tiled=True).astype(
            before_grad.dtype
        ),
        lax.all_gather(band_query_gain.astype(jnp.bfloat16), "img", axis=0, tiled=True).astype(
            band_query_gain.dtype
        ),
        lax.all_gather(band_key_gain.astype(jnp.bfloat16), "img", axis=0, tiled=True).astype(
            band_key_gain.dtype
        ),
    )
    labels_all = lax.all_gather(labels, "img", axis=0, tiled=True)
    img_index = lax.axis_index("img")
    band_index = lax.axis_index("band")
    ada_rows = width // lax.axis_size("img")
    ada_cols = 6 * width // lax.axis_size("band")
    time_rows = FREQ // lax.axis_size("img")
    time_cols = width // lax.axis_size("band")
    condition_part = lax.dynamic_slice_in_dim(condition_all, img_index * ada_rows, ada_rows, 1)
    modulation_part = lax.dynamic_slice_in_dim(modulation_all, band_index * ada_cols, ada_cols, 1)
    sum_ada = jnp.dot(condition_part.T, modulation_part, precision=highest)
    features_part = lax.dynamic_slice_in_dim(features_all, img_index * time_rows, time_rows, 1)
    before_part = lax.dynamic_slice_in_dim(before_all, band_index * time_cols, time_cols, 1)
    sum_time = jnp.dot(features_part.T, before_part, precision=highest)
    class_all = (labels_all[:, None] == jnp.arange(NCLASS, dtype=jnp.int32)[None, :]).astype(
        jnp.float32
    )
    sum_class = jnp.dot(class_all.T, before_all, precision=highest)
    sum_bias = jnp.sum(modulation_all, axis=0)
    sum_query_gain = jnp.sum(query_gain_rows, axis=0)
    sum_key_gain = jnp.sum(key_gain_rows, axis=0)
    part_qkv, part_proj, part_gateup, part_down = (
        lax.psum_scatter(
            grad_qkv.astype(jnp.bfloat16), "img", scatter_dimension=0, tiled=True
        ).astype(jnp.float32),
        lax.psum_scatter(
            grad_proj.astype(jnp.bfloat16), "img", scatter_dimension=0, tiled=True
        ).astype(jnp.float32),
        lax.psum_scatter(
            grad_gateup.astype(jnp.bfloat16), "img", scatter_dimension=0, tiled=True
        ).astype(jnp.float32),
        lax.psum_scatter(
            grad_down.astype(jnp.bfloat16), "img", scatter_dimension=0, tiled=True
        ).astype(jnp.float32),
    )
    sum_qkv, sum_proj, sum_gateup, sum_down = (
        lax.psum_scatter(
            part_qkv.astype(jnp.bfloat16), "band", scatter_dimension=1, tiled=True
        ).astype(jnp.float32),
        lax.psum_scatter(
            part_proj.astype(jnp.bfloat16), "band", scatter_dimension=1, tiled=True
        ).astype(jnp.float32),
        lax.psum_scatter(
            part_gateup.astype(jnp.bfloat16), "band", scatter_dimension=1, tiled=True
        ).astype(jnp.float32),
        lax.psum_scatter(
            part_down.astype(jnp.bfloat16), "band", scatter_dimension=1, tiled=True
        ).astype(jnp.float32),
    )
    return (
        result,
        grad_latents,
        sum_time,
        sum_class,
        sum_ada,
        sum_bias,
        sum_qkv,
        sum_query_gain,
        sum_key_gain,
        sum_proj,
        sum_gateup,
        sum_down,
    )


HDP = 80
LOG2E = math.log2(math.e)
VMEM_MAX = 62 * 2**20
bf16 = jnp.bfloat16
f32 = jnp.float32


def dot(left, right, left_dim, right_dim):
    return lax.dot_general(
        left, right, (((left_dim,), (right_dim,)), ((), ())), preferred_element_type=f32
    )


def params_of(**extra):
    return pltpu.CompilerParams(vmem_limit_bytes=VMEM_MAX, **extra)


def whole(shape):
    return pl.BlockSpec(shape, lambda *_: (0,) * len(shape), pipeline_mode=pl.Buffered(1))


def cost(flops, bytes_accessed, transcendentals=0):
    return pl.CostEstimate(
        flops=int(flops), bytes_accessed=int(bytes_accessed), transcendentals=int(transcendentals)
    )


def partner_rows(values, low_half):
    quarter = HD // 4
    return jnp.where(
        low_half, pltpu.roll(values, HD - quarter, 0), pltpu.roll(values, quarter, 0)
    )


def low_half_mask(patches):
    row = lax.broadcasted_iota(jnp.int32, (HD, patches), 0)
    quarter = HD // 4
    return (row < quarter) | ((row >= 2 * quarter) & (row < 3 * quarter))


def tail_rows(first, second, patches):
    row = lax.broadcasted_iota(jnp.int32, (HDP - HD, patches), 0)
    return jnp.where(row == 0, first, jnp.where(row == 1, second, 0.0))


def split_two(values):
    high = values.astype(bf16).astype(f32)
    return high, values - high


def front_kernel(
    x_ref, scale_ref, shift_ref, w_ref, gains_ref, cos_ref, sin_ref,
    entry_ref, heads_ref, unit_ref, factor_ref,
):
    section = pl.program_id(0)
    patches = x_ref.shape[0]

    @pl.when(section == 0)
    def _():
        source = x_ref[...].astype(f32)
        normed = source * lax.rsqrt(jnp.mean(source * source, axis=1, keepdims=True) + epsilon)
        entry_ref[...] = (normed * (1.0 + scale_ref[...]) + shift_ref[...]).astype(bf16)

    raw = dot(w_ref[...], entry_ref[...], 0, 1)

    @pl.when(section < 2)
    def _():
        mask = low_half_mask(patches)
        extra = tail_rows(*[jnp.where(section == 1, 1.0, 0.0)] * 2, patches)
        gain = gains_ref[0]
        for head in range(HEADS):
            part = raw[head * HD : (head + 1) * HD, :]
            factor = lax.rsqrt(jnp.mean(part * part, axis=0, keepdims=True) + epsilon)
            unit = part * factor
            scaled = unit * gain
            turned = scaled * cos_ref[...] + partner_rows(scaled, mask) * sin_ref[...]
            heads_ref[0, head] = jnp.concatenate([turned, extra], axis=0).astype(bf16)
            unit_ref[0, head] = unit.astype(bf16)
            factor_ref[0, head] = factor

    @pl.when(section == 2)
    def _():
        extra = tail_rows(1.0, 1.0, patches)
        for head in range(HEADS):
            part = raw[head * HD : (head + 1) * HD, :]
            heads_ref[0, head] = jnp.concatenate([part, extra], axis=0).astype(bf16)


def front(x, scale, shift, qkv_weight, gains, cosine, sine):
    patches, width = x.shape
    last = lambda s: jnp.minimum(s, 1)
    return pl.pallas_call(
        front_kernel,
        grid=(3,),
        in_specs=[
            whole((patches, width)),
            whole((1, width)),
            whole((1, width)),
            pl.BlockSpec((width, width), lambda s: (0, s)),
            pl.BlockSpec((1, HD, 1), lambda s: (last(s), 0, 0)),
            whole((HD, patches)),
            whole((HD, patches)),
        ],
        out_specs=[
            pl.BlockSpec((patches, width), lambda s: (0, 0)),
            pl.BlockSpec((1, HEADS, HDP, patches), lambda s: (s, 0, 0, 0)),
            pl.BlockSpec((1, HEADS, HD, patches), lambda s: (last(s), 0, 0, 0)),
            pl.BlockSpec((1, HEADS, 1, patches), lambda s: (last(s), 0, 0, 0)),
        ],
        out_shape=[
            jax.ShapeDtypeStruct((patches, width), bf16),
            jax.ShapeDtypeStruct((3, HEADS, HDP, patches), bf16),
            jax.ShapeDtypeStruct((2, HEADS, HD, patches), bf16),
            jax.ShapeDtypeStruct((2, HEADS, 1, patches), f32),
        ],
        compiler_params=params_of(),
        cost_estimate=cost(6 * patches * width * width, 24e6),
        name="front",
    )(x, scale, shift, qkv_weight, gains, cosine, sine)


def attend_kernel(q_ref, k_ref, v_ref, mixed_ref, lse_ref, qext_ref):
    patches = q_ref.shape[-1]
    step = patches // 2
    key = k_ref[...]
    value = v_ref[...]
    for start in range(0, patches, step):
        columns = slice(start, start + step)
        scores = dot(key, q_ref[:, columns], 0, 0)
        weights = jnp.exp2(scores).astype(bf16)
        summed = dot(value, weights, 1, 0)
        total = summed[HD : HD + 1, :]
        mixed_ref[:, columns] = (summed[:HD, :] / total).astype(bf16)
        high, low = split_two(-jnp.log2(total))
        extra = jnp.concatenate([jnp.zeros((HD, step), f32), tail_rows(high, low, step)], axis=0)
        qext_ref[:, columns] = q_ref[:, columns] + extra.astype(bf16)


def attend(heads):
    patches = heads.shape[-1]
    section = lambda member: pl.BlockSpec(
        (None, None, HDP, patches), lambda h: (member, h, 0, 0)
    )
    return pl.pallas_call(
        lambda q, k, v, mixed, qext: attend_kernel(q, k, v, mixed, None, qext),
        grid=(HEADS,),
        in_specs=[section(0), section(1), section(2)],
        out_specs=[
            pl.BlockSpec((None, HD, patches), lambda h: (h, 0, 0)),
            pl.BlockSpec((None, HDP, patches), lambda h: (h, 0, 0)),
        ],
        out_shape=[
            jax.ShapeDtypeStruct((HEADS, HD, patches), bf16),
            jax.ShapeDtypeStruct((HEADS, HDP, patches), bf16),
        ],
        compiler_params=params_of(),
        cost_estimate=cost(8 * HEADS * patches * patches * HDP, 14e6, HEADS * patches * patches),
        name="attend",
    )(heads, heads, heads)


def middle_kernel(
    mixed_ref, w_ref, x_ref, c_ref, vectors_ref, attended_ref, entry_ref, fed_grad_ref
):
    attended = dot(mixed_ref[...], w_ref[...], 0, 0)
    attended_bf = attended.astype(bf16)
    attended_ref[...] = attended_bf
    gate_one, scale_two, shift_two, gate_two = [vectors_ref[i : i + 1, :] for i in range(4)]
    middle = x_ref[...].astype(f32) + gate_one * attended_bf.astype(f32)
    normed = middle * lax.rsqrt(jnp.mean(middle * middle, axis=1, keepdims=True) + epsilon)
    entry_ref[...] = (normed * (1.0 + scale_two) + shift_two).astype(bf16)
    fed_grad_ref[...] = (c_ref[...].astype(f32) * gate_two).astype(bf16)


def middle_step(mixed, proj_weight, x, c, vectors):
    patches, width = x.shape
    rows = 256
    block = pl.BlockSpec((rows, width), lambda t: (t, 0))
    return pl.pallas_call(
        middle_kernel,
        grid=(patches // rows,),
        in_specs=[
            pl.BlockSpec((width, rows), lambda t: (0, t)),
            whole((width, width)),
            block,
            block,
            whole((8, width)),
        ],
        out_specs=[block] * 3,
        out_shape=[jax.ShapeDtypeStruct((patches, width), bf16)] * 3,
        compiler_params=params_of(),
        cost_estimate=cost(2 * patches * width * width, 17e6),
        name="middle",
    )(mixed, proj_weight, x, c, vectors)


def mlp_kernel(
    entry_ref, fed_grad_ref, wg_ref, wu_ref, wd_ref,
    fed_ref, entry_grad_ref, down_ref, gate_out_ref, up_out_ref,
    hidden_ref, gate_grad_ref, up_grad_ref,
):
    tile = pl.program_id(0)
    entry = entry_ref[...]
    fed_grad = fed_grad_ref[...]
    gate = dot(entry, wg_ref[...], 1, 0)
    up = dot(entry, wu_ref[...], 1, 0)
    sigma = jax.nn.sigmoid(gate)
    silu = gate * sigma
    hidden_ref[...] = (silu * up).astype(bf16)
    hidden_grad = dot(fed_grad, wd_ref[...], 1, 1)
    gate_grad_ref[...] = (hidden_grad * up * (sigma * (1.0 + gate * (1.0 - sigma)))).astype(bf16)
    up_grad_ref[...] = (hidden_grad * silu).astype(bf16)
    fed = dot(hidden_ref[...], wd_ref[...], 1, 0)
    entry_grad = dot(gate_grad_ref[...], wg_ref[...], 1, 1) + dot(
        up_grad_ref[...], wu_ref[...], 1, 1
    )

    @pl.when(tile == 0)
    def _():
        fed_ref[...] = fed
        entry_grad_ref[...] = entry_grad

    @pl.when(tile > 0)
    def _():
        fed_ref[...] += fed
        entry_grad_ref[...] += entry_grad

    down_ref[...] = dot(hidden_ref[...], fed_grad, 0, 0).astype(bf16)
    gate_out_ref[...] = dot(entry, gate_grad_ref[...], 0, 0).astype(bf16)
    up_out_ref[...] = dot(entry, up_grad_ref[...], 0, 0).astype(bf16)


def mlp(entry, fed_grad, gateup_weight, down_weight):
    patches, width = entry.shape
    inner = down_weight.shape[0]
    tile = 512
    tiles = inner // tile
    return pl.pallas_call(
        mlp_kernel,
        grid=(tiles,),
        in_specs=[
            whole((patches, width)),
            whole((patches, width)),
            pl.BlockSpec((width, tile), lambda t: (0, t)),
            pl.BlockSpec((width, tile), lambda t: (0, tiles + t)),
            pl.BlockSpec((tile, width), lambda t: (t, 0)),
        ],
        out_specs=[
            pl.BlockSpec((patches, width), lambda t: (0, 0)),
            pl.BlockSpec((patches, width), lambda t: (0, 0)),
            pl.BlockSpec((tile, width), lambda t: (t, 0)),
            pl.BlockSpec((width, tile), lambda t: (0, t)),
            pl.BlockSpec((width, tile), lambda t: (0, t)),
        ],
        out_shape=[
            jax.ShapeDtypeStruct((patches, width), f32),
            jax.ShapeDtypeStruct((patches, width), f32),
            jax.ShapeDtypeStruct((inner, width), bf16),
            jax.ShapeDtypeStruct((width, inner), bf16),
            jax.ShapeDtypeStruct((width, inner), bf16),
        ],
        scratch_shapes=[pltpu.VMEM((patches, tile), bf16)] * 3,
        compiler_params=params_of(),
        cost_estimate=cost(18 * patches * width * inner, 56e6),
        name="mlp",
    )(entry, fed_grad, gateup_weight, gateup_weight, down_weight)


def turn_kernel(
    fed_ref, entry_grad_ref, x_ref, attended_ref, c_ref, mixed_ref, w_ref, vectors_ref,
    result_ref, middle_grad_ref, mixed_grad_ref, grad_proj_ref, sums_ref, total_ref,
):
    step = pl.program_id(0)
    gate_one, scale_two, _, gate_two = [vectors_ref[i : i + 1, :] for i in range(4)]
    attended = attended_ref[...].astype(f32)
    upstream = c_ref[...].astype(f32)
    fed = fed_ref[...]
    middle = x_ref[...].astype(f32) + gate_one * attended
    result_ref[...] = (middle + gate_two * fed).astype(bf16)
    factor = lax.rsqrt(jnp.mean(middle * middle, axis=1, keepdims=True) + epsilon)
    normed = middle * factor
    entry_grad = entry_grad_ref[...]
    inner = entry_grad * (1.0 + scale_two)
    middle_grad = upstream + factor * (
        inner - normed * jnp.mean(inner * normed, axis=1, keepdims=True)
    )
    middle_grad_ref[...] = middle_grad
    attended_grad = (middle_grad * gate_one).astype(bf16)
    mixed_grad_ref[...] = dot(w_ref[...], attended_grad, 1, 1).astype(bf16)
    grad_proj = dot(mixed_ref[...], attended_grad, 1, 0)
    add = lambda v: jnp.sum(v, axis=0, keepdims=True)
    sums = jnp.concatenate(
        [
            add(middle_grad * attended),
            add(entry_grad),
            add(entry_grad * normed),
            add(upstream * fed),
            jnp.zeros((4, fed.shape[1]), f32),
        ],
        axis=0,
    )

    @pl.when(step == 0)
    def _():
        total_ref[...] = grad_proj
        sums_ref[...] = sums

    @pl.when(step > 0)
    def _():
        total_ref[...] += grad_proj
        sums_ref[...] += sums

    @pl.when(step == pl.num_programs(0) - 1)
    def _():
        grad_proj_ref[...] = total_ref[...].astype(bf16)


def turn_step(fed, entry_grad, x, attended, c, mixed, proj_weight, vectors):
    patches, width = x.shape
    rows = 256
    block = pl.BlockSpec((rows, width), lambda t: (t, 0))
    across = pl.BlockSpec((width, rows), lambda t: (0, t))
    return pl.pallas_call(
        turn_kernel,
        grid=(patches // rows,),
        in_specs=[block] * 5 + [across, whole((width, width)), whole((8, width))],
        out_specs=[
            block,
            block,
            across,
            pl.BlockSpec((width, width), lambda t: (0, 0)),
            pl.BlockSpec((8, width), lambda t: (0, 0)),
        ],
        out_shape=[
            jax.ShapeDtypeStruct((patches, width), bf16),
            jax.ShapeDtypeStruct((patches, width), f32),
            jax.ShapeDtypeStruct((width, patches), bf16),
            jax.ShapeDtypeStruct((width, width), bf16),
            jax.ShapeDtypeStruct((8, width), f32),
        ],
        scratch_shapes=[pltpu.VMEM((width, width), f32)],
        compiler_params=params_of(),
        cost_estimate=cost(4 * patches * width * width, 35e6),
        name="turn",
    )(fed, entry_grad, x, attended, c, mixed, proj_weight, vectors)


def attend_back_kernel(
    q_ref, k_ref, v_ref, mg_ref, mixed_ref, unit_ref, factor_ref, gains_ref, cos_ref, sin_ref,
    out_ref, gain_out_ref, mg_ext_ref, acc_ref,
):
    head = pl.program_id(0)
    patches = q_ref.shape[-1]
    step = patches // 2
    scaling = HD ** (-0.5)
    mixed_grad = mg_ref[...].astype(f32)
    offsets = jnp.sum(mixed_grad * mixed_ref[...].astype(f32), axis=0, keepdims=True)
    high, low = split_two(-offsets)
    mg_ext_ref[...] = jnp.concatenate(
        [mixed_grad, tail_rows(high, low, patches)], axis=0
    ).astype(bf16)
    key = k_ref[...]
    value = v_ref[...]
    for start in range(0, patches, step):
        columns = slice(start, start + step)
        query = q_ref[:, columns]
        grads = mg_ext_ref[:, columns]
        probs = jnp.exp2(dot(key, query, 0, 0))
        score_grad = (probs * dot(value, grads, 0, 0)).astype(bf16)
        probs_bf = probs.astype(bf16)
        acc_ref[0, :, columns] = dot(key, score_grad, 1, 0)
        key_term = dot(query, score_grad, 1, 1)
        value_term = dot(grads, probs_bf, 1, 1)
        if start == 0:
            acc_ref[1] = key_term
            acc_ref[2] = value_term
        else:
            acc_ref[1] += key_term
            acc_ref[2] += value_term
    mask = low_half_mask(patches)
    for member, weight in ((0, scaling), (1, 1.0 / LOG2E)):
        grads = acc_ref[member, :HD, :] * weight
        turned = grads * cos_ref[...] + partner_rows(grads * sin_ref[...], mask)
        unit = unit_ref[member].astype(f32)
        product = turned * unit

        @pl.when(head == 0)
        def _():
            gain_out_ref[member] = product

        @pl.when(head > 0)
        def _():
            gain_out_ref[member] += product

        inner = turned * gains_ref[member]
        raw = factor_ref[member] * (inner - unit * jnp.mean(inner * unit, axis=0, keepdims=True))
        out_ref[member] = raw.astype(bf16)
    out_ref[2] = acc_ref[2, :HD, :].astype(bf16)


def attend_back(query, heads, mixed_grad, mixed, unit, factor, gains, cosine, sine):
    patches = query.shape[-1]
    section = lambda member: pl.BlockSpec(
        (None, None, HDP, patches), lambda h: (member, h, 0, 0)
    )
    single = lambda rows: pl.BlockSpec((None, rows, patches), lambda h: (h, 0, 0))
    pair = lambda rows: pl.BlockSpec((2, None, rows, patches), lambda h: (0, h, 0, 0))
    return pl.pallas_call(
        attend_back_kernel,
        grid=(HEADS,),
        in_specs=[
            single(HDP),
            section(1),
            section(2),
            single(HD),
            single(HD),
            pair(HD),
            pair(1),
            whole((2, HD, 1)),
            whole((HD, patches)),
            whole((HD, patches)),
        ],
        out_specs=[
            pl.BlockSpec((3, None, HD, patches), lambda h: (0, h, 0, 0)),
            pl.BlockSpec((2, HD, patches), lambda h: (0, 0, 0)),
        ],
        out_shape=[
            jax.ShapeDtypeStruct((3, HEADS, HD, patches), bf16),
            jax.ShapeDtypeStruct((2, HD, patches), f32),
        ],
        scratch_shapes=[
            pltpu.VMEM((HDP, patches), bf16),
            pltpu.VMEM((3, HDP, patches), f32),
        ],
        compiler_params=params_of(),
        cost_estimate=cost(20 * HEADS * patches * patches * HDP, 32e6, HEADS * patches**2),
        name="attend_back",
    )(query, heads, heads, mixed_grad, mixed, unit, factor, gains, cosine, sine)


def back_kernel(pg_ref, w_ref, entry_ref, grad_ref, entry_grad_ref):
    section = pl.program_id(0)
    grad_ref[...] = dot(entry_ref[...], pg_ref[...], 0, 1).astype(bf16)
    term = dot(w_ref[...], pg_ref[...], 1, 0)

    @pl.when(section == 0)
    def _():
        entry_grad_ref[...] = term

    @pl.when(section > 0)
    def _():
        entry_grad_ref[...] += term


def back_step(projected_grad, qkv_weight, entry):
    patches, width = entry.shape
    return pl.pallas_call(
        back_kernel,
        grid=(3,),
        in_specs=[
            pl.BlockSpec((None, width, patches), lambda s: (s, 0, 0)),
            pl.BlockSpec((width, width), lambda s: (0, s)),
            whole((patches, width)),
        ],
        out_specs=[
            pl.BlockSpec((width, width), lambda s: (0, s)),
            pl.BlockSpec((width, patches), lambda s: (0, 0)),
        ],
        out_shape=[
            jax.ShapeDtypeStruct((width, 3 * width), bf16),
            jax.ShapeDtypeStruct((width, patches), f32),
        ],
        compiler_params=params_of(),
        cost_estimate=cost(12 * patches * width * width, 32e6),
        name="back",
    )(projected_grad, qkv_weight, entry)


def last_kernel(entry_grad_ref, x_ref, middle_grad_ref, scale_ref, out_ref, sums_ref):
    step = pl.program_id(0)
    entry_grad = entry_grad_ref[...].T
    source = x_ref[...].astype(f32)
    factor = lax.rsqrt(jnp.mean(source * source, axis=1, keepdims=True) + epsilon)
    normed = source * factor
    inner = entry_grad * (1.0 + scale_ref[...])
    grads = middle_grad_ref[...] + factor * (
        inner - normed * jnp.mean(inner * normed, axis=1, keepdims=True)
    )
    out_ref[...] = grads.astype(bf16)
    add = lambda v: jnp.sum(v, axis=0, keepdims=True)
    sums = jnp.concatenate(
        [add(entry_grad), add(entry_grad * normed), jnp.zeros((6, source.shape[1]), f32)], axis=0
    )

    @pl.when(step == 0)
    def _():
        sums_ref[...] = sums

    @pl.when(step > 0)
    def _():
        sums_ref[...] += sums


def last_step(entry_grad, x, middle_grad, scale):
    patches, width = x.shape
    rows = 256
    block = pl.BlockSpec((rows, width), lambda t: (t, 0))
    return pl.pallas_call(
        last_kernel,
        grid=(patches // rows,),
        in_specs=[
            pl.BlockSpec((width, rows), lambda t: (0, t)),
            block,
            block,
            whole((1, width)),
        ],
        out_specs=[block, pl.BlockSpec((8, width), lambda t: (0, 0))],
        out_shape=[
            jax.ShapeDtypeStruct((patches, width), bf16),
            jax.ShapeDtypeStruct((8, width), f32),
        ],
        compiler_params=params_of(),
        cost_estimate=cost(20 * patches * width, 17e6),
        name="last",
    )(entry_grad, x, middle_grad, scale)


def pick(values, index):
    return lax.dynamic_index_in_dim(values, index, 0, keepdims=False)


def per_device_whole(
    latents,
    cotangent,
    labels,
    group_ids,
    group_logits,
    row_pos,
    col_pos,
    time_weight,
    class_table,
    ada_weight,
    ada_bias,
    qkv_weight,
    query_gain,
    key_gain,
    proj_weight,
    gateup_weight,
    down_weight,
):
    width = latents.shape[-1]
    bands = lax.axis_size("band")
    img_index = lax.axis_index("img")
    band_index = lax.axis_index("band")
    half = latents.shape[1]

    def exchange(own):
        parts = [pick(own, band_index)]
        for shift in range(1, bands):
            pairs = [(i, (i + shift) % bands) for i in range(bands)]
            away = pick(own, lax.rem(band_index + shift, bands))
            parts.append(lax.ppermute(away, "band", pairs))
        return jnp.concatenate(parts, axis=0)

    def give_back(values):
        back = [values[:half]]
        for shift in range(1, bands):
            pairs = [(i, (i - shift) % bands) for i in range(bands)]
            back.append(
                lax.ppermute(values[shift * half : (shift + 1) * half], "band", pairs)
            )
        stacked = jnp.stack(back)
        order = lax.rem(jnp.arange(bands) - band_index + bands, bands)
        return jnp.take(stacked, order, axis=0)

    x = exchange(latents)
    c = exchange(cotangent)
    places = jnp.stack([row_pos, col_pos], axis=1)
    place_parts = [places]
    for shift in range(1, bands):
        pairs = [(i, (i + shift) % bands) for i in range(bands)]
        place_parts.append(lax.ppermute(places, "band", pairs))
    places = jnp.concatenate(place_parts, axis=0)

    quarter = HD // 4
    frequency = jnp.exp(-math.log(10000.0) * jnp.arange(quarter, dtype=f32) / quarter)
    angles = frequency[:, None] * places.astype(f32).T[:, None, :]
    cosine, sine = jnp.cos(angles), jnp.sin(angles)
    cosine = jnp.concatenate([cosine[0], cosine[0], cosine[1], cosine[1]], axis=0)
    sine = jnp.concatenate([-sine[0], sine[0], -sine[1], sine[1]], axis=0)

    def condition_of(group_ids, labels):
        group_hot = (group_ids[:, None] == jnp.arange(GROUPS, dtype=jnp.int32)[None, :]).astype(f32)
        times = jax.nn.sigmoid(jnp.dot(group_hot, group_logits, precision=highest))
        features = time_features(times, FREQ // 2).astype(bf16)
        before = jnp.dot(features, time_weight, preferred_element_type=f32) + jnp.take(
            class_table, labels, axis=0
        ).astype(f32)
        return features, before, jax.nn.silu(before).astype(bf16)

    own_group = pick(group_ids, band_index)[None]
    own_label = pick(labels, band_index)[None]
    _, _, condition = condition_of(own_group, own_label)
    modulation = jnp.dot(condition, ada_weight, preferred_element_type=f32) + ada_bias
    modes = modulation.reshape(6, width)
    shift_one, scale_one = modes[0:1], modes[1:2]
    vectors = jnp.concatenate([modes[2:3], modes[4:5], modes[3:4], modes[5:6], modes[2:6]], axis=0)

    scaling = HD ** (-0.5)
    gains = jnp.stack([query_gain, key_gain])[:, :, None]
    scaled_gains = gains * jnp.array([scaling * LOG2E, 1.0], f32)[:, None, None]
    entry_one, heads, unit, factor = front(
        x, scale_one, shift_one, qkv_weight, scaled_gains, cosine, sine
    )
    mixed, query = attend(heads)
    patches = x.shape[0]
    mixed_flat = mixed.reshape(width, patches)
    attended, entry_two, fed_grad = middle_step(mixed_flat, proj_weight, x, c, vectors)
    fed, entry_two_grad, grad_down, grad_gate, grad_up = mlp(
        entry_two, fed_grad, gateup_weight, down_weight
    )
    result, middle_grad, mixed_grad, grad_proj, sums_two = turn_step(
        fed, entry_two_grad, x, attended, c, mixed_flat, proj_weight, vectors
    )
    projected_grad, gain_terms = attend_back(
        query, heads, mixed_grad.reshape(HEADS, HD, patches), mixed, unit, factor, gains,
        cosine, sine,
    )
    grad_qkv, entry_one_grad = back_step(
        projected_grad.reshape(3, width, patches), qkv_weight, entry_one
    )
    grad_latents, sums_one = last_step(entry_one_grad, x, middle_grad, scale_one)

    everything = ("img", "band")
    own_grad = jnp.concatenate(
        [
            sums_one[0],
            sums_one[1],
            sums_two[0],
            sums_two[1],
            sums_two[2],
            sums_two[3],
            jnp.sum(gain_terms, axis=2).reshape(-1),
        ]
    ).astype(bf16)
    gathered = lax.all_gather(own_grad[None], everything, axis=0, tiled=True)
    codes = lax.all_gather(
        jnp.stack([group_ids, labels], axis=1), "img", axis=0, tiled=True
    )
    modulation_all = gathered[:, : 6 * width]
    gain_sums = jnp.sum(gathered[:, 6 * width :].astype(f32), axis=0)
    sum_query_gain, sum_key_gain = gain_sums[:HD], gain_sums[HD:]
    features_all, before_all, condition_all = condition_of(codes[:, 0], codes[:, 1])
    before_grad = lax.dot_general(
        modulation_all, ada_weight, (((1,), (1,)), ((), ())), preferred_element_type=f32
    ) * silu_slope(before_all)
    ada_rows = width // lax.axis_size("img")
    ada_cols = 6 * width // bands
    time_rows = FREQ // lax.axis_size("img")
    time_cols = width // bands
    condition_part = lax.dynamic_slice_in_dim(condition_all, img_index * ada_rows, ada_rows, 1)
    modulation_part = lax.dynamic_slice_in_dim(modulation_all, band_index * ada_cols, ada_cols, 1)
    sum_ada = jnp.dot(condition_part.T, modulation_part, preferred_element_type=f32)
    features_part = lax.dynamic_slice_in_dim(features_all, img_index * time_rows, time_rows, 1)
    before_part = lax.dynamic_slice_in_dim(before_grad, band_index * time_cols, time_cols, 1)
    sum_time = jnp.dot(features_part.astype(f32).T, before_part, precision=highest)
    class_all = (codes[:, 1][:, None] == jnp.arange(NCLASS, dtype=jnp.int32)[None, :]).astype(f32)
    sum_class = jnp.dot(class_all.T, before_grad, precision=highest)
    sum_bias = jnp.sum(modulation_all.astype(f32), axis=0)

    def scattered(grad, dim):
        part = lax.psum_scatter(grad, "img", scatter_dimension=0, tiled=True)
        return part

    part_down = scattered(grad_down, 0)
    part_gate = scattered(grad_gate, 0)
    part_up = scattered(grad_up, 0)
    part_gateup = jnp.concatenate([part_gate, part_up], axis=1)
    part_proj = scattered(grad_proj, 0)
    part_qkv = scattered(grad_qkv, 0)
    sum_qkv, sum_proj, sum_gateup, sum_down = [
        lax.psum_scatter(part, "band", scatter_dimension=1, tiled=True).astype(f32)
        for part in (part_qkv, part_proj, part_gateup, part_down)
    ]
    return (
        give_back(result),
        give_back(grad_latents),
        sum_time,
        sum_class,
        sum_ada,
        sum_bias,
        sum_qkv,
        sum_query_gain,
        sum_key_gain,
        sum_proj,
        sum_gateup,
        sum_down,
    )


def per_device(latents, *others):
    if latents.shape[0] == lax.axis_size("band"):
        return per_device_whole(latents, *others)
    return per_device_banded(latents, *others)


def solution(mesh):
    return jax.shard_map(
        per_device,
        mesh=mesh,
        in_specs=(
            P("img", "band", None),
            P("img", "band", None),
            P("img"),
            P("img"),
            P(),
            P("band"),
            P("band"),
            P(),
            P(),
            P(),
            P(),
            P(),
            P(),
            P(),
            P(),
            P(),
            P(),
        ),
        out_specs=(
            P("img", "band", None),
            P("img", "band", None),
            P("img", "band"),
            P(),
            P("img", "band"),
            P(),
            P("img", "band"),
            P(),
            P(),
            P("img", "band"),
            P("img", "band"),
            P("img", "band"),
        ),
        check_vma=False,
    )
```

```python
import functools
import math

import jax
import jax.numpy as jnp
from jax import lax
from jax.experimental import pallas as pl
from jax.experimental.pallas import tpu as pltpu
from jax.sharding import PartitionSpec as P

HEADS = 16
HD = 72
FF = 3072
NCLASS = 1000
FREQ = 256
GROUPS = 8


highest = lax.Precision.HIGHEST
epsilon = 1e-06


def unit_rms(values):
    return values * lax.rsqrt(jnp.mean(values * values, axis=-1, keepdims=True) + epsilon)


def unit_rms_back(values, grads):
    factor = lax.rsqrt(jnp.mean(values * values, axis=-1, keepdims=True) + epsilon)
    normed = values * factor
    return factor * (grads - normed * jnp.mean(grads * normed, axis=-1, keepdims=True))


def rope_tables(row_pos, col_pos, quarter):
    frequency = jnp.exp(-math.log(10000.0) * jnp.arange(quarter, dtype=jnp.float32) / quarter)
    row_angle = row_pos.astype(jnp.float32)[:, None] * frequency[None, :]
    col_angle = col_pos.astype(jnp.float32)[:, None] * frequency[None, :]
    cosine = jnp.concatenate(
        [jnp.cos(row_angle), jnp.cos(row_angle), jnp.cos(col_angle), jnp.cos(col_angle)], axis=-1
    )
    sine = jnp.concatenate(
        [-jnp.sin(row_angle), jnp.sin(row_angle), -jnp.sin(col_angle), jnp.sin(col_angle)], axis=-1
    )
    return (cosine, sine)


def partner(values, quarter):
    return jnp.concatenate(
        [
            values[..., quarter : 2 * quarter],
            values[..., :quarter],
            values[..., 3 * quarter :],
            values[..., 2 * quarter : 3 * quarter],
        ],
        axis=-1,
    )


def time_features(times, half):
    frequency = jnp.exp(-math.log(10000.0) * jnp.arange(half, dtype=jnp.float32) / half)
    angles = 1000.0 * times[:, None] * frequency[None, :]
    return jnp.concatenate([jnp.cos(angles), jnp.sin(angles)], axis=-1)


def silu_slope(values):
    sigma = jax.nn.sigmoid(values)
    return sigma * (1.0 + values * (1.0 - sigma))


def per_device_banded(
    latents,
    cotangent,
    labels,
    group_ids,
    group_logits,
    row_pos,
    col_pos,
    time_weight,
    class_table,
    ada_weight,
    ada_bias,
    qkv_weight,
    query_gain,
    key_gain,
    proj_weight,
    gateup_weight,
    down_weight,
):
    images, rows, width = latents.shape
    quarter = HD // 4
    scaling = HD ** (-0.5)
    group_hot = (group_ids[:, None] == jnp.arange(GROUPS, dtype=jnp.int32)[None, :]).astype(
        jnp.float32
    )
    times = jax.nn.sigmoid(jnp.dot(group_hot, group_logits, precision=highest))
    features = time_features(times, FREQ // 2).astype(jnp.bfloat16)
    class_hot = (labels[:, None] == jnp.arange(NCLASS, dtype=jnp.int32)[None, :]).astype(
        jnp.bfloat16
    )
    before = jnp.dot(features, time_weight, preferred_element_type=jnp.float32) + jnp.dot(
        class_hot, class_table, preferred_element_type=jnp.float32
    )
    condition = jax.nn.silu(before).astype(jnp.bfloat16)
    modulation = jnp.dot(condition, ada_weight, preferred_element_type=jnp.float32) + ada_bias
    pieces = [modulation[:, None, member * width : (member + 1) * width] for member in range(6)]
    shift_one, scale_one, gate_one, shift_two, scale_two, gate_two = pieces
    cosine, sine = rope_tables(row_pos, col_pos, quarter)
    cosine = cosine[None, :, None, :]
    sine = sine[None, :, None, :]

    def turned(values):
        return values * cosine + partner(values, quarter) * sine

    def turned_back(grads):
        return grads * cosine + partner(grads * sine, quarter)

    source = latents.astype(jnp.float32)
    normed_one = unit_rms(source)
    entry_one = (normed_one * (1.0 + scale_one) + shift_one).astype(jnp.bfloat16)
    projected = jnp.einsum("bpd,de->bpe", entry_one, qkv_weight, preferred_element_type=jnp.float32)
    shape = (images, rows, HEADS, HD)
    query_raw = projected[..., :width].reshape(shape)
    key_raw = projected[..., width : 2 * width].reshape(shape)
    value_bf = projected[..., 2 * width :].reshape(shape).astype(jnp.bfloat16)
    query_unit = unit_rms(query_raw)
    key_unit = unit_rms(key_raw)
    query_bf = turned(query_unit * query_gain).astype(jnp.bfloat16)
    key_bf = turned(key_unit * key_gain).astype(jnp.bfloat16)
    peak = jnp.full((images, HEADS, rows), -1e30, jnp.float32)
    key_piece = lax.all_gather(key_bf, "band", axis=1, tiled=True)
    value_piece = lax.all_gather(value_bf, "band", axis=1, tiled=True)
    scores = (
        jnp.einsum("bqhd,bkhd->bhqk", query_bf, key_piece, preferred_element_type=jnp.float32)
        * scaling
    )
    new_peak = jnp.maximum(peak, jnp.max(scores, axis=-1))
    weights = jnp.exp(scores - new_peak[..., None])
    total = jnp.sum(weights, axis=-1)
    update = jnp.einsum(
        "bhqk,bkhd->bqhd",
        weights.astype(jnp.bfloat16),
        value_piece,
        preferred_element_type=jnp.float32,
    )
    accum = update
    peak, total, accum = (new_peak, total, accum)
    mixed = accum / jnp.transpose(total, (0, 2, 1))[..., None]
    log_total = peak + jnp.log(total)
    mixed_bf = mixed.reshape(images, rows, width).astype(jnp.bfloat16)
    attended = jnp.einsum("bpd,de->bpe", mixed_bf, proj_weight, preferred_element_type=jnp.float32)
    middle = source + gate_one * attended
    normed_two = unit_rms(middle)
    entry_two = (normed_two * (1.0 + scale_two) + shift_two).astype(jnp.bfloat16)
    gate_up = jnp.einsum(
        "bpd,de->bpe", entry_two, gateup_weight, preferred_element_type=jnp.float32
    )
    gate_part = gate_up[..., :FF]
    up_part = gate_up[..., FF:]
    hidden = (jax.nn.silu(gate_part) * up_part).astype(jnp.bfloat16)
    fed = jnp.einsum("bpf,fd->bpd", hidden, down_weight, preferred_element_type=jnp.float32)
    result = (middle + gate_two * fed).astype(jnp.bfloat16)
    upstream = cotangent.astype(jnp.float32)
    fed_grad = (upstream * gate_two).astype(jnp.bfloat16)
    grad_gate_two = jnp.sum(upstream * fed, axis=1)
    grad_down = jnp.einsum("bpf,bpd->fd", hidden, fed_grad, preferred_element_type=jnp.float32)
    hidden_grad = jnp.einsum(
        "bpd,fd->bpf", fed_grad, down_weight, preferred_element_type=jnp.float32
    )
    gate_grad = hidden_grad * up_part * silu_slope(gate_part)
    up_grad = hidden_grad * jax.nn.silu(gate_part)
    gate_up_grad = jnp.concatenate([gate_grad, up_grad], axis=-1).astype(jnp.bfloat16)
    grad_gateup = jnp.einsum(
        "bpd,bpe->de", entry_two, gate_up_grad, preferred_element_type=jnp.float32
    )
    entry_two_grad = jnp.einsum(
        "bpe,de->bpd", gate_up_grad, gateup_weight, preferred_element_type=jnp.float32
    )
    grad_scale_two = jnp.sum(entry_two_grad * normed_two, axis=1)
    grad_shift_two = jnp.sum(entry_two_grad, axis=1)
    middle_grad = upstream + unit_rms_back(middle, entry_two_grad * (1.0 + scale_two))
    grad_gate_one = jnp.sum(middle_grad * attended, axis=1)
    attended_grad = (middle_grad * gate_one).astype(jnp.bfloat16)
    grad_proj = jnp.einsum(
        "bpd,bpe->de", mixed_bf, attended_grad, preferred_element_type=jnp.float32
    )
    mixed_grad = jnp.einsum(
        "bpe,de->bpd", attended_grad, proj_weight, preferred_element_type=jnp.float32
    )
    mixed_grad_bf = mixed_grad.reshape(shape).astype(jnp.bfloat16)
    offsets = jnp.transpose(jnp.sum(mixed_grad_bf.astype(jnp.float32) * mixed, axis=-1), (0, 2, 1))
    key_piece = lax.all_gather(key_bf, "band", axis=1, tiled=True)
    value_piece = lax.all_gather(value_bf, "band", axis=1, tiled=True)
    scores = (
        jnp.einsum("bqhd,bkhd->bhqk", query_bf, key_piece, preferred_element_type=jnp.float32)
        * scaling
    )
    probs = jnp.exp(scores - log_total[..., None])
    prob_grad = jnp.einsum(
        "bqhd,bkhd->bhqk", mixed_grad_bf, value_piece, preferred_element_type=jnp.float32
    )
    score_grad = (probs * (prob_grad - offsets[..., None])).astype(jnp.bfloat16)
    query_grad = (
        jnp.einsum("bhqk,bkhd->bqhd", score_grad, key_piece, preferred_element_type=jnp.float32)
        * scaling
    )
    key_term = (
        jnp.einsum("bhqk,bqhd->bkhd", score_grad, query_bf, preferred_element_type=jnp.float32)
        * scaling
    )
    value_term = jnp.einsum(
        "bhqk,bqhd->bkhd",
        probs.astype(jnp.bfloat16),
        mixed_grad_bf,
        preferred_element_type=jnp.float32,
    )
    key_grads = key_term
    value_grads = value_term
    query_grad, key_grads, value_grads = (query_grad, key_grads, value_grads)
    key_local, value_local = (
        lax.psum_scatter(
            key_grads.astype(jnp.bfloat16), "band", scatter_dimension=1, tiled=True
        ).astype(jnp.float32),
        lax.psum_scatter(
            value_grads.astype(jnp.bfloat16), "band", scatter_dimension=1, tiled=True
        ).astype(jnp.float32),
    )
    query_turned = turned_back(query_grad)
    key_turned = turned_back(key_local)
    local_query_gain = jnp.sum(query_turned * query_unit, axis=(0, 1, 2))
    local_key_gain = jnp.sum(key_turned * key_unit, axis=(0, 1, 2))
    query_raw_grad = unit_rms_back(query_raw, query_turned * query_gain)
    key_raw_grad = unit_rms_back(key_raw, key_turned * key_gain)
    flat = (images, rows, width)
    projected_grad = jnp.concatenate(
        [query_raw_grad.reshape(flat), key_raw_grad.reshape(flat), value_local.reshape(flat)],
        axis=-1,
    ).astype(jnp.bfloat16)
    grad_qkv = jnp.einsum(
        "bpd,bpe->de", entry_one, projected_grad, preferred_element_type=jnp.float32
    )
    entry_one_grad = jnp.einsum(
        "bpe,de->bpd", projected_grad, qkv_weight, preferred_element_type=jnp.float32
    )
    grad_scale_one = jnp.sum(entry_one_grad * normed_one, axis=1)
    grad_shift_one = jnp.sum(entry_one_grad, axis=1)
    source_grad = middle_grad + unit_rms_back(source, entry_one_grad * (1.0 + scale_one))
    grad_latents = source_grad.astype(jnp.bfloat16)
    band_partial = jnp.concatenate(
        [
            grad_shift_one,
            grad_scale_one,
            grad_gate_one,
            grad_shift_two,
            grad_scale_two,
            grad_gate_two,
        ],
        axis=-1,
    )
    modulation_grad, band_query_gain, band_key_gain = (
        lax.psum(band_partial.astype(jnp.bfloat16), "band").astype(jnp.float32),
        lax.psum(local_query_gain[None, :].astype(jnp.bfloat16), "band").astype(jnp.float32),
        lax.psum(local_key_gain[None, :].astype(jnp.bfloat16), "band").astype(jnp.float32),
    )
    condition_grad = jnp.dot(modulation_grad, ada_weight.astype(jnp.float32).T, precision=highest)
    before_grad = condition_grad * silu_slope(before)
    condition_all, features_all, modulation_all, before_all, query_gain_rows, key_gain_rows = (
        lax.all_gather(
            condition.astype(jnp.float32).astype(jnp.bfloat16), "img", axis=0, tiled=True
        ).astype(jnp.float32),
        lax.all_gather(
            features.astype(jnp.float32).astype(jnp.bfloat16), "img", axis=0, tiled=True
        ).astype(jnp.float32),
        lax.all_gather(modulation_grad.astype(jnp.bfloat16), "img", axis=0, tiled=True).astype(
            modulation_grad.dtype
        ),
        lax.all_gather(before_grad.astype(jnp.bfloat16), "img", axis=0, tiled=True).astype(
            before_grad.dtype
        ),
        lax.all_gather(band_query_gain.astype(jnp.bfloat16), "img", axis=0, tiled=True).astype(
            band_query_gain.dtype
        ),
        lax.all_gather(band_key_gain.astype(jnp.bfloat16), "img", axis=0, tiled=True).astype(
            band_key_gain.dtype
        ),
    )
    labels_all = lax.all_gather(labels, "img", axis=0, tiled=True)
    img_index = lax.axis_index("img")
    band_index = lax.axis_index("band")
    ada_rows = width // lax.axis_size("img")
    ada_cols = 6 * width // lax.axis_size("band")
    time_rows = FREQ // lax.axis_size("img")
    time_cols = width // lax.axis_size("band")
    condition_part = lax.dynamic_slice_in_dim(condition_all, img_index * ada_rows, ada_rows, 1)
    modulation_part = lax.dynamic_slice_in_dim(modulation_all, band_index * ada_cols, ada_cols, 1)
    sum_ada = jnp.dot(condition_part.T, modulation_part, precision=highest)
    features_part = lax.dynamic_slice_in_dim(features_all, img_index * time_rows, time_rows, 1)
    before_part = lax.dynamic_slice_in_dim(before_all, band_index * time_cols, time_cols, 1)
    sum_time = jnp.dot(features_part.T, before_part, precision=highest)
    class_all = (labels_all[:, None] == jnp.arange(NCLASS, dtype=jnp.int32)[None, :]).astype(
        jnp.float32
    )
    sum_class = jnp.dot(class_all.T, before_all, precision=highest)
    sum_bias = jnp.sum(modulation_all, axis=0)
    sum_query_gain = jnp.sum(query_gain_rows, axis=0)
    sum_key_gain = jnp.sum(key_gain_rows, axis=0)
    part_qkv, part_proj, part_gateup, part_down = (
        lax.psum_scatter(
            grad_qkv.astype(jnp.bfloat16), "img", scatter_dimension=0, tiled=True
        ).astype(jnp.float32),
        lax.psum_scatter(
            grad_proj.astype(jnp.bfloat16), "img", scatter_dimension=0, tiled=True
        ).astype(jnp.float32),
        lax.psum_scatter(
            grad_gateup.astype(jnp.bfloat16), "img", scatter_dimension=0, tiled=True
        ).astype(jnp.float32),
        lax.psum_scatter(
            grad_down.astype(jnp.bfloat16), "img", scatter_dimension=0, tiled=True
        ).astype(jnp.float32),
    )
    sum_qkv, sum_proj, sum_gateup, sum_down = (
        lax.psum_scatter(
            part_qkv.astype(jnp.bfloat16), "band", scatter_dimension=1, tiled=True
        ).astype(jnp.float32),
        lax.psum_scatter(
            part_proj.astype(jnp.bfloat16), "band", scatter_dimension=1, tiled=True
        ).astype(jnp.float32),
        lax.psum_scatter(
            part_gateup.astype(jnp.bfloat16), "band", scatter_dimension=1, tiled=True
        ).astype(jnp.float32),
        lax.psum_scatter(
            part_down.astype(jnp.bfloat16), "band", scatter_dimension=1, tiled=True
        ).astype(jnp.float32),
    )
    return (
        result,
        grad_latents,
        sum_time,
        sum_class,
        sum_ada,
        sum_bias,
        sum_qkv,
        sum_query_gain,
        sum_key_gain,
        sum_proj,
        sum_gateup,
        sum_down,
    )


HDP = 80
LOG2E = math.log2(math.e)
VMEM_MAX = 62 * 2**20
bf16 = jnp.bfloat16
f32 = jnp.float32


def dot(left, right, left_dim, right_dim):
    return lax.dot_general(
        left, right, (((left_dim,), (right_dim,)), ((), ())), preferred_element_type=f32
    )


def params_of(**extra):
    return pltpu.CompilerParams(vmem_limit_bytes=VMEM_MAX, **extra)


def whole(shape):
    return pl.BlockSpec(shape, lambda *_: (0,) * len(shape), pipeline_mode=pl.Buffered(1))


def cost(flops, bytes_accessed, transcendentals=0):
    return pl.CostEstimate(
        flops=int(flops), bytes_accessed=int(bytes_accessed), transcendentals=int(transcendentals)
    )


def partner_rows(values, low_half):
    quarter = HD // 4
    return jnp.where(
        low_half, pltpu.roll(values, HD - quarter, 0), pltpu.roll(values, quarter, 0)
    )


def low_half_mask(patches):
    row = lax.broadcasted_iota(jnp.int32, (HD, patches), 0)
    quarter = HD // 4
    return (row < quarter) | ((row >= 2 * quarter) & (row < 3 * quarter))


def tail_rows(first, second, patches):
    row = lax.broadcasted_iota(jnp.int32, (HDP - HD, patches), 0)
    return jnp.where(row == 0, first, jnp.where(row == 1, second, 0.0))


def split_two(values):
    high = values.astype(bf16).astype(f32)
    return high, values - high


MESH_ID = pl.DeviceIdType.MESH


def pair_axes():
    bits = lax.axis_size("img").bit_length() - 1
    return ["y"] + [f"b{bit}" for bit in reversed(range(bits))]


def own_places():
    img = lax.axis_index("img")
    places = {"y": lax.axis_index("band")}
    for bit in range(lax.axis_size("img").bit_length() - 1):
        places[f"b{bit}"] = lax.rem(lax.div(img, 2**bit), 2)
    return places


def partner_id(axis, places):
    if axis == "y":
        return {"band": 1 - places["y"]}
    bit = int(axis[1:])
    return {"img": lax.axis_index("img") + (1 - 2 * places[axis]) * 2**bit}


def greet(places):
    barrier = pltpu.get_barrier_semaphore()
    for axis in places:
        pl.semaphore_signal(
            barrier, inc=1, device_id=partner_id(axis, places), device_id_type=MESH_ID
        )
    pl.semaphore_wait(barrier, len(places))


class Halving:
    def __init__(self, places, dims, order, held, arrived, send, receive, lead=(), tail=()):
        self.places, self.dims, self.order = places, list(dims), list(order)
        self.held, self.arrived, self.send, self.receive = held, arrived, send, receive
        self.lead, self.tail = tuple(lead), tuple(tail)

    def source_index(self, mine):
        first = self.order[0]
        place = self.places[first] if mine else 1 - self.places[first]
        return [place if name == first else slice(None) for name in self.dims]

    def held_index(self, step, mine):
        picked = []
        for name in self.dims:
            place = self.order.index(name)
            if place == 0:
                continue
            if place < step:
                picked.append(self.places[name])
            elif place == step:
                picked.append(self.places[name] if mine else 1 - self.places[name])
            else:
                picked.append(slice(None))
        return picked

    def copy(self, step, source=None):
        if step == 0:
            block = source.at[tuple(self.source_index(False)) + self.tail]
        else:
            block = self.held.at[self.lead + tuple(self.held_index(step, False))]
        arrived = self.arrived[step]
        return pltpu.make_async_remote_copy(
            src_ref=block,
            dst_ref=arrived.at[self.lead] if self.lead else arrived,
            send_sem=self.send.at[self.lead + (step,)],
            recv_sem=self.receive.at[self.lead + (step,)],
            device_id=partner_id(self.order[step], self.places),
            device_id_type=MESH_ID,
        )

    def own_half(self, source, semaphore):
        return pltpu.make_async_copy(
            source.at[tuple(self.source_index(True)) + self.tail],
            self.held.at[self.lead] if self.lead else self.held,
            semaphore,
        )

    def add(self, step, source=None, put=None):
        picked = self.held_index(step, True)
        free = [place for place, entry in enumerate(picked) if isinstance(entry, slice)]
        if not free:
            total = self.held[self.lead + tuple(picked)].astype(f32)
            put(total + self.arrived[step][self.lead + (...,)].astype(f32))
            return

        def one(number, _):
            digits = [lax.rem(lax.div(number, 2**place), 2) for place in range(len(free))]
            target = list(picked)
            for place, digit in zip(free, digits):
                target[place] = digit
            if source is not None:
                rest = iter(digits)
                spot = [next(rest) if isinstance(e, slice) else e for e in self.source_index(True)]
                old = source[tuple(spot)]
            else:
                old = self.held[self.lead + tuple(target)]
            self.held[self.lead + tuple(target)] = (
                old + self.arrived[step][self.lead + tuple(digits)]
            )
            return 0

        lax.fori_loop(0, 2 ** len(free), one, 0)


def halving_scratch(dims, tail, lead=()):
    left = len(dims) - 1
    shapes = [lead + (2,) * left + tail]
    shapes += [lead + (2,) * (left - step) + tail for step in range(len(dims))]
    semaphores = pltpu.SemaphoreType.DMA(lead + (len(dims),))
    return [pltpu.VMEM(shape, bf16) for shape in shapes] + [semaphores, semaphores]


def order_of(dims, *first):
    rest = [name for name in reversed(dims) if name not in first]
    return list(first) + rest


def front_kernel(
    x_ref, scale_ref, shift_ref, w_ref, gains_ref, cos_ref, sin_ref,
    entry_ref, heads_ref, unit_ref, factor_ref,
):
    section = pl.program_id(0)
    patches = x_ref.shape[0]

    @pl.when(section == 0)
    def _():
        source = x_ref[...].astype(f32)
        normed = source * lax.rsqrt(jnp.mean(source * source, axis=1, keepdims=True) + epsilon)
        entry_ref[...] = (normed * (1.0 + scale_ref[...]) + shift_ref[...]).astype(bf16)

    raw = dot(w_ref[...], entry_ref[...], 0, 1)

    @pl.when(section < 2)
    def _():
        mask = low_half_mask(patches)
        extra = tail_rows(*[jnp.where(section == 1, 1.0, 0.0)] * 2, patches)
        gain = gains_ref[0]
        for head in range(HEADS):
            part = raw[head * HD : (head + 1) * HD, :]
            factor = lax.rsqrt(jnp.mean(part * part, axis=0, keepdims=True) + epsilon)
            unit = part * factor
            scaled = unit * gain
            turned = scaled * cos_ref[...] + partner_rows(scaled, mask) * sin_ref[...]
            heads_ref[0, head] = jnp.concatenate([turned, extra], axis=0).astype(bf16)
            unit_ref[0, head] = unit.astype(bf16)
            factor_ref[0, head] = factor

    @pl.when(section == 2)
    def _():
        extra = tail_rows(1.0, 1.0, patches)
        for head in range(HEADS):
            part = raw[head * HD : (head + 1) * HD, :]
            heads_ref[0, head] = jnp.concatenate([part, extra], axis=0).astype(bf16)


def front(x, scale, shift, qkv_weight, gains, cosine, sine):
    patches, width = x.shape
    last = lambda s: jnp.minimum(s, 1)
    return pl.pallas_call(
        front_kernel,
        grid=(3,),
        in_specs=[
            whole((patches, width)),
            whole((1, width)),
            whole((1, width)),
            pl.BlockSpec((width, width), lambda s: (0, s)),
            pl.BlockSpec((1, HD, 1), lambda s: (last(s), 0, 0)),
            whole((HD, patches)),
            whole((HD, patches)),
        ],
        out_specs=[
            pl.BlockSpec((patches, width), lambda s: (0, 0)),
            pl.BlockSpec((1, HEADS, HDP, patches), lambda s: (s, 0, 0, 0)),
            pl.BlockSpec((1, HEADS, HD, patches), lambda s: (last(s), 0, 0, 0)),
            pl.BlockSpec((1, HEADS, 1, patches), lambda s: (last(s), 0, 0, 0)),
        ],
        out_shape=[
            jax.ShapeDtypeStruct((patches, width), bf16),
            jax.ShapeDtypeStruct((3, HEADS, HDP, patches), bf16),
            jax.ShapeDtypeStruct((2, HEADS, HD, patches), bf16),
            jax.ShapeDtypeStruct((2, HEADS, 1, patches), f32),
        ],
        compiler_params=params_of(),
        cost_estimate=cost(6 * patches * width * width, 24e6),
        name="front",
    )(x, scale, shift, qkv_weight, gains, cosine, sine)


def attend_kernel(q_ref, k_ref, v_ref, mixed_ref, lse_ref, qext_ref):
    patches = q_ref.shape[-1]
    step = patches // 2
    key = k_ref[...]
    value = v_ref[...]
    for start in range(0, patches, step):
        columns = slice(start, start + step)
        scores = dot(key, q_ref[:, columns], 0, 0)
        weights = jnp.exp2(scores).astype(bf16)
        summed = dot(value, weights, 1, 0)
        total = summed[HD : HD + 1, :]
        mixed_ref[:, columns] = (summed[:HD, :] / total).astype(bf16)
        high, low = split_two(-jnp.log2(total))
        extra = jnp.concatenate([jnp.zeros((HD, step), f32), tail_rows(high, low, step)], axis=0)
        qext_ref[:, columns] = q_ref[:, columns] + extra.astype(bf16)


def attend(heads):
    patches = heads.shape[-1]
    section = lambda member: pl.BlockSpec(
        (None, None, HDP, patches), lambda h: (member, h, 0, 0)
    )
    return pl.pallas_call(
        lambda q, k, v, mixed, qext: attend_kernel(q, k, v, mixed, None, qext),
        grid=(HEADS,),
        in_specs=[section(0), section(1), section(2)],
        out_specs=[
            pl.BlockSpec((None, HD, patches), lambda h: (h, 0, 0)),
            pl.BlockSpec((None, HDP, patches), lambda h: (h, 0, 0)),
        ],
        out_shape=[
            jax.ShapeDtypeStruct((HEADS, HD, patches), bf16),
            jax.ShapeDtypeStruct((HEADS, HDP, patches), bf16),
        ],
        compiler_params=params_of(),
        cost_estimate=cost(8 * HEADS * patches * patches * HDP, 14e6, HEADS * patches * patches),
        name="attend",
    )(heads, heads, heads)


def middle_kernel(
    mixed_ref, w_ref, x_ref, c_ref, vectors_ref, attended_ref, entry_ref, fed_grad_ref
):
    attended = dot(mixed_ref[...], w_ref[...], 0, 0)
    attended_bf = attended.astype(bf16)
    attended_ref[...] = attended_bf
    gate_one, scale_two, shift_two, gate_two = [vectors_ref[i : i + 1, :] for i in range(4)]
    middle = x_ref[...].astype(f32) + gate_one * attended_bf.astype(f32)
    normed = middle * lax.rsqrt(jnp.mean(middle * middle, axis=1, keepdims=True) + epsilon)
    entry_ref[...] = (normed * (1.0 + scale_two) + shift_two).astype(bf16)
    fed_grad_ref[...] = (c_ref[...].astype(f32) * gate_two).astype(bf16)


def middle_step(mixed, proj_weight, x, c, vectors):
    patches, width = x.shape
    rows = 256
    block = pl.BlockSpec((rows, width), lambda t: (t, 0))
    return pl.pallas_call(
        middle_kernel,
        grid=(patches // rows,),
        in_specs=[
            pl.BlockSpec((width, rows), lambda t: (0, t)),
            whole((width, width)),
            block,
            block,
            whole((8, width)),
        ],
        out_specs=[block] * 3,
        out_shape=[jax.ShapeDtypeStruct((patches, width), bf16)] * 3,
        compiler_params=params_of(),
        cost_estimate=cost(2 * patches * width * width, 17e6),
        name="middle",
    )(mixed, proj_weight, x, c, vectors)


MLP_TILE = 512
MLP_SUB = 256
HOSTED = 4


def mlp_kernel(
    dims, entry_ref, fed_grad_ref, wg_ref, wu_ref, wd_ref,
    fed_ref, entry_grad_ref, down_ref, done_ref, left_ref,
    hidden_ref, gate_grad_ref, up_grad_ref, source_ref, left_sem, held, *rest,
):
    *arrived, send, receive = rest
    tile = pl.program_id(0)
    places = own_places()
    orders = [order_of(dims, "b0", "y", "b1"), order_of(dims, "b0", "b1", "y")]
    steps = len(dims)

    def streams(number):
        slot = lax.rem(number, 2)
        return [
            Halving(places, dims, orders[sub], held, arrived, send, receive, (slot, sub))
            for sub in range(2)
        ]

    def advance(number, step):
        @pl.when((number >= 0) & (number < HOSTED))
        def _():
            for sub, stream in enumerate(streams(number)):
                source = source_ref.at[sub]
                stream.copy(step, source).wait()

                def put(values):
                    done_ref[number, sub] = values.astype(bf16)

                stream.add(step, source if step == 0 else None, put)
                if step + 1 < steps:
                    stream.copy(step + 1).start()

    @pl.when(tile == 0)
    def _():
        greet(places)

    entry = entry_ref[...]
    fed_grad = fed_grad_ref[...]
    gate = dot(entry, wg_ref[...], 1, 0)
    up = dot(entry, wu_ref[...], 1, 0)
    advance(tile - 2, 3)
    advance(tile - 1, 0)
    sigma = jax.nn.sigmoid(gate)
    silu = gate * sigma
    hidden_ref[...] = (silu * up).astype(bf16)
    hidden_grad = dot(fed_grad, wd_ref[...], 1, 1)
    gate_grad_ref[...] = (hidden_grad * up * (sigma * (1.0 + gate * (1.0 - sigma)))).astype(bf16)
    up_grad_ref[...] = (hidden_grad * silu).astype(bf16)
    fed = dot(hidden_ref[...], wd_ref[...], 1, 0)
    entry_grad = dot(gate_grad_ref[...], wg_ref[...], 1, 1) + dot(
        up_grad_ref[...], wu_ref[...], 1, 1
    )

    @pl.when(tile == 0)
    def _():
        fed_ref[...] = fed
        entry_grad_ref[...] = entry_grad

    @pl.when(tile > 0)
    def _():
        fed_ref[...] += fed
        entry_grad_ref[...] += entry_grad

    for step in range(4, steps):
        advance(tile - 2, step)
    advance(tile - 1, 1)
    down = dot(hidden_ref[...], fed_grad, 0, 0)
    column_half = down.shape[1] // 2
    down_ref[0] = down[:, :column_half].astype(bf16)
    down_ref[1] = down[:, column_half:].astype(bf16)
    grads = [dot(entry, ref[...], 0, 0) for ref in (gate_grad_ref, up_grad_ref)]
    advance(tile - 1, 2)

    def leave(number):
        return pltpu.make_async_copy(
            source_ref, left_ref.at[jnp.maximum(number - HOSTED, 0)], left_sem
        )

    @pl.when(tile > HOSTED)
    def _():
        leave(tile - 1).wait()

    blocks = 2 ** (steps - 1)
    rows = grads[0].shape[0] // blocks
    for half, grad in enumerate(grads):
        for block in range(blocks):
            spot = tuple(block // 2**bit % 2 for bit in reversed(range(steps - 1)))
            part = grad[block * rows : (block + 1) * rows, :].astype(bf16)
            for sub in range(2):
                source_ref[(sub, half) + spot] = part[:, sub * MLP_SUB : (sub + 1) * MLP_SUB]

    @pl.when(tile < HOSTED)
    def _():
        for sub, stream in enumerate(streams(tile)):
            stream.copy(0, source_ref.at[sub]).start()

    @pl.when(tile >= HOSTED)
    def _():
        leave(tile).start()

    @pl.when(tile == pl.num_programs(0) - 1)
    def _():
        leave(tile).wait()


def mlp(entry, fed_grad, gateup_weight, down_weight):
    patches, width = entry.shape
    inner = down_weight.shape[0]
    tile = MLP_TILE
    tiles = inner // tile
    dims = pair_axes()
    rows = width // lax.axis_size("img")
    tail = (rows, MLP_SUB)
    return pl.pallas_call(
        functools.partial(mlp_kernel, dims),
        grid=(tiles,),
        in_specs=[
            whole((patches, width)),
            whole((patches, width)),
            pl.BlockSpec((width, tile), lambda t: (0, t)),
            pl.BlockSpec((width, tile), lambda t: (0, tiles + t)),
            pl.BlockSpec((tile, width), lambda t: (t, 0)),
        ],
        out_specs=[
            whole((patches, width)),
            whole((patches, width)),
            pl.BlockSpec((2, tile, width // 2), lambda t: (0, t, 0)),
            whole((HOSTED, 2) + tail),
            pl.BlockSpec(memory_space=pl.ANY),
        ],
        out_shape=[
            jax.ShapeDtypeStruct((patches, width), f32),
            jax.ShapeDtypeStruct((patches, width), f32),
            jax.ShapeDtypeStruct((2, inner, width // 2), bf16),
            jax.ShapeDtypeStruct((HOSTED, 2) + tail, bf16),
            jax.ShapeDtypeStruct((tiles - HOSTED, 2) + (2,) * len(dims) + tail, bf16),
        ],
        scratch_shapes=[pltpu.VMEM((patches, tile), bf16)] * 3
        + [pltpu.VMEM((2,) + (2,) * len(dims) + tail, bf16), pltpu.SemaphoreType.DMA]
        + halving_scratch(dims, tail, (2, 2)),
        compiler_params=params_of(collective_id=0, has_side_effects=True),
        cost_estimate=cost(18 * patches * width * inner, 56e6),
        name="mlp",
    )(entry, fed_grad, gateup_weight, gateup_weight, down_weight)


def turn_kernel(
    fed_ref, entry_grad_ref, x_ref, attended_ref, c_ref, mixed_ref, w_ref, vectors_ref,
    result_ref, middle_grad_ref, mixed_grad_ref, grad_proj_ref, sums_ref, total_ref,
):
    step = pl.program_id(0)
    gate_one, scale_two, _, gate_two = [vectors_ref[i : i + 1, :] for i in range(4)]
    attended = attended_ref[...].astype(f32)
    upstream = c_ref[...].astype(f32)
    fed = fed_ref[...]
    middle = x_ref[...].astype(f32) + gate_one * attended
    result_ref[...] = (middle + gate_two * fed).astype(bf16)
    factor = lax.rsqrt(jnp.mean(middle * middle, axis=1, keepdims=True) + epsilon)
    normed = middle * factor
    entry_grad = entry_grad_ref[...]
    inner = entry_grad * (1.0 + scale_two)
    middle_grad = upstream + factor * (
        inner - normed * jnp.mean(inner * normed, axis=1, keepdims=True)
    )
    middle_grad_ref[...] = middle_grad
    attended_grad = (middle_grad * gate_one).astype(bf16)
    mixed_grad_ref[...] = dot(w_ref[...], attended_grad, 1, 1).astype(bf16)
    grad_proj = dot(mixed_ref[...], attended_grad, 1, 0)
    add = lambda v: jnp.sum(v, axis=0, keepdims=True)
    sums = jnp.concatenate(
        [
            add(middle_grad * attended),
            add(entry_grad),
            add(entry_grad * normed),
            add(upstream * fed),
            jnp.zeros((4, fed.shape[1]), f32),
        ],
        axis=0,
    )

    @pl.when(step == 0)
    def _():
        total_ref[...] = grad_proj
        sums_ref[...] = sums

    @pl.when(step > 0)
    def _():
        total_ref[...] += grad_proj
        sums_ref[...] += sums

    @pl.when(step == pl.num_programs(0) - 1)
    def _():
        half = total_ref.shape[1] // 2
        grad_proj_ref[0] = total_ref[:, :half].astype(bf16)
        grad_proj_ref[1] = total_ref[:, half:].astype(bf16)


def turn_step(fed, entry_grad, x, attended, c, mixed, proj_weight, vectors):
    patches, width = x.shape
    rows = 256
    block = pl.BlockSpec((rows, width), lambda t: (t, 0))
    across = pl.BlockSpec((width, rows), lambda t: (0, t))
    return pl.pallas_call(
        turn_kernel,
        grid=(patches // rows,),
        in_specs=[block] * 5 + [across, whole((width, width)), whole((8, width))],
        out_specs=[
            block,
            block,
            across,
            pl.BlockSpec((2, width, width // 2), lambda t: (0, 0, 0)),
            pl.BlockSpec((8, width), lambda t: (0, 0)),
        ],
        out_shape=[
            jax.ShapeDtypeStruct((patches, width), bf16),
            jax.ShapeDtypeStruct((patches, width), f32),
            jax.ShapeDtypeStruct((width, patches), bf16),
            jax.ShapeDtypeStruct((2, width, width // 2), bf16),
            jax.ShapeDtypeStruct((8, width), f32),
        ],
        scratch_shapes=[pltpu.VMEM((width, width), f32)],
        compiler_params=params_of(),
        cost_estimate=cost(4 * patches * width * width, 35e6),
        name="turn",
    )(fed, entry_grad, x, attended, c, mixed, proj_weight, vectors)


def back_plan(dims):
    first, second = pl.ds(0, 96), pl.ds(96, 96)
    return [
        ("down", (0,), (first,), order_of(dims, "b0", "b1", "b2", "y"), (0, 2, 8, 11, 13, 15)),
        ("down", (1,), (second,), order_of(dims, "b0", "b2", "b1", "y"), (0, 2, 8, 11, 13, 15)),
        ("left", (0, 0), (), order_of(dims, "b0", "y", "b1"), (0, 3, 7, 10, 12, 14)),
        ("left", (1, 0), (), order_of(dims, "b0", "y", "b1"), (0, 3, 7, 10, 12, 14)),
        ("left", (0, 1), (), order_of(dims, "b0", "y", "b2"), (0, 3, 10, 12, 14, 15)),
        ("left", (1, 1), (), order_of(dims, "b0", "y", "b2"), (0, 3, 10, 12, 14, 15)),
        ("proj", (), (), order_of(dims, "b0", "y", "b1"), (1, 4, 12, 14, 15, 15)),
    ]


def attend_back_kernel(
    dims, q_ref, k_ref, v_ref, mg_ref, mixed_ref, unit_ref, factor_ref, gains_ref, cos_ref,
    sin_ref, down_ref, left_ref, proj_ref,
    out_ref, gain_out_ref, down_out_ref, left_out_ref, proj_out_ref,
    mg_ext_ref, acc_ref, own_sem, *buffers,
):
    head = pl.program_id(0)
    places = own_places()
    steps = len(dims)
    sizes = steps + 3
    groups = {
        name: buffers[place * sizes : (place + 1) * sizes]
        for place, name in enumerate(("down", "left", "proj"))
    }
    sources = {"down": down_ref, "left": left_ref, "proj": proj_ref}
    outs = {"down": down_out_ref, "left": left_out_ref, "proj": proj_out_ref}

    @pl.when(head == 0)
    def _():
        greet(places)

    def streams():
        for number, (name, lead, rows, order, heads) in enumerate(back_plan(dims)):
            held, *arrived, send, receive = groups[name]
            source, tail = sources[name], ()
            if name == "down":
                tail = rows + (slice(None),)
            if name == "left":
                source = source.at[lead]
            stream = Halving(places, dims, order, held, arrived, send, receive, lead, tail)
            yield number, name, lead, stream, source, heads

    def advance(now, last=False):
        for number, name, lead, stream, source, heads in streams():
            for step in range(-1, steps):
                if (heads[step + 1] == now) and (last == (step == steps - 1 and now == HEADS - 1)):
                    due(now, number, name, lead, stream, source, step)

    def due(now, number, name, lead, stream, source, step):
        @pl.when(head == now)
        def _():
            if step < 0:
                stream.copy(0, source).start()
                stream.own_half(source, own_sem.at[number]).start()
                return
            stream.copy(step, source).wait()
            if step == 0:
                stream.own_half(source, own_sem.at[number]).wait()

            def put(values):
                outs[name][lead + (...,)] = values.astype(bf16)

            stream.add(step, None, put)
            if step + 1 < steps:
                stream.copy(step + 1).start()

    for now in range(HEADS):
        advance(now)
    patches = q_ref.shape[-1]
    step = patches // 2
    scaling = HD ** (-0.5)
    mixed_grad = mg_ref[...].astype(f32)
    offsets = jnp.sum(mixed_grad * mixed_ref[...].astype(f32), axis=0, keepdims=True)
    high, low = split_two(-offsets)
    mg_ext_ref[...] = jnp.concatenate(
        [mixed_grad, tail_rows(high, low, patches)], axis=0
    ).astype(bf16)
    key = k_ref[...]
    value = v_ref[...]
    for start in range(0, patches, step):
        columns = slice(start, start + step)
        query = q_ref[:, columns]
        grads = mg_ext_ref[:, columns]
        probs = jnp.exp2(dot(key, query, 0, 0))
        score_grad = (probs * dot(value, grads, 0, 0)).astype(bf16)
        probs_bf = probs.astype(bf16)
        acc_ref[0, :, columns] = dot(key, score_grad, 1, 0)
        key_term = dot(query, score_grad, 1, 1)
        value_term = dot(grads, probs_bf, 1, 1)
        if start == 0:
            acc_ref[1] = key_term
            acc_ref[2] = value_term
        else:
            acc_ref[1] += key_term
            acc_ref[2] += value_term
    mask = low_half_mask(patches)
    for member, weight in ((0, scaling), (1, 1.0 / LOG2E)):
        grads = acc_ref[member, :HD, :] * weight
        turned = grads * cos_ref[...] + partner_rows(grads * sin_ref[...], mask)
        unit = unit_ref[member].astype(f32)
        product = turned * unit

        @pl.when(head == 0)
        def _():
            gain_out_ref[member] = product

        @pl.when(head > 0)
        def _():
            gain_out_ref[member] += product

        inner = turned * gains_ref[member]
        raw = factor_ref[member] * (inner - unit * jnp.mean(inner * unit, axis=0, keepdims=True))
        out_ref[member] = raw.astype(bf16)
    out_ref[2] = acc_ref[2, :HD, :].astype(bf16)
    advance(HEADS - 1, True)


def attend_back(
    query, heads, mixed_grad, mixed, unit, factor, gains, cosine, sine, down, left, proj
):
    patches = query.shape[-1]
    dims = pair_axes()
    split = (2,) * (len(dims) - 1)
    devices = lax.axis_size("img")
    down = down.reshape((2,) + split + (down.shape[1] // devices, down.shape[2]))
    proj = proj.reshape((2,) + split + (proj.shape[1] // devices, proj.shape[2]))
    down_tail = (down.shape[-2] // 2, down.shape[-1])
    left_tail, proj_tail = left.shape[-2:], proj.shape[-2:]
    left_lead = left.shape[:2]
    anywhere = pl.BlockSpec(memory_space=pl.ANY)
    section = lambda member: pl.BlockSpec(
        (None, None, HDP, patches), lambda h: (member, h, 0, 0)
    )
    single = lambda rows: pl.BlockSpec((None, rows, patches), lambda h: (h, 0, 0))
    pair = lambda rows: pl.BlockSpec((2, None, rows, patches), lambda h: (0, h, 0, 0))
    return pl.pallas_call(
        functools.partial(attend_back_kernel, dims),
        grid=(HEADS,),
        in_specs=[
            single(HDP),
            section(1),
            section(2),
            single(HD),
            single(HD),
            pair(HD),
            pair(1),
            whole((2, HD, 1)),
            whole((HD, patches)),
            whole((HD, patches)),
            anywhere,
            anywhere,
            anywhere,
        ],
        out_specs=[
            pl.BlockSpec((3, None, HD, patches), lambda h: (0, h, 0, 0)),
            pl.BlockSpec((2, HD, patches), lambda h: (0, 0, 0)),
            whole((2,) + down_tail),
            whole(left_lead + left_tail),
            whole(proj_tail),
        ],
        out_shape=[
            jax.ShapeDtypeStruct((3, HEADS, HD, patches), bf16),
            jax.ShapeDtypeStruct((2, HD, patches), f32),
            jax.ShapeDtypeStruct((2,) + down_tail, bf16),
            jax.ShapeDtypeStruct(left_lead + left_tail, bf16),
            jax.ShapeDtypeStruct(proj_tail, bf16),
        ],
        scratch_shapes=[
            pltpu.VMEM((HDP, patches), bf16),
            pltpu.VMEM((3, HDP, patches), f32),
            pltpu.SemaphoreType.DMA((len(back_plan(dims)),)),
        ]
        + halving_scratch(dims, down_tail, (2,))
        + halving_scratch(dims, left_tail, left_lead)
        + halving_scratch(dims, proj_tail),
        compiler_params=params_of(collective_id=1, has_side_effects=True),
        cost_estimate=cost(20 * HEADS * patches * patches * HDP, 32e6, HEADS * patches**2),
        name="attend_back",
    )(
        query, heads, heads, mixed_grad, mixed, unit, factor, gains, cosine, sine, down, left, proj
    )


def back_kernel(pg_ref, w_ref, entry_ref, grad_ref, entry_grad_ref):
    section = pl.program_id(0)
    grad_ref[...] = dot(entry_ref[...], pg_ref[...], 0, 1).astype(bf16)
    term = dot(w_ref[...], pg_ref[...], 1, 0)

    @pl.when(section == 0)
    def _():
        entry_grad_ref[...] = term

    @pl.when(section > 0)
    def _():
        entry_grad_ref[...] += term


def back_step(projected_grad, qkv_weight, entry):
    patches, width = entry.shape
    return pl.pallas_call(
        back_kernel,
        grid=(3,),
        in_specs=[
            pl.BlockSpec((None, width, patches), lambda s: (s, 0, 0)),
            pl.BlockSpec((width, width), lambda s: (0, s)),
            whole((patches, width)),
        ],
        out_specs=[
            pl.BlockSpec((width, width), lambda s: (0, s)),
            pl.BlockSpec((width, patches), lambda s: (0, 0)),
        ],
        out_shape=[
            jax.ShapeDtypeStruct((width, 3 * width), bf16),
            jax.ShapeDtypeStruct((width, patches), f32),
        ],
        compiler_params=params_of(),
        cost_estimate=cost(12 * patches * width * width, 32e6),
        name="back",
    )(projected_grad, qkv_weight, entry)


def last_kernel(entry_grad_ref, x_ref, middle_grad_ref, scale_ref, out_ref, sums_ref):
    step = pl.program_id(0)
    entry_grad = entry_grad_ref[...].T
    source = x_ref[...].astype(f32)
    factor = lax.rsqrt(jnp.mean(source * source, axis=1, keepdims=True) + epsilon)
    normed = source * factor
    inner = entry_grad * (1.0 + scale_ref[...])
    grads = middle_grad_ref[...] + factor * (
        inner - normed * jnp.mean(inner * normed, axis=1, keepdims=True)
    )
    out_ref[...] = grads.astype(bf16)
    add = lambda v: jnp.sum(v, axis=0, keepdims=True)
    sums = jnp.concatenate(
        [add(entry_grad), add(entry_grad * normed), jnp.zeros((6, source.shape[1]), f32)], axis=0
    )

    @pl.when(step == 0)
    def _():
        sums_ref[...] = sums

    @pl.when(step > 0)
    def _():
        sums_ref[...] += sums


def last_step(entry_grad, x, middle_grad, scale):
    patches, width = x.shape
    rows = 256
    block = pl.BlockSpec((rows, width), lambda t: (t, 0))
    return pl.pallas_call(
        last_kernel,
        grid=(patches // rows,),
        in_specs=[
            pl.BlockSpec((width, rows), lambda t: (0, t)),
            block,
            block,
            whole((1, width)),
        ],
        out_specs=[block, pl.BlockSpec((8, width), lambda t: (0, 0))],
        out_shape=[
            jax.ShapeDtypeStruct((patches, width), bf16),
            jax.ShapeDtypeStruct((8, width), f32),
        ],
        compiler_params=params_of(),
        cost_estimate=cost(20 * patches * width, 17e6),
        name="last",
    )(entry_grad, x, middle_grad, scale)


def pick(values, index):
    return lax.dynamic_index_in_dim(values, index, 0, keepdims=False)


def per_device_whole(
    latents,
    cotangent,
    labels,
    group_ids,
    group_logits,
    row_pos,
    col_pos,
    time_weight,
    class_table,
    ada_weight,
    ada_bias,
    qkv_weight,
    query_gain,
    key_gain,
    proj_weight,
    gateup_weight,
    down_weight,
):
    width = latents.shape[-1]
    bands = lax.axis_size("band")
    img_index = lax.axis_index("img")
    band_index = lax.axis_index("band")
    half = latents.shape[1]

    def exchange(own):
        parts = [pick(own, band_index)]
        for shift in range(1, bands):
            pairs = [(i, (i + shift) % bands) for i in range(bands)]
            away = pick(own, lax.rem(band_index + shift, bands))
            parts.append(lax.ppermute(away, "band", pairs))
        return jnp.concatenate(parts, axis=0)

    def give_back(values):
        back = [values[:half]]
        for shift in range(1, bands):
            pairs = [(i, (i - shift) % bands) for i in range(bands)]
            back.append(
                lax.ppermute(values[shift * half : (shift + 1) * half], "band", pairs)
            )
        stacked = jnp.stack(back)
        order = lax.rem(jnp.arange(bands) - band_index + bands, bands)
        return jnp.take(stacked, order, axis=0)

    x = exchange(latents)
    c = exchange(cotangent)
    places = jnp.stack([row_pos, col_pos], axis=1)
    place_parts = [places]
    for shift in range(1, bands):
        pairs = [(i, (i + shift) % bands) for i in range(bands)]
        place_parts.append(lax.ppermute(places, "band", pairs))
    places = jnp.concatenate(place_parts, axis=0)

    quarter = HD // 4
    frequency = jnp.exp(-math.log(10000.0) * jnp.arange(quarter, dtype=f32) / quarter)
    angles = frequency[:, None] * places.astype(f32).T[:, None, :]
    cosine, sine = jnp.cos(angles), jnp.sin(angles)
    cosine = jnp.concatenate([cosine[0], cosine[0], cosine[1], cosine[1]], axis=0)
    sine = jnp.concatenate([-sine[0], sine[0], -sine[1], sine[1]], axis=0)

    def condition_of(group_ids, labels):
        group_hot = (group_ids[:, None] == jnp.arange(GROUPS, dtype=jnp.int32)[None, :]).astype(f32)
        times = jax.nn.sigmoid(jnp.dot(group_hot, group_logits, precision=highest))
        features = time_features(times, FREQ // 2).astype(bf16)
        before = jnp.dot(features, time_weight, preferred_element_type=f32) + jnp.take(
            class_table, labels, axis=0
        ).astype(f32)
        return features, before, jax.nn.silu(before).astype(bf16)

    own_group = pick(group_ids, band_index)[None]
    own_label = pick(labels, band_index)[None]
    _, _, condition = condition_of(own_group, own_label)
    modulation = jnp.dot(condition, ada_weight, preferred_element_type=f32) + ada_bias
    modes = modulation.reshape(6, width)
    shift_one, scale_one = modes[0:1], modes[1:2]
    vectors = jnp.concatenate([modes[2:3], modes[4:5], modes[3:4], modes[5:6], modes[2:6]], axis=0)

    scaling = HD ** (-0.5)
    gains = jnp.stack([query_gain, key_gain])[:, :, None]
    scaled_gains = gains * jnp.array([scaling * LOG2E, 1.0], f32)[:, None, None]
    entry_one, heads, unit, factor = front(
        x, scale_one, shift_one, qkv_weight, scaled_gains, cosine, sine
    )
    mixed, query = attend(heads)
    patches = x.shape[0]
    mixed_flat = mixed.reshape(width, patches)
    attended, entry_two, fed_grad = middle_step(mixed_flat, proj_weight, x, c, vectors)
    fed, entry_two_grad, grad_down, gateup_done, gateup_left = mlp(
        entry_two, fed_grad, gateup_weight, down_weight
    )
    result, middle_grad, mixed_grad, grad_proj, sums_two = turn_step(
        fed, entry_two_grad, x, attended, c, mixed_flat, proj_weight, vectors
    )
    projected_grad, gain_terms, sum_down, gateup_rest, sum_proj = attend_back(
        query, heads, mixed_grad.reshape(HEADS, HD, patches), mixed, unit, factor, gains,
        cosine, sine, grad_down, gateup_left, grad_proj,
    )
    grad_qkv, entry_one_grad = back_step(
        projected_grad.reshape(3, width, patches), qkv_weight, entry_one
    )
    grad_latents, sums_one = last_step(entry_one_grad, x, middle_grad, scale_one)

    everything = ("img", "band")
    own_grad = jnp.concatenate(
        [
            sums_one[0],
            sums_one[1],
            sums_two[0],
            sums_two[1],
            sums_two[2],
            sums_two[3],
            jnp.sum(gain_terms, axis=2).reshape(-1),
        ]
    ).astype(bf16)
    gathered = lax.all_gather(own_grad[None], everything, axis=0, tiled=True)
    codes = lax.all_gather(
        jnp.stack([group_ids, labels], axis=1), "img", axis=0, tiled=True
    )
    modulation_all = gathered[:, : 6 * width]
    gain_sums = jnp.sum(gathered[:, 6 * width :].astype(f32), axis=0)
    sum_query_gain, sum_key_gain = gain_sums[:HD], gain_sums[HD:]
    features_all, before_all, condition_all = condition_of(codes[:, 0], codes[:, 1])
    before_grad = lax.dot_general(
        modulation_all, ada_weight, (((1,), (1,)), ((), ())), preferred_element_type=f32
    ) * silu_slope(before_all)
    ada_rows = width // lax.axis_size("img")
    ada_cols = 6 * width // bands
    time_rows = FREQ // lax.axis_size("img")
    time_cols = width // bands
    condition_part = lax.dynamic_slice_in_dim(condition_all, img_index * ada_rows, ada_rows, 1)
    modulation_part = lax.dynamic_slice_in_dim(modulation_all, band_index * ada_cols, ada_cols, 1)
    sum_ada = jnp.dot(condition_part.T, modulation_part, preferred_element_type=f32)
    features_part = lax.dynamic_slice_in_dim(features_all, img_index * time_rows, time_rows, 1)
    before_part = lax.dynamic_slice_in_dim(before_grad, band_index * time_cols, time_cols, 1)
    sum_time = jnp.dot(features_part.astype(f32).T, before_part, precision=highest)
    class_all = (codes[:, 1][:, None] == jnp.arange(NCLASS, dtype=jnp.int32)[None, :]).astype(f32)
    sum_class = jnp.dot(class_all.T, before_grad, precision=highest)
    sum_bias = jnp.sum(modulation_all.astype(f32), axis=0)

    sum_down = sum_down.reshape(-1, sum_down.shape[-1]).astype(f32)
    sum_proj = sum_proj.astype(f32)
    gateup = jnp.concatenate([gateup_done, gateup_rest], axis=0)
    sum_gateup = jnp.transpose(gateup, (2, 0, 1, 3)).reshape(gateup.shape[2], -1).astype(f32)
    part_qkv = lax.psum_scatter(grad_qkv, "img", scatter_dimension=0, tiled=True)
    sum_qkv = lax.psum_scatter(part_qkv, "band", scatter_dimension=1, tiled=True).astype(f32)
    return (
        give_back(result),
        give_back(grad_latents),
        sum_time,
        sum_class,
        sum_ada,
        sum_bias,
        sum_qkv,
        sum_query_gain,
        sum_key_gain,
        sum_proj,
        sum_gateup,
        sum_down,
    )


def per_device(latents, *others):
    devices = lax.axis_size("img")
    if latents.shape[0] == lax.axis_size("band") == 2 and devices >= 8 and devices & (devices - 1) == 0:
        return per_device_whole(latents, *others)
    return per_device_banded(latents, *others)


def solution(mesh):
    return jax.shard_map(
        per_device,
        mesh=mesh,
        in_specs=(
            P("img", "band", None),
            P("img", "band", None),
            P("img"),
            P("img"),
            P(),
            P("band"),
            P("band"),
            P(),
            P(),
            P(),
            P(),
            P(),
            P(),
            P(),
            P(),
            P(),
            P(),
        ),
        out_specs=(
            P("img", "band", None),
            P("img", "band", None),
            P("img", "band"),
            P(),
            P("img", "band"),
            P(),
            P("img", "band"),
            P(),
            P(),
            P("img", "band"),
            P("img", "band"),
            P("img", "band"),
        ),
        check_vma=False,
    )
```

```python
import functools
import math

import jax
import jax.numpy as jnp
from jax import lax
from jax.experimental import pallas as pl
from jax.experimental.pallas import tpu as pltpu
from jax.sharding import PartitionSpec as P

HEADS = 16
HD = 72
FF = 3072
NCLASS = 1000
FREQ = 256
GROUPS = 8


highest = lax.Precision.HIGHEST
epsilon = 1e-06


def unit_rms(values):
    return values * lax.rsqrt(jnp.mean(values * values, axis=-1, keepdims=True) + epsilon)


def unit_rms_back(values, grads):
    factor = lax.rsqrt(jnp.mean(values * values, axis=-1, keepdims=True) + epsilon)
    normed = values * factor
    return factor * (grads - normed * jnp.mean(grads * normed, axis=-1, keepdims=True))


def rope_tables(row_pos, col_pos, quarter):
    frequency = jnp.exp(-math.log(10000.0) * jnp.arange(quarter, dtype=jnp.float32) / quarter)
    row_angle = row_pos.astype(jnp.float32)[:, None] * frequency[None, :]
    col_angle = col_pos.astype(jnp.float32)[:, None] * frequency[None, :]
    cosine = jnp.concatenate(
        [jnp.cos(row_angle), jnp.cos(row_angle), jnp.cos(col_angle), jnp.cos(col_angle)], axis=-1
    )
    sine = jnp.concatenate(
        [-jnp.sin(row_angle), jnp.sin(row_angle), -jnp.sin(col_angle), jnp.sin(col_angle)], axis=-1
    )
    return (cosine, sine)


def partner(values, quarter):
    return jnp.concatenate(
        [
            values[..., quarter : 2 * quarter],
            values[..., :quarter],
            values[..., 3 * quarter :],
            values[..., 2 * quarter : 3 * quarter],
        ],
        axis=-1,
    )


def time_features(times, half):
    frequency = jnp.exp(-math.log(10000.0) * jnp.arange(half, dtype=jnp.float32) / half)
    angles = 1000.0 * times[:, None] * frequency[None, :]
    return jnp.concatenate([jnp.cos(angles), jnp.sin(angles)], axis=-1)


def silu_slope(values):
    sigma = jax.nn.sigmoid(values)
    return sigma * (1.0 + values * (1.0 - sigma))


def per_device_banded(
    latents,
    cotangent,
    labels,
    group_ids,
    group_logits,
    row_pos,
    col_pos,
    time_weight,
    class_table,
    ada_weight,
    ada_bias,
    qkv_weight,
    query_gain,
    key_gain,
    proj_weight,
    gateup_weight,
    down_weight,
):
    images, rows, width = latents.shape
    quarter = HD // 4
    scaling = HD ** (-0.5)
    group_hot = (group_ids[:, None] == jnp.arange(GROUPS, dtype=jnp.int32)[None, :]).astype(
        jnp.float32
    )
    times = jax.nn.sigmoid(jnp.dot(group_hot, group_logits, precision=highest))
    features = time_features(times, FREQ // 2).astype(jnp.bfloat16)
    class_hot = (labels[:, None] == jnp.arange(NCLASS, dtype=jnp.int32)[None, :]).astype(
        jnp.bfloat16
    )
    before = jnp.dot(features, time_weight, preferred_element_type=jnp.float32) + jnp.dot(
        class_hot, class_table, preferred_element_type=jnp.float32
    )
    condition = jax.nn.silu(before).astype(jnp.bfloat16)
    modulation = jnp.dot(condition, ada_weight, preferred_element_type=jnp.float32) + ada_bias
    pieces = [modulation[:, None, member * width : (member + 1) * width] for member in range(6)]
    shift_one, scale_one, gate_one, shift_two, scale_two, gate_two = pieces
    cosine, sine = rope_tables(row_pos, col_pos, quarter)
    cosine = cosine[None, :, None, :]
    sine = sine[None, :, None, :]

    def turned(values):
        return values * cosine + partner(values, quarter) * sine

    def turned_back(grads):
        return grads * cosine + partner(grads * sine, quarter)

    source = latents.astype(jnp.float32)
    normed_one = unit_rms(source)
    entry_one = (normed_one * (1.0 + scale_one) + shift_one).astype(jnp.bfloat16)
    projected = jnp.einsum("bpd,de->bpe", entry_one, qkv_weight, preferred_element_type=jnp.float32)
    shape = (images, rows, HEADS, HD)
    query_raw = projected[..., :width].reshape(shape)
    key_raw = projected[..., width : 2 * width].reshape(shape)
    value_bf = projected[..., 2 * width :].reshape(shape).astype(jnp.bfloat16)
    query_unit = unit_rms(query_raw)
    key_unit = unit_rms(key_raw)
    query_bf = turned(query_unit * query_gain).astype(jnp.bfloat16)
    key_bf = turned(key_unit * key_gain).astype(jnp.bfloat16)
    peak = jnp.full((images, HEADS, rows), -1e30, jnp.float32)
    key_piece = lax.all_gather(key_bf, "band", axis=1, tiled=True)
    value_piece = lax.all_gather(value_bf, "band", axis=1, tiled=True)
    scores = (
        jnp.einsum("bqhd,bkhd->bhqk", query_bf, key_piece, preferred_element_type=jnp.float32)
        * scaling
    )
    new_peak = jnp.maximum(peak, jnp.max(scores, axis=-1))
    weights = jnp.exp(scores - new_peak[..., None])
    total = jnp.sum(weights, axis=-1)
    update = jnp.einsum(
        "bhqk,bkhd->bqhd",
        weights.astype(jnp.bfloat16),
        value_piece,
        preferred_element_type=jnp.float32,
    )
    accum = update
    peak, total, accum = (new_peak, total, accum)
    mixed = accum / jnp.transpose(total, (0, 2, 1))[..., None]
    log_total = peak + jnp.log(total)
    mixed_bf = mixed.reshape(images, rows, width).astype(jnp.bfloat16)
    attended = jnp.einsum("bpd,de->bpe", mixed_bf, proj_weight, preferred_element_type=jnp.float32)
    middle = source + gate_one * attended
    normed_two = unit_rms(middle)
    entry_two = (normed_two * (1.0 + scale_two) + shift_two).astype(jnp.bfloat16)
    gate_up = jnp.einsum(
        "bpd,de->bpe", entry_two, gateup_weight, preferred_element_type=jnp.float32
    )
    gate_part = gate_up[..., :FF]
    up_part = gate_up[..., FF:]
    hidden = (jax.nn.silu(gate_part) * up_part).astype(jnp.bfloat16)
    fed = jnp.einsum("bpf,fd->bpd", hidden, down_weight, preferred_element_type=jnp.float32)
    result = (middle + gate_two * fed).astype(jnp.bfloat16)
    upstream = cotangent.astype(jnp.float32)
    fed_grad = (upstream * gate_two).astype(jnp.bfloat16)
    grad_gate_two = jnp.sum(upstream * fed, axis=1)
    grad_down = jnp.einsum("bpf,bpd->fd", hidden, fed_grad, preferred_element_type=jnp.float32)
    hidden_grad = jnp.einsum(
        "bpd,fd->bpf", fed_grad, down_weight, preferred_element_type=jnp.float32
    )
    gate_grad = hidden_grad * up_part * silu_slope(gate_part)
    up_grad = hidden_grad * jax.nn.silu(gate_part)
    gate_up_grad = jnp.concatenate([gate_grad, up_grad], axis=-1).astype(jnp.bfloat16)
    grad_gateup = jnp.einsum(
        "bpd,bpe->de", entry_two, gate_up_grad, preferred_element_type=jnp.float32
    )
    entry_two_grad = jnp.einsum(
        "bpe,de->bpd", gate_up_grad, gateup_weight, preferred_element_type=jnp.float32
    )
    grad_scale_two = jnp.sum(entry_two_grad * normed_two, axis=1)
    grad_shift_two = jnp.sum(entry_two_grad, axis=1)
    middle_grad = upstream + unit_rms_back(middle, entry_two_grad * (1.0 + scale_two))
    grad_gate_one = jnp.sum(middle_grad * attended, axis=1)
    attended_grad = (middle_grad * gate_one).astype(jnp.bfloat16)
    grad_proj = jnp.einsum(
        "bpd,bpe->de", mixed_bf, attended_grad, preferred_element_type=jnp.float32
    )
    mixed_grad = jnp.einsum(
        "bpe,de->bpd", attended_grad, proj_weight, preferred_element_type=jnp.float32
    )
    mixed_grad_bf = mixed_grad.reshape(shape).astype(jnp.bfloat16)
    offsets = jnp.transpose(jnp.sum(mixed_grad_bf.astype(jnp.float32) * mixed, axis=-1), (0, 2, 1))
    key_piece = lax.all_gather(key_bf, "band", axis=1, tiled=True)
    value_piece = lax.all_gather(value_bf, "band", axis=1, tiled=True)
    scores = (
        jnp.einsum("bqhd,bkhd->bhqk", query_bf, key_piece, preferred_element_type=jnp.float32)
        * scaling
    )
    probs = jnp.exp(scores - log_total[..., None])
    prob_grad = jnp.einsum(
        "bqhd,bkhd->bhqk", mixed_grad_bf, value_piece, preferred_element_type=jnp.float32
    )
    score_grad = (probs * (prob_grad - offsets[..., None])).astype(jnp.bfloat16)
    query_grad = (
        jnp.einsum("bhqk,bkhd->bqhd", score_grad, key_piece, preferred_element_type=jnp.float32)
        * scaling
    )
    key_term = (
        jnp.einsum("bhqk,bqhd->bkhd", score_grad, query_bf, preferred_element_type=jnp.float32)
        * scaling
    )
    value_term = jnp.einsum(
        "bhqk,bqhd->bkhd",
        probs.astype(jnp.bfloat16),
        mixed_grad_bf,
        preferred_element_type=jnp.float32,
    )
    key_grads = key_term
    value_grads = value_term
    query_grad, key_grads, value_grads = (query_grad, key_grads, value_grads)
    key_local, value_local = (
        lax.psum_scatter(
            key_grads.astype(jnp.bfloat16), "band", scatter_dimension=1, tiled=True
        ).astype(jnp.float32),
        lax.psum_scatter(
            value_grads.astype(jnp.bfloat16), "band", scatter_dimension=1, tiled=True
        ).astype(jnp.float32),
    )
    query_turned = turned_back(query_grad)
    key_turned = turned_back(key_local)
    local_query_gain = jnp.sum(query_turned * query_unit, axis=(0, 1, 2))
    local_key_gain = jnp.sum(key_turned * key_unit, axis=(0, 1, 2))
    query_raw_grad = unit_rms_back(query_raw, query_turned * query_gain)
    key_raw_grad = unit_rms_back(key_raw, key_turned * key_gain)
    flat = (images, rows, width)
    projected_grad = jnp.concatenate(
        [query_raw_grad.reshape(flat), key_raw_grad.reshape(flat), value_local.reshape(flat)],
        axis=-1,
    ).astype(jnp.bfloat16)
    grad_qkv = jnp.einsum(
        "bpd,bpe->de", entry_one, projected_grad, preferred_element_type=jnp.float32
    )
    entry_one_grad = jnp.einsum(
        "bpe,de->bpd", projected_grad, qkv_weight, preferred_element_type=jnp.float32
    )
    grad_scale_one = jnp.sum(entry_one_grad * normed_one, axis=1)
    grad_shift_one = jnp.sum(entry_one_grad, axis=1)
    source_grad = middle_grad + unit_rms_back(source, entry_one_grad * (1.0 + scale_one))
    grad_latents = source_grad.astype(jnp.bfloat16)
    band_partial = jnp.concatenate(
        [
            grad_shift_one,
            grad_scale_one,
            grad_gate_one,
            grad_shift_two,
            grad_scale_two,
            grad_gate_two,
        ],
        axis=-1,
    )
    modulation_grad, band_query_gain, band_key_gain = (
        lax.psum(band_partial.astype(jnp.bfloat16), "band").astype(jnp.float32),
        lax.psum(local_query_gain[None, :].astype(jnp.bfloat16), "band").astype(jnp.float32),
        lax.psum(local_key_gain[None, :].astype(jnp.bfloat16), "band").astype(jnp.float32),
    )
    condition_grad = jnp.dot(modulation_grad, ada_weight.astype(jnp.float32).T, precision=highest)
    before_grad = condition_grad * silu_slope(before)
    condition_all, features_all, modulation_all, before_all, query_gain_rows, key_gain_rows = (
        lax.all_gather(
            condition.astype(jnp.float32).astype(jnp.bfloat16), "img", axis=0, tiled=True
        ).astype(jnp.float32),
        lax.all_gather(
            features.astype(jnp.float32).astype(jnp.bfloat16), "img", axis=0, tiled=True
        ).astype(jnp.float32),
        lax.all_gather(modulation_grad.astype(jnp.bfloat16), "img", axis=0, tiled=True).astype(
            modulation_grad.dtype
        ),
        lax.all_gather(before_grad.astype(jnp.bfloat16), "img", axis=0, tiled=True).astype(
            before_grad.dtype
        ),
        lax.all_gather(band_query_gain.astype(jnp.bfloat16), "img", axis=0, tiled=True).astype(
            band_query_gain.dtype
        ),
        lax.all_gather(band_key_gain.astype(jnp.bfloat16), "img", axis=0, tiled=True).astype(
            band_key_gain.dtype
        ),
    )
    labels_all = lax.all_gather(labels, "img", axis=0, tiled=True)
    img_index = lax.axis_index("img")
    band_index = lax.axis_index("band")
    ada_rows = width // lax.axis_size("img")
    ada_cols = 6 * width // lax.axis_size("band")
    time_rows = FREQ // lax.axis_size("img")
    time_cols = width // lax.axis_size("band")
    condition_part = lax.dynamic_slice_in_dim(condition_all, img_index * ada_rows, ada_rows, 1)
    modulation_part = lax.dynamic_slice_in_dim(modulation_all, band_index * ada_cols, ada_cols, 1)
    sum_ada = jnp.dot(condition_part.T, modulation_part, precision=highest)
    features_part = lax.dynamic_slice_in_dim(features_all, img_index * time_rows, time_rows, 1)
    before_part = lax.dynamic_slice_in_dim(before_all, band_index * time_cols, time_cols, 1)
    sum_time = jnp.dot(features_part.T, before_part, precision=highest)
    class_all = (labels_all[:, None] == jnp.arange(NCLASS, dtype=jnp.int32)[None, :]).astype(
        jnp.float32
    )
    sum_class = jnp.dot(class_all.T, before_all, precision=highest)
    sum_bias = jnp.sum(modulation_all, axis=0)
    sum_query_gain = jnp.sum(query_gain_rows, axis=0)
    sum_key_gain = jnp.sum(key_gain_rows, axis=0)
    part_qkv, part_proj, part_gateup, part_down = (
        lax.psum_scatter(
            grad_qkv.astype(jnp.bfloat16), "img", scatter_dimension=0, tiled=True
        ).astype(jnp.float32),
        lax.psum_scatter(
            grad_proj.astype(jnp.bfloat16), "img", scatter_dimension=0, tiled=True
        ).astype(jnp.float32),
        lax.psum_scatter(
            grad_gateup.astype(jnp.bfloat16), "img", scatter_dimension=0, tiled=True
        ).astype(jnp.float32),
        lax.psum_scatter(
            grad_down.astype(jnp.bfloat16), "img", scatter_dimension=0, tiled=True
        ).astype(jnp.float32),
    )
    sum_qkv, sum_proj, sum_gateup, sum_down = (
        lax.psum_scatter(
            part_qkv.astype(jnp.bfloat16), "band", scatter_dimension=1, tiled=True
        ).astype(jnp.float32),
        lax.psum_scatter(
            part_proj.astype(jnp.bfloat16), "band", scatter_dimension=1, tiled=True
        ).astype(jnp.float32),
        lax.psum_scatter(
            part_gateup.astype(jnp.bfloat16), "band", scatter_dimension=1, tiled=True
        ).astype(jnp.float32),
        lax.psum_scatter(
            part_down.astype(jnp.bfloat16), "band", scatter_dimension=1, tiled=True
        ).astype(jnp.float32),
    )
    return (
        result,
        grad_latents,
        sum_time,
        sum_class,
        sum_ada,
        sum_bias,
        sum_qkv,
        sum_query_gain,
        sum_key_gain,
        sum_proj,
        sum_gateup,
        sum_down,
    )


HDP = 80
LOG2E = math.log2(math.e)
VMEM_MAX = 62 * 2**20
bf16 = jnp.bfloat16
f32 = jnp.float32


def dot(left, right, left_dim, right_dim):
    return lax.dot_general(
        left, right, (((left_dim,), (right_dim,)), ((), ())), preferred_element_type=f32
    )


def params_of(**extra):
    return pltpu.CompilerParams(vmem_limit_bytes=VMEM_MAX, **extra)


def whole(shape):
    return pl.BlockSpec(shape, lambda *_: (0,) * len(shape), pipeline_mode=pl.Buffered(1))


def cost(flops, bytes_accessed, transcendentals=0):
    return pl.CostEstimate(
        flops=int(flops), bytes_accessed=int(bytes_accessed), transcendentals=int(transcendentals)
    )


def partner_rows(values, low_half):
    quarter = HD // 4
    return jnp.where(
        low_half, pltpu.roll(values, HD - quarter, 0), pltpu.roll(values, quarter, 0)
    )


def low_half_mask(patches):
    row = lax.broadcasted_iota(jnp.int32, (HD, patches), 0)
    quarter = HD // 4
    return (row < quarter) | ((row >= 2 * quarter) & (row < 3 * quarter))


def tail_rows(first, second, patches):
    row = lax.broadcasted_iota(jnp.int32, (HDP - HD, patches), 0)
    return jnp.where(row == 0, first, jnp.where(row == 1, second, 0.0))


def split_two(values):
    high = values.astype(bf16).astype(f32)
    return high, values - high


MESH_ID = pl.DeviceIdType.MESH


def pair_axes():
    bits = lax.axis_size("img").bit_length() - 1
    return ["y"] + [f"b{bit}" for bit in reversed(range(bits))]


def own_places():
    img = lax.axis_index("img")
    places = {"y": lax.axis_index("band")}
    for bit in range(lax.axis_size("img").bit_length() - 1):
        places[f"b{bit}"] = lax.rem(lax.div(img, 2**bit), 2)
    return places


def partner_id(axis, places):
    if axis == "y":
        return {"band": 1 - places["y"]}
    bit = int(axis[1:])
    return {"img": lax.axis_index("img") + (1 - 2 * places[axis]) * 2**bit}


def greet(places):
    barrier = pltpu.get_barrier_semaphore()
    for axis in places:
        pl.semaphore_signal(
            barrier, inc=1, device_id=partner_id(axis, places), device_id_type=MESH_ID
        )
    pl.semaphore_wait(barrier, len(places))


def dispatch(value, cases):
    if not cases:
        return
    keys = sorted(cases)
    if len(keys) == 1:
        pl.when(value == keys[0])(cases[keys[0]])
        return
    middle = keys[len(keys) // 2]
    low = {key: cases[key] for key in keys if key < middle}
    high = {key: cases[key] for key in keys if key >= middle}
    pl.when(value < middle)(functools.partial(dispatch, value, low))
    pl.when(value >= middle)(functools.partial(dispatch, value, high))


class Halving:
    def __init__(self, places, dims, order, held, arrived, send, receive, lead=(), tail=()):
        self.places, self.dims, self.order = places, list(dims), list(order)
        self.held, self.arrived, self.send, self.receive = held, arrived, send, receive
        self.lead, self.tail = tuple(lead), tuple(tail)

    def source_index(self, mine):
        first = self.order[0]
        place = self.places[first] if mine else 1 - self.places[first]
        return [place if name == first else slice(None) for name in self.dims]

    def held_index(self, step, mine):
        picked = []
        for name in self.dims:
            place = self.order.index(name)
            if place == 0:
                continue
            if place < step:
                picked.append(self.places[name])
            elif place == step:
                picked.append(self.places[name] if mine else 1 - self.places[name])
            else:
                picked.append(slice(None))
        return picked

    def settled(self, step):
        picked = []
        for name in self.dims:
            place = self.order.index(name)
            if place > 0:
                picked.append(self.places[name] if place < step else slice(None))
        return self.lead + tuple(picked)

    def copy(self, step, source=None):
        if step == 0:
            block = source.at[tuple(self.source_index(False)) + self.tail]
        else:
            block = self.held.at[self.lead + tuple(self.held_index(step, False))]
        arrived = self.arrived[step]
        return pltpu.make_async_remote_copy(
            src_ref=block,
            dst_ref=arrived.at[self.lead] if self.lead else arrived,
            send_sem=self.send.at[self.lead + (step,)],
            recv_sem=self.receive.at[self.lead + (step,)],
            device_id=partner_id(self.order[step], self.places),
            device_id_type=MESH_ID,
        )

    def own_half(self, source, semaphore):
        return pltpu.make_async_copy(
            source.at[tuple(self.source_index(True)) + self.tail],
            self.held.at[self.lead] if self.lead else self.held,
            semaphore,
        )

    def add(self, step, source=None, put=None):
        picked = self.held_index(step, True)
        spot = self.lead + tuple(picked)
        if source is None:
            old = self.held[spot + (...,)]
        else:
            old = source[tuple(self.source_index(True)) + self.tail + (...,)]
        new = self.arrived[step][self.lead + (...,)]
        if step == len(self.order) - 1:
            put(old.astype(f32) + new.astype(f32))
        else:
            self.held[spot + (...,)] = old + new


class Doubling:
    def __init__(self, places, dims, order, blocks, send, receive):
        self.places, self.dims, self.order = places, list(dims), list(order)
        self.blocks, self.send, self.receive = blocks, send, receive

    def own(self):
        return tuple(self.places[name] for name in self.dims)

    def copy(self, step):
        known = self.order[:step]
        spot = tuple(slice(None) if n in known else self.places[n] for n in self.dims)
        return pltpu.make_async_remote_copy(
            src_ref=self.blocks.at[spot],
            dst_ref=self.blocks.at[spot],
            send_sem=self.send.at[step],
            recv_sem=self.receive.at[step],
            device_id=partner_id(self.order[step], self.places),
            device_id_type=MESH_ID,
        )


def doubling_order(dims):
    bits = [name for name in dims if name not in ("y", "b0", "b1")]
    return bits + ["y", "b1", "b0"]


def doubling_scratch(dims):
    return [pltpu.SemaphoreType.DMA((len(dims),))] * 2


def halving_scratch(dims, tail, lead=()):
    left = len(dims) - 1
    shapes = [lead + (2,) * left + tail]
    shapes += [lead + (2,) * (left - step) + tail for step in range(len(dims))]
    semaphores = pltpu.SemaphoreType.DMA(lead + (len(dims),))
    return [pltpu.VMEM(shape, bf16) for shape in shapes] + [semaphores, semaphores]


def order_of(dims, *first):
    rest = [name for name in reversed(dims) if name not in first]
    return list(first) + rest


def front_kernel(
    own_ref, other_ref, scale_ref, shift_ref, w_ref, gains_ref, cos_ref, sin_ref,
    entry_ref, heads_ref, unit_ref, factor_ref,
):
    section = pl.program_id(0)
    patches = entry_ref.shape[0]
    half = patches // 2

    @pl.when(section == 0)
    def _():
        for number, ref in enumerate((own_ref, other_ref)):
            source = ref[...].astype(f32)
            normed = source * lax.rsqrt(jnp.mean(source * source, axis=1, keepdims=True) + epsilon)
            entry_ref[number * half : (number + 1) * half, :] = (
                normed * (1.0 + scale_ref[...]) + shift_ref[...]
            ).astype(bf16)

    raw = dot(w_ref[...], entry_ref[...], 0, 1)

    @pl.when(section < 2)
    def _():
        mask = low_half_mask(patches)
        extra = tail_rows(*[jnp.where(section == 1, 1.0, 0.0)] * 2, patches)
        gain = gains_ref[0]
        for head in range(HEADS):
            part = raw[head * HD : (head + 1) * HD, :]
            factor = lax.rsqrt(jnp.mean(part * part, axis=0, keepdims=True) + epsilon)
            unit = part * factor
            scaled = unit * gain
            turned = scaled * cos_ref[...] + partner_rows(scaled, mask) * sin_ref[...]
            heads_ref[0, head] = jnp.concatenate([turned, extra], axis=0).astype(bf16)
            unit_ref[0, head] = unit.astype(bf16)
            factor_ref[0, head] = factor

    @pl.when(section == 2)
    def _():
        extra = tail_rows(1.0, 1.0, patches)
        for head in range(HEADS):
            part = raw[head * HD : (head + 1) * HD, :]
            heads_ref[0, head] = jnp.concatenate([part, extra], axis=0).astype(bf16)


def own_image(rows, width, block):
    return pl.BlockSpec((None, rows, width), lambda t: (lax.axis_index("band"), block(t), 0))


def front(images, other, scale, shift, qkv_weight, gains, cosine, sine):
    half, width = other.shape
    patches = 2 * half
    last = lambda s: jnp.minimum(s, 1)
    return pl.pallas_call(
        front_kernel,
        grid=(3,),
        in_specs=[
            own_image(half, width, lambda s: 0),
            whole((half, width)),
            whole((1, width)),
            whole((1, width)),
            pl.BlockSpec((width, width), lambda s: (0, s)),
            pl.BlockSpec((1, HD, 1), lambda s: (last(s), 0, 0)),
            whole((HD, patches)),
            whole((HD, patches)),
        ],
        out_specs=[
            pl.BlockSpec((patches, width), lambda s: (0, 0)),
            pl.BlockSpec((1, HEADS, HDP, patches), lambda s: (s, 0, 0, 0)),
            pl.BlockSpec((1, HEADS, HD, patches), lambda s: (last(s), 0, 0, 0)),
            pl.BlockSpec((1, HEADS, 1, patches), lambda s: (last(s), 0, 0, 0)),
        ],
        out_shape=[
            jax.ShapeDtypeStruct((patches, width), bf16),
            jax.ShapeDtypeStruct((3, HEADS, HDP, patches), bf16),
            jax.ShapeDtypeStruct((2, HEADS, HD, patches), bf16),
            jax.ShapeDtypeStruct((2, HEADS, 1, patches), f32),
        ],
        compiler_params=params_of(),
        cost_estimate=cost(6 * patches * width * width, 24e6),
        name="front",
    )(images, other, scale, shift, qkv_weight, gains, cosine, sine)


def attend_kernel(q_ref, k_ref, v_ref, mixed_ref, lse_ref, qext_ref):
    patches = q_ref.shape[-1]
    step = patches // 2
    key = k_ref[...]
    value = v_ref[...]
    for start in range(0, patches, step):
        columns = slice(start, start + step)
        scores = dot(key, q_ref[:, columns], 0, 0)
        weights = jnp.exp2(scores).astype(bf16)
        summed = dot(value, weights, 1, 0)
        total = summed[HD : HD + 1, :]
        mixed_ref[:, columns] = (summed[:HD, :] / total).astype(bf16)
        high, low = split_two(-jnp.log2(total))
        extra = jnp.concatenate([jnp.zeros((HD, step), f32), tail_rows(high, low, step)], axis=0)
        qext_ref[:, columns] = q_ref[:, columns] + extra.astype(bf16)


def attend(heads):
    patches = heads.shape[-1]
    section = lambda member: pl.BlockSpec(
        (None, None, HDP, patches), lambda h: (member, h, 0, 0)
    )
    return pl.pallas_call(
        lambda q, k, v, mixed, qext: attend_kernel(q, k, v, mixed, None, qext),
        grid=(HEADS,),
        in_specs=[section(0), section(1), section(2)],
        out_specs=[
            pl.BlockSpec((None, HD, patches), lambda h: (h, 0, 0)),
            pl.BlockSpec((None, HDP, patches), lambda h: (h, 0, 0)),
        ],
        out_shape=[
            jax.ShapeDtypeStruct((HEADS, HD, patches), bf16),
            jax.ShapeDtypeStruct((HEADS, HDP, patches), bf16),
        ],
        compiler_params=params_of(),
        cost_estimate=cost(8 * HEADS * patches * patches * HDP, 14e6, HEADS * patches * patches),
        name="attend",
    )(heads, heads, heads)


def middle_kernel(
    mixed_ref, w_ref, own_x_ref, other_x_ref, own_c_ref, other_c_ref, vectors_ref,
    attended_ref, entry_ref, fed_grad_ref,
):
    in_own = pl.program_id(0) < pl.num_programs(0) // 2
    x = jnp.where(in_own, own_x_ref[...].astype(f32), other_x_ref[...].astype(f32))
    c = jnp.where(in_own, own_c_ref[...].astype(f32), other_c_ref[...].astype(f32))
    attended = dot(mixed_ref[...], w_ref[...], 0, 0)
    attended_bf = attended.astype(bf16)
    attended_ref[...] = attended_bf
    gate_one, scale_two, shift_two, gate_two = [vectors_ref[i : i + 1, :] for i in range(4)]
    middle = x + gate_one * attended_bf.astype(f32)
    normed = middle * lax.rsqrt(jnp.mean(middle * middle, axis=1, keepdims=True) + epsilon)
    entry_ref[...] = (normed * (1.0 + scale_two) + shift_two).astype(bf16)
    fed_grad_ref[...] = (c * gate_two).astype(bf16)


def middle_step(mixed, proj_weight, latents, other_x, cotangent, other_c, vectors):
    half, width = other_x.shape
    patches = 2 * half
    rows = 256
    blocks = half // rows
    block = pl.BlockSpec((rows, width), lambda t: (t, 0))
    own = own_image(rows, width, lambda t: jnp.minimum(t, blocks - 1))
    other = pl.BlockSpec((rows, width), lambda t: (jnp.maximum(t - blocks, 0), 0))
    return pl.pallas_call(
        middle_kernel,
        grid=(patches // rows,),
        in_specs=[
            pl.BlockSpec((width, rows), lambda t: (0, t)),
            whole((width, width)),
            own,
            other,
            own,
            other,
            whole((8, width)),
        ],
        out_specs=[block] * 3,
        out_shape=[jax.ShapeDtypeStruct((patches, width), bf16)] * 3,
        compiler_params=params_of(),
        cost_estimate=cost(2 * patches * width * width, 17e6),
        name="middle",
    )(mixed, proj_weight, latents, other_x, cotangent, other_c, vectors)


MLP_TILE = 512
MLP_SUB = 256
HOSTED = 5
CARRIED = ((3, 4), (4, 2))


def mlp_kernel(
    dims, entry_ref, fed_grad_ref, wg_ref, wu_ref, wd_ref,
    fed_ref, entry_grad_ref, down_ref, done_ref, left_ref, *rest,
):
    carry_refs, rest = rest[: 2 * len(CARRIED)], rest[2 * len(CARRIED) :]
    hidden_ref, gate_grad_ref, up_grad_ref, source_ref, left_sem, held, *arrived, send, receive = rest
    tile = pl.program_id(0)
    places = own_places()
    orders = mlp_orders(dims)
    steps = len(dims)

    def streams(number):
        slot = lax.rem(number, 2)
        return [
            Halving(places, dims, orders[sub], held, arrived, send, receive, (slot, sub))
            for sub in range(2)
        ]

    def advance(number, step):
        @pl.when((number >= 0) & (number < HOSTED))
        def _():
            for sub, stream in enumerate(streams(number)):
                source = source_ref.at[sub]
                stream.copy(step, source).wait()

                def put(values):
                    done_ref[number, sub] = values.astype(bf16)

                stream.add(step, source if step == 0 else None, put)
                leaves = [place for place, (_, ended) in enumerate(CARRIED) if ended == step + 1]
                for place in leaves:

                    @pl.when(number == CARRIED[place][0])
                    def _():
                        carry_refs[2 * place + sub][...] = held[stream.settled(step + 1)]

                if step + 1 < steps:
                    goes_on = True
                    for place in leaves:
                        goes_on = goes_on & (number != CARRIED[place][0])
                    if leaves:
                        pl.when(goes_on)(stream.copy(step + 1).start)
                    else:
                        stream.copy(step + 1).start()

    @pl.when(tile == 0)
    def _():
        fed_ref[...] = jnp.zeros_like(fed_ref)
        entry_grad_ref[...] = jnp.zeros_like(entry_grad_ref)
        greet(places)

    entry = entry_ref[...]
    fed_grad = fed_grad_ref[...]
    gate = dot(entry, wg_ref[...], 1, 0)
    up = dot(entry, wu_ref[...], 1, 0)
    sigma = jax.nn.sigmoid(gate)
    silu = gate * sigma
    hidden_ref[...] = (silu * up).astype(bf16)
    hidden_grad = dot(fed_grad, wd_ref[...], 1, 1)
    gate_grad_ref[...] = (hidden_grad * up * (sigma * (1.0 + gate * (1.0 - sigma)))).astype(bf16)
    up_grad_ref[...] = (hidden_grad * silu).astype(bf16)
    advance(tile - 3, 4)
    advance(tile - 2, 2)
    advance(tile - 1, 0)
    fed_ref[...] += dot(hidden_ref[...], wd_ref[...], 1, 0)
    entry_grad_ref[...] += dot(gate_grad_ref[...], wg_ref[...], 1, 1) + dot(
        up_grad_ref[...], wu_ref[...], 1, 1
    )
    down = dot(hidden_ref[...], fed_grad, 0, 0).astype(bf16)
    column_half = down.shape[1] // 2
    down_ref[0] = down[:, :column_half]
    down_ref[1] = down[:, column_half:]
    grads = [dot(entry, ref[...], 0, 0) for ref in (gate_grad_ref, up_grad_ref)]
    blocks = 2 ** (steps - 1)
    rows = grads[0].shape[0] // blocks
    for half, grad in enumerate(grads):
        for block in range(blocks):
            spot = tuple(block // 2**bit % 2 for bit in reversed(range(steps - 1)))
            part = grad[block * rows : (block + 1) * rows, :].astype(bf16)
            for sub in range(2):
                source_ref[(sub, half) + spot] = part[:, sub * MLP_SUB : (sub + 1) * MLP_SUB]

    @pl.when(tile < HOSTED)
    def _():
        for sub, stream in enumerate(streams(tile)):
            stream.copy(0, source_ref.at[sub]).start()

    @pl.when(tile == HOSTED)
    def _():
        pltpu.make_async_copy(source_ref, left_ref, left_sem).start()

    advance(tile - 2, 3)
    advance(tile - 1, 1)

    @pl.when(tile == HOSTED)
    def _():
        pltpu.make_async_copy(source_ref, left_ref, left_sem).wait()


def mlp_orders(dims):
    return [order_of(dims, "b0", "y", "b2", "b1"), order_of(dims, "b0", "b1", "y", "b2")]


def carried_orders(dims):
    return [order[ended:] for _, ended in CARRIED for order in mlp_orders(dims)]


def carried_dims(dims):
    return [[name for name in dims if name in order] for order in carried_orders(dims)]


def mlp(entry, fed_grad, gateup_weight, down_weight):
    patches, width = entry.shape
    inner = down_weight.shape[0]
    tile = MLP_TILE
    tiles = inner // tile
    dims = pair_axes()
    rows = width // lax.axis_size("img")
    tail = (rows, MLP_SUB)
    carried = [(2,) * len(names) + tail for names in carried_dims(dims)]
    return pl.pallas_call(
        functools.partial(mlp_kernel, dims),
        grid=(tiles,),
        in_specs=[
            whole((patches, width)),
            whole((patches, width)),
            pl.BlockSpec((width, tile), lambda t: (0, t)),
            pl.BlockSpec((width, tile), lambda t: (0, tiles + t)),
            pl.BlockSpec((tile, width), lambda t: (t, 0)),
        ],
        out_specs=[
            whole((patches, width)),
            whole((patches, width)),
            pl.BlockSpec((2, tile, width // 2), lambda t: (0, t, 0)),
            whole((HOSTED - len(CARRIED), 2) + tail),
            pl.BlockSpec(memory_space=pl.ANY),
        ]
        + [whole(shape) for shape in carried],
        out_shape=[
            jax.ShapeDtypeStruct((patches, width), f32),
            jax.ShapeDtypeStruct((patches, width), f32),
            jax.ShapeDtypeStruct((2, inner, width // 2), bf16),
            jax.ShapeDtypeStruct((HOSTED - len(CARRIED), 2) + tail, bf16),
            jax.ShapeDtypeStruct((2,) + (2,) * len(dims) + tail, bf16),
        ]
        + [jax.ShapeDtypeStruct(shape, bf16) for shape in carried],
        scratch_shapes=[pltpu.VMEM((patches, tile), bf16)] * 3
        + [pltpu.VMEM((2,) + (2,) * len(dims) + tail, bf16), pltpu.SemaphoreType.DMA]
        + halving_scratch(dims, tail, (2, 2)),
        compiler_params=params_of(collective_id=0, has_side_effects=True),
        cost_estimate=cost(18 * patches * width * inner, 56e6),
        name="mlp",
    )(entry, fed_grad, gateup_weight, gateup_weight, down_weight)


TURN_ROWS = 128


def core_plan(dims):
    return [
        ("down", 0, order_of(dims, "b0", "y", "b1", "b2", "b3"), (2, 9, 25, 31, 35, 40)),
        ("down", 1, order_of(dims, "b0", "b2", "y", "b3", "b1"), (2, 9, 23, 27, 33, 35)),
        ("down", 2, order_of(dims, "b0", "b2", "b3", "b1", "y"), (0, 6, 21, 31, 35, 37)),
        ("down", 3, order_of(dims, "b0", "b1", "b2", "y", "b3"), (2, 9, 23, 31, 35, 40)),
        ("left", 0, order_of(dims, "b0", "b1", "y", "b2", "b3"), (1, 6, 11, 21, 25, 29)),
        ("left", 1, order_of(dims, "b0", "b2", "b1", "b3", "y"), (0, 3, 9, 15, 19, 21)),
        ("proj", 0, order_of(dims, "b0", "b1", "y", "b2", "b3"), (7, 11, 27, 33, 37, 44)),
        ("carry", 0, ["b3"], (0, 3)),
        ("carry", 1, ["b3"], (0, 3)),
        ("carry", 2, ["b2", "b1", "b3"], (0, 4, 6, 9)),
        ("carry", 3, ["y", "b2", "b3"], (0, 7, 11, 15)),
    ]


def core_kernel(
    dims, fed_ref, entry_grad_ref, own_x_ref, other_x_ref, own_c_ref, other_c_ref, attended_ref,
    all_mixed_ref, w_ref, vectors_ref, codes_ref,
    q_ref, k_ref, v_ref, mixed_ref, unit_ref, factor_ref, gains_ref, cos_ref, sin_ref,
    down_ref, left_ref, *rest,
):
    carry_refs, rest = rest[: 2 * len(CARRIED)], rest[2 * len(CARRIED) :]
    (
        result_ref, middle_grad_ref, out_ref, gain_out_ref,
        down_out_ref, left_out_ref, carry_out_ref, proj_out_ref, modes_out_ref,
        attended_grad_ref, mixed_grad_ref, proj_ref, rows_ref, row_send, row_receive,
        mg_ext_ref, acc_ref, own_sem, modes_ref, doubling_send, doubling_receive, *buffers,
    ) = rest
    step = pl.program_id(0)
    places = own_places()
    patches = q_ref.shape[-1]
    turns = patches // TURN_ROWS
    axes = len(dims)
    carries = carried_dims(dims)
    groups, used = {}, 0
    kinds = [("down", axes), ("left", axes), ("proj", axes)]
    kinds += [(f"carry{part}", len(names)) for part, names in enumerate(carries)]
    for name, count in kinds:
        groups[name] = buffers[used : used + count + 3]
        used += count + 3

    def streams():
        for number, (name, part, order, points) in enumerate(core_plan(dims)):
            names, lead, tail = dims, (), ()
            if name == "down":
                lead = (part,)
                source = down_ref
                rows = source.shape[-2] // 4
                tail = (pl.ds(part * rows, rows), slice(None))
                out, spot = down_out_ref, (part,)
            elif name == "left":
                lead = (part,)
                source = left_ref.at[part]
                out, spot = left_out_ref, (part,)
            elif name == "proj":
                source, out, spot = proj_ref, proj_out_ref, ()
            else:
                names = carries[part]
                source = carry_refs[part]
                out, spot = carry_out_ref, (part,)
            held, *arrived, send, receive = groups[name if name in groups else f"{name}{part}"]
            stream = Halving(places, names, order, held, arrived, send, receive, lead, tail)
            yield number, name, stream, source, points, out, spot

    def events(point):
        for number, name, stream, source, points, out, spot in streams():
            local = name in ("proj", "carry")
            steps = len(points) - 1
            for phase in range(-1, steps):
                if points[phase + 1] != point:
                    continue
                if phase >= 0:
                    stream.copy(phase, source).wait()
                    if phase == 0 and not local:
                        stream.own_half(source, own_sem.at[number]).wait()

                    def put(values):
                        out[spot + (...,)] = values.astype(bf16)

                    stream.add(phase, source if local and phase == 0 else None, put)
                if phase + 1 < steps:
                    stream.copy(phase + 1, source).start()
                    if phase < 0 and not local:
                        stream.own_half(source, own_sem.at[number]).start()

    band = places["y"]

    def away(number):
        return pltpu.make_async_remote_copy(
            src_ref=rows_ref.at[number],
            dst_ref=result_ref.at[band, pl.ds(number * TURN_ROWS, TURN_ROWS)],
            send_sem=row_send.at[number],
            recv_sem=row_receive.at[number],
            device_id=partner_id("y", places),
            device_id_type=MESH_ID,
        )

    def stay(number):
        return pltpu.make_async_copy(
            rows_ref.at[number + turns // 2],
            result_ref.at[band, pl.ds(number * TURN_ROWS, TURN_ROWS)],
            row_send.at[number + turns // 2],
        )

    @pl.when(step == 0)
    def _():
        greet(places)

    doubling = Doubling(places, dims, doubling_order(dims), modes_ref, doubling_send, doubling_receive)
    width = w_ref.shape[0]
    half = width // 2
    pair = 2 * TURN_ROWS

    def turn(number):
        x_ref, c_ref = (own_x_ref, own_c_ref) if number >= turns // 2 else (other_x_ref, other_c_ref)
        gate_one, scale_two, _, gate_two = [vectors_ref[i : i + 1, :] for i in range(4)]
        attended = attended_ref[...].astype(f32)
        upstream = c_ref[...].astype(f32)
        fed = fed_ref[...]
        middle = x_ref[...].astype(f32) + gate_one * attended
        rows_ref[number] = (middle + gate_two * fed).astype(bf16)
        factor = lax.rsqrt(jnp.mean(middle * middle, axis=1, keepdims=True) + epsilon)
        normed = middle * factor
        entry_grad = entry_grad_ref[...]
        inner = entry_grad * (1.0 + scale_two)
        middle_grad = upstream + factor * (
            inner - normed * jnp.mean(inner * normed, axis=1, keepdims=True)
        )
        middle_grad_ref[...] = middle_grad
        start = (number + turns // 2) % turns * TURN_ROWS
        attended_grad_ref[start : start + TURN_ROWS, :] = (middle_grad * gate_one).astype(bf16)
        add = lambda v: jnp.sum(v, axis=0, keepdims=True)
        sums = jnp.concatenate(
            [
                add(middle_grad * attended),
                add(entry_grad),
                add(entry_grad * normed),
                add(upstream * fed),
            ],
            axis=0,
        )
        if number == 0:
            modes_ref[doubling.own() + (slice(None), slice(0, width))] = sums
            modes_ref[doubling.own() + (slice(None), slice(width, None))] = codes_ref[...]
        else:
            modes_ref[doubling.own() + (slice(None), slice(0, width))] += sums
        if number < turns // 2:
            away(number).start()
        else:
            stay(number - turns // 2).start()
        if number % 2 == 1:
            first = start - TURN_ROWS
            grads = dot(w_ref[...], attended_grad_ref[first : first + pair, :], 1, 1)
            for head in range(HEADS):
                mixed_grad_ref[head, :, first : first + pair] = grads[
                    head * HD : (head + 1) * HD, :
                ].astype(bf16)
        if number == turns - 1:
            blocks = 2 ** (axes - 1)
            rows = width // blocks
            grads = dot(all_mixed_ref[...], attended_grad_ref[...], 1, 0)
            for block in range(blocks):
                spot = tuple(block // 2**bit % 2 for bit in reversed(range(axes - 1)))
                part = grads[block * rows : (block + 1) * rows, :]
                proj_ref[(0,) + spot] = part[:, :half].astype(bf16)
                proj_ref[(1,) + spot] = part[:, half:].astype(bf16)
            doubling.copy(0).start()
        events(number)

    for number in range(turns):

        @pl.when(step == number)
        def _():
            turn(number)

    points = {point for plan in core_plan(dims) for point in plan[3]}

    class Events:
        @staticmethod
        def at_head(head, end):
            def run(now):
                if turns + 2 * now + end in points:
                    events(turns + 2 * now + end)
                turn, odd = divmod(now - 2, 2)
                if end and odd == 0 and 0 <= turn < axes:
                    doubling.copy(turn).wait()
                    if turn + 1 < axes:
                        doubling.copy(turn + 1).start()

            wanted = [
                now
                for now in range(HEADS)
                if turns + 2 * now + end in points or (end and now in range(2, 2 + 2 * axes, 2))
            ]
            dispatch(head, {now: functools.partial(run, now) for now in wanted})

    @pl.when(step >= turns)
    def _():
        attend_back(
            step - turns, Events(), mixed_grad_ref,
            q_ref, k_ref, v_ref, mixed_ref, unit_ref, factor_ref, gains_ref, cos_ref, sin_ref,
            out_ref, gain_out_ref, mg_ext_ref, acc_ref,
        )

    @pl.when(step == pl.num_programs(0) - 1)
    def _():
        last = max(point for stream in core_plan(dims) for point in stream[3])
        for point in range(turns + 2 * HEADS, last + 1):
            events(point)
        modes_out_ref[...] = modes_ref[...]
        for number in range(turns // 2):
            away(number).wait()
            stay(number).wait()


def attend_back(
    head, events, mixed_grad_ref,
    q_ref, k_ref, v_ref, mixed_ref, unit_ref, factor_ref, gains_ref, cos_ref, sin_ref,
    out_ref, gain_out_ref, mg_ext_ref, acc_ref,
):
    patches = q_ref.shape[-1]
    step = patches // 2
    scaling = HD ** (-0.5)
    mixed_grad = mixed_grad_ref[head].astype(f32)
    offsets = jnp.sum(mixed_grad * mixed_ref[...].astype(f32), axis=0, keepdims=True)
    high, low = split_two(-offsets)
    mg_ext_ref[...] = jnp.concatenate(
        [mixed_grad, tail_rows(high, low, patches)], axis=0
    ).astype(bf16)
    key = k_ref[...]
    value = v_ref[...]
    for start in range(0, patches, step):
        columns = slice(start, start + step)
        query = q_ref[:, columns]
        grads = mg_ext_ref[:, columns]
        probs = jnp.exp2(dot(key, query, 0, 0))
        score_grad = (probs * dot(value, grads, 0, 0)).astype(bf16)
        probs_bf = probs.astype(bf16)
        acc_ref[0, :, columns] = dot(key, score_grad, 1, 0)
        key_term = dot(query, score_grad, 1, 1)
        value_term = dot(grads, probs_bf, 1, 1)
        if start == 0:
            acc_ref[1] = key_term
            acc_ref[2] = value_term
            events.at_head(head, 0)
        else:
            acc_ref[1] += key_term
            acc_ref[2] += value_term
    mask = low_half_mask(patches)
    for member, weight in ((0, scaling), (1, 1.0 / LOG2E)):
        grads = acc_ref[member, :HD, :] * weight
        turned = grads * cos_ref[...] + partner_rows(grads * sin_ref[...], mask)
        unit = unit_ref[member].astype(f32)
        product = turned * unit

        @pl.when(head == 0)
        def _():
            gain_out_ref[member] = product

        @pl.when(head > 0)
        def _():
            gain_out_ref[member] += product

        inner = turned * gains_ref[member]
        raw = factor_ref[member] * (inner - unit * jnp.mean(inner * unit, axis=0, keepdims=True))
        out_ref[member] = raw.astype(bf16)
    out_ref[2] = acc_ref[2, :HD, :].astype(bf16)
    events.at_head(head, 1)


def core_step(
    fed, entry_grad, latents, other_x, cotangent, other_c, attended, mixed, proj_weight, vectors,
    codes, query, heads, unit, factor, gains, cosine, sine, down, left, carries,
):
    half, width = other_x.shape
    patches = 2 * half
    dims = pair_axes()
    turns = patches // TURN_ROWS
    devices = lax.axis_size("img")
    split = (2,) * len(dims)
    down = down.reshape(split + (down.shape[1] // devices, down.shape[2]))
    down_tail = (down.shape[-2] // 4, down.shape[-1])
    left_tail = left.shape[-2:]
    proj_tail = (width // devices, width // 2)
    row_block = lambda t: lax.rem(jnp.minimum(t, turns - 1) + turns // 2, turns)
    block = pl.BlockSpec((TURN_ROWS, width), lambda t: (row_block(t), 0))
    own = own_image(TURN_ROWS, width, lambda t: jnp.clip(t - turns // 2, 0, turns // 2 - 1))
    other = pl.BlockSpec((TURN_ROWS, width), lambda t: (jnp.minimum(t, turns // 2 - 1), 0))
    head_of = lambda t: jnp.maximum(t - turns, 0)
    section = lambda member: pl.BlockSpec(
        (None, None, HDP, patches), lambda t: (member, head_of(t), 0, 0)
    )
    single = lambda rows: pl.BlockSpec((None, rows, patches), lambda t: (head_of(t), 0, 0))
    couple = lambda rows: pl.BlockSpec((2, None, rows, patches), lambda t: (0, head_of(t), 0, 0))
    anywhere = pl.BlockSpec(memory_space=pl.ANY)
    sums = [(4,) + down_tail, (2,) + left_tail, (len(carries),) + left_tail, proj_tail, ()]
    sums[-1] = split + (codes.shape[0], width + codes.shape[1])
    return pl.pallas_call(
        functools.partial(core_kernel, dims),
        grid=(turns + HEADS,),
        in_specs=[
            block,
            block,
            own,
            other,
            own,
            other,
            block,
            whole((width, patches)),
            whole((width, width)),
            whole((8, width)),
            whole(codes.shape),
            single(HDP),
            section(1),
            section(2),
            single(HD),
            couple(HD),
            couple(1),
            whole((2, HD, 1)),
            whole((HD, patches)),
            whole((HD, patches)),
            anywhere,
            anywhere,
        ]
        + [whole(carry.shape) for carry in carries],
        out_specs=[
            anywhere,
            block,
            pl.BlockSpec((3, None, HD, patches), lambda t: (0, head_of(t), 0, 0)),
            whole((2, HD, patches)),
        ]
        + [whole(shape) for shape in sums],
        out_shape=[
            jax.ShapeDtypeStruct((2, half, width), bf16),
            jax.ShapeDtypeStruct((patches, width), f32),
            jax.ShapeDtypeStruct((3, HEADS, HD, patches), bf16),
            jax.ShapeDtypeStruct((2, HD, patches), f32),
        ]
        + [jax.ShapeDtypeStruct(shape, bf16) for shape in sums[:-1]]
        + [jax.ShapeDtypeStruct(sums[-1], f32)],
        scratch_shapes=[
            pltpu.VMEM((patches, width), bf16),
            pltpu.VMEM((HEADS, HD, patches), bf16),
            pltpu.VMEM(split + proj_tail, bf16),
            pltpu.VMEM((turns, TURN_ROWS, width), bf16),
            pltpu.SemaphoreType.DMA((turns,)),
            pltpu.SemaphoreType.DMA((turns // 2,)),
            pltpu.VMEM((HDP, patches), bf16),
            pltpu.VMEM((3, HDP, patches), f32),
            pltpu.SemaphoreType.DMA((len(core_plan(dims)),)),
            pltpu.VMEM(sums[-1], f32),
        ]
        + doubling_scratch(dims)
        + halving_scratch(dims, down_tail, (4,))
        + halving_scratch(dims, left_tail, (2,))
        + halving_scratch(dims, proj_tail)
        + [ref for names in carried_dims(dims) for ref in halving_scratch(names, left_tail)],
        compiler_params=params_of(collective_id=1, has_side_effects=True),
        cost_estimate=cost(24 * HEADS * patches * patches * HDP, 70e6, HEADS * patches**2),
        name="core",
    )(
        fed, entry_grad, latents, other_x, cotangent, other_c, attended, mixed, proj_weight,
        vectors, codes, query, heads, heads, mixed.reshape(HEADS, HD, patches), unit, factor,
        gains, cosine, sine, down, left, *carries,
    )


BACK_ROWS = 256


def tail_plan(dims):
    return [
        ("pair", pl.ds(0, 384), order_of(dims, "b0", "b1", "y", "b3", "b2"), (1, 4, 9, 27, 36, 40)),
        ("pair", pl.ds(384, 384), order_of(dims, "b0", "y", "b1", "b2", "b3"), (1, 4, 18, 27, 35, 40)),
        ("pair", pl.ds(768, 384), order_of(dims, "b0", "b2", "b1", "b3", "y"), (1, 4, 15, 24, 33, 39)),
        ("single", None, order_of(dims, "b0", "b2", "b1", "y", "b3"), (2, 5, 25, 35, 45, 51)),
    ]


def back_kernel(
    dims, pg_ref, w_ref, entry_ref, own_x_ref, other_x_ref, middle_grad_ref, scale_ref,
    gain_terms_ref,
    latents_out_ref, sums_out_ref, pair_out_ref, single_out_ref,
    entry_grad_ref, pair_ref, single_ref, rows_ref, row_send, row_receive, *buffers,
):
    step = pl.program_id(0)
    places = own_places()
    phases = len(dims)
    size = phases + 3
    *buffers, sums_ref, send, receive = buffers
    streams = []
    for place, (name, columns, order, when) in enumerate(tail_plan(dims)):
        held, *arrived, s, r = buffers[place * size : (place + 1) * size]
        tail = () if columns is None else (slice(None), columns)
        stream = Halving(places, dims, order, held, arrived, s, r, (), tail)
        if name == "pair":
            streams.append((stream, pair_ref, when, pair_out_ref.at[:, columns]))
        else:
            streams.append((stream, single_ref, when, single_out_ref))
    doubling = Doubling(places, dims, doubling_order(dims), sums_ref, send, receive)
    width = entry_grad_ref.shape[0]
    half = width // 2
    blocks = 2 ** (phases - 1)
    rows = width // blocks

    @pl.when(step == 0)
    def _():
        entry_grad_ref[...] = jnp.zeros_like(entry_grad_ref)
        greet(places)

    @pl.when(step < 3)
    def _():
        grad = dot(entry_ref[...], pg_ref[...], 0, 1)

        def spot(block):
            return tuple(block // 2**bit % 2 for bit in reversed(range(phases - 1)))

        def part(block):
            return grad[block * rows : (block + 1) * rows, :]

        @pl.when(step < 2)
        def _():
            for block in range(blocks):
                pair_ref[(step,) + spot(block)] = part(block).astype(bf16)

        @pl.when(step == 2)
        def _():
            for block in range(blocks):
                single_ref[(0,) + spot(block)] = part(block)[:, :half].astype(bf16)
                single_ref[(1,) + spot(block)] = part(block)[:, half:].astype(bf16)

    @pl.when((step >= 3) & (step < 6))
    def _():
        entry_grad_ref[...] += dot(w_ref[...], pg_ref[...], 1, 0)

    band = places["y"]

    def away(number):
        return pltpu.make_async_remote_copy(
            src_ref=rows_ref.at[number],
            dst_ref=latents_out_ref.at[band, pl.ds(number * BACK_ROWS, BACK_ROWS)],
            send_sem=row_send.at[number],
            recv_sem=row_receive.at[number],
            device_id=partner_id("y", places),
            device_id_type=MESH_ID,
        )

    def stay(number):
        return pltpu.make_async_copy(
            rows_ref.at[number + 2],
            latents_out_ref.at[band, pl.ds(number * BACK_ROWS, BACK_ROWS)],
            row_send.at[number + 2],
        )

    for number in range(4):
        block = (number + 2) % 4

        @pl.when(step == 6 + number)
        def _():
            entry_grad = entry_grad_ref[:, block * BACK_ROWS : (block + 1) * BACK_ROWS].T
            source = (other_x_ref if number < 2 else own_x_ref)[...].astype(f32)
            factor = lax.rsqrt(jnp.mean(source * source, axis=1, keepdims=True) + epsilon)
            normed = source * factor
            inner = entry_grad * (1.0 + scale_ref[...])
            grads = middle_grad_ref[...] + factor * (
                inner - normed * jnp.mean(inner * normed, axis=1, keepdims=True)
            )
            rows_ref[number] = grads.astype(bf16)
            add = lambda v: jnp.sum(v, axis=0, keepdims=True)
            sums = jnp.concatenate([add(entry_grad), add(entry_grad * normed)], axis=0)
            if number == 0:
                sums_ref[doubling.own() + (slice(0, 2),)] = sums
                sums_ref[doubling.own() + (slice(2, 4),)] = gain_terms_ref[...]
            else:
                sums_ref[doubling.own() + (slice(0, 2),)] += sums
            if number < 2:
                away(number).start()
            else:
                stay(number - 2).start()

    def due(now):
        for stream, source, when, out in streams:
            for phase in range(-1, phases):
                if when[phase + 1] != now:
                    continue
                if phase >= 0:
                    stream.copy(phase, source).wait()

                    def put(values):
                        out[...] = values.astype(bf16)

                    stream.add(phase, source if phase == 0 else None, put)
                if phase + 1 < phases:
                    stream.copy(phase + 1, source).start()

    for now in range(1, 10):

        @pl.when(step == now)
        def _():
            if now == 9:
                doubling.copy(0).start()
            due(now)
            if now == 9:
                last = max(point for plan in tail_plan(dims) for point in plan[3])
                for later in range(10, last + 1):
                    due(later)
                    turn, odd = divmod(later - 12, 3)
                    if odd == 0 and 0 <= turn < phases:
                        doubling.copy(turn).wait()
                        if turn + 1 < phases:
                            doubling.copy(turn + 1).start()
                sums_out_ref[...] = sums_ref[...]
                for number in range(2):
                    away(number).wait()
                    stay(number).wait()


def back_step(
    projected_grad, qkv_weight, entry, latents, other_x, middle_grad, scale, gain_rows
):
    patches, width = entry.shape
    dims = pair_axes()
    rows = width // lax.axis_size("img")
    sections = (0, 2, 1, 0, 1, 2)

    def section_of(step):
        place = jnp.int32(sections[-1])
        for number, section in enumerate(sections[:-1]):
            place = jnp.where(step == number, section, place)
        return place

    weight_section = lambda t: jnp.where(t < 4, 0, jnp.minimum(t - 3, 2))
    row_block = lambda t: lax.rem(jnp.clip(t - 6, 0, 3) + 2, 4)
    block = pl.BlockSpec((BACK_ROWS, width), lambda t: (row_block(t), 0))
    own = own_image(BACK_ROWS, width, lambda t: jnp.clip(t - 8, 0, 1))
    other = pl.BlockSpec((BACK_ROWS, width), lambda t: (jnp.clip(t - 6, 0, 1), 0))
    tails = [(rows, 384)] * 3 + [(rows, width // 2)]
    sums = [(rows, width), (rows, width // 2)]
    wide = (2,) * len(dims)
    scratch = [
        pltpu.VMEM((width, patches), f32),
        pltpu.VMEM(wide + (rows, width), bf16),
        pltpu.VMEM(wide + (rows, width // 2), bf16),
        pltpu.VMEM((4, BACK_ROWS, width), bf16),
        pltpu.SemaphoreType.DMA((4,)),
        pltpu.SemaphoreType.DMA((2,)),
    ]
    for tail in tails:
        scratch += halving_scratch(dims, tail)
    return pl.pallas_call(
        functools.partial(back_kernel, dims),
        grid=(10,),
        in_specs=[
            pl.BlockSpec((None, width, patches), lambda t: (section_of(t), 0, 0)),
            pl.BlockSpec((width, width), lambda t: (0, weight_section(t))),
            whole((patches, width)),
            own,
            other,
            block,
            whole((1, width)),
            whole((2, width)),
        ],
        out_specs=[
            pl.BlockSpec(memory_space=pl.ANY),
            whole(wide + (4, width)),
        ]
        + [whole(shape) for shape in sums],
        out_shape=[
            jax.ShapeDtypeStruct((2, patches // 2, width), bf16),
            jax.ShapeDtypeStruct(wide + (4, width), f32),
        ]
        + [jax.ShapeDtypeStruct(shape, bf16) for shape in sums],
        scratch_shapes=scratch + [pltpu.VMEM(wide + (4, width), f32)] + doubling_scratch(dims),
        compiler_params=params_of(collective_id=2, has_side_effects=True),
        cost_estimate=cost(12 * patches * width * width, 40e6),
        name="back",
    )(projected_grad, qkv_weight, entry, latents, other_x, middle_grad, scale, gain_rows)


def pick(values, index):
    return lax.dynamic_index_in_dim(values, index, 0, keepdims=False)


def per_device_whole(
    latents,
    cotangent,
    labels,
    group_ids,
    group_logits,
    row_pos,
    col_pos,
    time_weight,
    class_table,
    ada_weight,
    ada_bias,
    qkv_weight,
    query_gain,
    key_gain,
    proj_weight,
    gateup_weight,
    down_weight,
):
    width = latents.shape[-1]
    bands = lax.axis_size("band")
    img_index = lax.axis_index("img")
    band_index = lax.axis_index("band")

    def from_other(values):
        return lax.ppermute(values, "band", [(0, 1), (1, 0)])

    other_x = from_other(pick(latents, 1 - band_index))
    other_c = from_other(pick(cotangent, 1 - band_index))
    places = jnp.stack([row_pos, col_pos], axis=1)
    places = jnp.concatenate([places, from_other(places)], axis=0)

    quarter = HD // 4
    frequency = jnp.exp(-math.log(10000.0) * jnp.arange(quarter, dtype=f32) / quarter)
    angles = frequency[:, None] * places.astype(f32).T[:, None, :]
    cosine, sine = jnp.cos(angles), jnp.sin(angles)
    cosine = jnp.concatenate([cosine[0], cosine[0], cosine[1], cosine[1]], axis=0)
    sine = jnp.concatenate([-sine[0], sine[0], -sine[1], sine[1]], axis=0)

    def condition_of(group_ids, labels):
        group_hot = (group_ids[:, None] == jnp.arange(GROUPS, dtype=jnp.int32)[None, :]).astype(f32)
        times = jax.nn.sigmoid(jnp.dot(group_hot, group_logits, precision=highest))
        features = time_features(times, FREQ // 2).astype(bf16)
        before = jnp.dot(features, time_weight, preferred_element_type=f32) + jnp.take(
            class_table, labels, axis=0
        ).astype(f32)
        return features, before, jax.nn.silu(before).astype(bf16)

    own_group = pick(group_ids, band_index)[None]
    own_label = pick(labels, band_index)[None]
    _, _, condition = condition_of(own_group, own_label)
    modulation = jnp.dot(condition, ada_weight, preferred_element_type=f32) + ada_bias
    modes = modulation.reshape(6, width)
    shift_one, scale_one = modes[0:1], modes[1:2]
    vectors = jnp.concatenate([modes[2:3], modes[4:5], modes[3:4], modes[5:6], modes[2:6]], axis=0)

    scaling = HD ** (-0.5)
    gains = jnp.stack([query_gain, key_gain])[:, :, None]
    scaled_gains = gains * jnp.array([scaling * LOG2E, 1.0], f32)[:, None, None]
    entry_one, heads, unit, factor = front(
        latents, other_x, scale_one, shift_one, qkv_weight, scaled_gains, cosine, sine
    )
    mixed, query = attend(heads)
    mixed = mixed.reshape(width, -1)
    attended, entry_two, fed_grad = middle_step(
        mixed, proj_weight, latents, other_x, cotangent, other_c, vectors
    )
    fed, entry_two_grad, grad_down, gateup_done, gateup_left, *carries = mlp(
        entry_two, fed_grad, gateup_weight, down_weight
    )
    codes = jnp.stack([own_label, own_group], axis=0).astype(f32)
    codes = jnp.pad(codes, ((0, 2), (0, 127)))
    (
        result, middle_grad, projected_grad, gain_terms,
        sum_down, gateup_last, gateup_carried, sum_proj, modes_early,
    ) = core_step(
        fed, entry_two_grad, latents, other_x, cotangent, other_c, attended, mixed, proj_weight,
        vectors, codes, query, heads, unit, factor, gains, cosine, sine, grad_down, gateup_left,
        carries,
    )
    gain_rows = jnp.pad(jnp.sum(gain_terms, axis=2), ((0, 0), (0, width - HD)))
    grad_latents, modes_late, qkv_pair, qkv_single = back_step(
        projected_grad.reshape(3, width, -1), qkv_weight, entry_one, latents, other_x, middle_grad,
        scale_one, gain_rows,
    )
    modes_early = modes_early.reshape(-1, 4, modes_early.shape[-1])
    modes_late = modes_late.reshape(-1, 4, width)
    modulation_all = jnp.concatenate(
        [modes_late[:, 0], modes_late[:, 1]] + [modes_early[:, place, :width] for place in range(4)],
        axis=1,
    ).astype(bf16)
    gain_sums = jnp.sum(modes_late[:, 2:, :HD], axis=0)
    sum_query_gain, sum_key_gain = gain_sums[0], gain_sums[1]
    codes = modes_early[:, :2, width].astype(jnp.int32).T
    features_all, before_all, condition_all = condition_of(codes[1], codes[0])
    before_grad = lax.dot_general(
        modulation_all, ada_weight, (((1,), (1,)), ((), ())), preferred_element_type=f32
    ) * silu_slope(before_all)
    ada_rows = width // lax.axis_size("img")
    ada_cols = 6 * width // bands
    time_rows = FREQ // lax.axis_size("img")
    time_cols = width // bands
    condition_part = lax.dynamic_slice_in_dim(condition_all, img_index * ada_rows, ada_rows, 1)
    modulation_part = lax.dynamic_slice_in_dim(modulation_all, band_index * ada_cols, ada_cols, 1)
    sum_ada = jnp.dot(condition_part.T, modulation_part, preferred_element_type=f32)
    features_part = lax.dynamic_slice_in_dim(features_all, img_index * time_rows, time_rows, 1)
    before_part = lax.dynamic_slice_in_dim(before_grad, band_index * time_cols, time_cols, 1)
    sum_time = jnp.dot(features_part.astype(f32).T, before_part, precision=highest)
    class_all = (codes[0][:, None] == jnp.arange(NCLASS, dtype=jnp.int32)[None, :]).astype(f32)
    sum_class = jnp.dot(class_all.T, before_grad, precision=highest)
    sum_bias = jnp.sum(modulation_all.astype(f32), axis=0)

    sum_down = sum_down.reshape(-1, sum_down.shape[-1]).astype(f32)
    sum_proj = sum_proj.astype(f32)
    gateup_carried = gateup_carried.reshape((len(CARRIED), 2) + gateup_carried.shape[1:])
    gateup = jnp.concatenate([gateup_done, gateup_carried, gateup_last[None]], axis=0)
    sum_gateup = jnp.transpose(gateup, (2, 0, 1, 3)).reshape(gateup.shape[2], -1).astype(f32)
    sum_qkv = jnp.where(
        band_index == 0,
        jnp.concatenate([qkv_pair, qkv_single], axis=1),
        jnp.concatenate([qkv_single, qkv_pair], axis=1),
    ).astype(f32)
    return (
        result,
        grad_latents,
        sum_time,
        sum_class,
        sum_ada,
        sum_bias,
        sum_qkv,
        sum_query_gain,
        sum_key_gain,
        sum_proj,
        sum_gateup,
        sum_down,
    )


def per_device(latents, *others):
    if latents.shape[0] == lax.axis_size("band") == 2 and lax.axis_size("img") == 16:
        return per_device_whole(latents, *others)
    return per_device_banded(latents, *others)


def solution(mesh):
    return jax.shard_map(
        per_device,
        mesh=mesh,
        in_specs=(
            P("img", "band", None),
            P("img", "band", None),
            P("img"),
            P("img"),
            P(),
            P("band"),
            P("band"),
            P(),
            P(),
            P(),
            P(),
            P(),
            P(),
            P(),
            P(),
            P(),
            P(),
        ),
        out_specs=(
            P("img", "band", None),
            P("img", "band", None),
            P("img", "band"),
            P(),
            P("img", "band"),
            P(),
            P("img", "band"),
            P(),
            P(),
            P("img", "band"),
            P("img", "band"),
            P("img", "band"),
        ),
        check_vma=False,
    )
```

```python
import functools
import math

import jax
import jax.numpy as jnp
from jax import lax
from jax.experimental import pallas as pl
from jax.experimental.pallas import tpu as pltpu
from jax.sharding import PartitionSpec as P

HEADS = 16
HD = 72
FF = 3072
NCLASS = 1000
FREQ = 256
GROUPS = 8


highest = lax.Precision.HIGHEST
epsilon = 1e-06


def unit_rms(values):
    return values * lax.rsqrt(jnp.mean(values * values, axis=-1, keepdims=True) + epsilon)


def unit_rms_back(values, grads):
    factor = lax.rsqrt(jnp.mean(values * values, axis=-1, keepdims=True) + epsilon)
    normed = values * factor
    return factor * (grads - normed * jnp.mean(grads * normed, axis=-1, keepdims=True))


def rope_tables(row_pos, col_pos, quarter):
    frequency = jnp.exp(-math.log(10000.0) * jnp.arange(quarter, dtype=jnp.float32) / quarter)
    row_angle = row_pos.astype(jnp.float32)[:, None] * frequency[None, :]
    col_angle = col_pos.astype(jnp.float32)[:, None] * frequency[None, :]
    cosine = jnp.concatenate(
        [jnp.cos(row_angle), jnp.cos(row_angle), jnp.cos(col_angle), jnp.cos(col_angle)], axis=-1
    )
    sine = jnp.concatenate(
        [-jnp.sin(row_angle), jnp.sin(row_angle), -jnp.sin(col_angle), jnp.sin(col_angle)], axis=-1
    )
    return (cosine, sine)


def partner(values, quarter):
    return jnp.concatenate(
        [
            values[..., quarter : 2 * quarter],
            values[..., :quarter],
            values[..., 3 * quarter :],
            values[..., 2 * quarter : 3 * quarter],
        ],
        axis=-1,
    )


def time_features(times, half):
    frequency = jnp.exp(-math.log(10000.0) * jnp.arange(half, dtype=jnp.float32) / half)
    angles = 1000.0 * times[:, None] * frequency[None, :]
    return jnp.concatenate([jnp.cos(angles), jnp.sin(angles)], axis=-1)


def silu_slope(values):
    sigma = jax.nn.sigmoid(values)
    return sigma * (1.0 + values * (1.0 - sigma))


def per_device_banded(
    latents,
    cotangent,
    labels,
    group_ids,
    group_logits,
    row_pos,
    col_pos,
    time_weight,
    class_table,
    ada_weight,
    ada_bias,
    qkv_weight,
    query_gain,
    key_gain,
    proj_weight,
    gateup_weight,
    down_weight,
):
    images, rows, width = latents.shape
    quarter = HD // 4
    scaling = HD ** (-0.5)
    group_hot = (group_ids[:, None] == jnp.arange(GROUPS, dtype=jnp.int32)[None, :]).astype(
        jnp.float32
    )
    times = jax.nn.sigmoid(jnp.dot(group_hot, group_logits, precision=highest))
    features = time_features(times, FREQ // 2).astype(jnp.bfloat16)
    class_hot = (labels[:, None] == jnp.arange(NCLASS, dtype=jnp.int32)[None, :]).astype(
        jnp.bfloat16
    )
    before = jnp.dot(features, time_weight, preferred_element_type=jnp.float32) + jnp.dot(
        class_hot, class_table, preferred_element_type=jnp.float32
    )
    condition = jax.nn.silu(before).astype(jnp.bfloat16)
    modulation = jnp.dot(condition, ada_weight, preferred_element_type=jnp.float32) + ada_bias
    pieces = [modulation[:, None, member * width : (member + 1) * width] for member in range(6)]
    shift_one, scale_one, gate_one, shift_two, scale_two, gate_two = pieces
    cosine, sine = rope_tables(row_pos, col_pos, quarter)
    cosine = cosine[None, :, None, :]
    sine = sine[None, :, None, :]

    def turned(values):
        return values * cosine + partner(values, quarter) * sine

    def turned_back(grads):
        return grads * cosine + partner(grads * sine, quarter)

    source = latents.astype(jnp.float32)
    normed_one = unit_rms(source)
    entry_one = (normed_one * (1.0 + scale_one) + shift_one).astype(jnp.bfloat16)
    projected = jnp.einsum("bpd,de->bpe", entry_one, qkv_weight, preferred_element_type=jnp.float32)
    shape = (images, rows, HEADS, HD)
    query_raw = projected[..., :width].reshape(shape)
    key_raw = projected[..., width : 2 * width].reshape(shape)
    value_bf = projected[..., 2 * width :].reshape(shape).astype(jnp.bfloat16)
    query_unit = unit_rms(query_raw)
    key_unit = unit_rms(key_raw)
    query_bf = turned(query_unit * query_gain).astype(jnp.bfloat16)
    key_bf = turned(key_unit * key_gain).astype(jnp.bfloat16)
    peak = jnp.full((images, HEADS, rows), -1e30, jnp.float32)
    key_piece = lax.all_gather(key_bf, "band", axis=1, tiled=True)
    value_piece = lax.all_gather(value_bf, "band", axis=1, tiled=True)
    scores = (
        jnp.einsum("bqhd,bkhd->bhqk", query_bf, key_piece, preferred_element_type=jnp.float32)
        * scaling
    )
    new_peak = jnp.maximum(peak, jnp.max(scores, axis=-1))
    weights = jnp.exp(scores - new_peak[..., None])
    total = jnp.sum(weights, axis=-1)
    update = jnp.einsum(
        "bhqk,bkhd->bqhd",
        weights.astype(jnp.bfloat16),
        value_piece,
        preferred_element_type=jnp.float32,
    )
    accum = update
    peak, total, accum = (new_peak, total, accum)
    mixed = accum / jnp.transpose(total, (0, 2, 1))[..., None]
    log_total = peak + jnp.log(total)
    mixed_bf = mixed.reshape(images, rows, width).astype(jnp.bfloat16)
    attended = jnp.einsum("bpd,de->bpe", mixed_bf, proj_weight, preferred_element_type=jnp.float32)
    middle = source + gate_one * attended
    normed_two = unit_rms(middle)
    entry_two = (normed_two * (1.0 + scale_two) + shift_two).astype(jnp.bfloat16)
    gate_up = jnp.einsum(
        "bpd,de->bpe", entry_two, gateup_weight, preferred_element_type=jnp.float32
    )
    gate_part = gate_up[..., :FF]
    up_part = gate_up[..., FF:]
    hidden = (jax.nn.silu(gate_part) * up_part).astype(jnp.bfloat16)
    fed = jnp.einsum("bpf,fd->bpd", hidden, down_weight, preferred_element_type=jnp.float32)
    result = (middle + gate_two * fed).astype(jnp.bfloat16)
    upstream = cotangent.astype(jnp.float32)
    fed_grad = (upstream * gate_two).astype(jnp.bfloat16)
    grad_gate_two = jnp.sum(upstream * fed, axis=1)
    grad_down = jnp.einsum("bpf,bpd->fd", hidden, fed_grad, preferred_element_type=jnp.float32)
    hidden_grad = jnp.einsum(
        "bpd,fd->bpf", fed_grad, down_weight, preferred_element_type=jnp.float32
    )
    gate_grad = hidden_grad * up_part * silu_slope(gate_part)
    up_grad = hidden_grad * jax.nn.silu(gate_part)
    gate_up_grad = jnp.concatenate([gate_grad, up_grad], axis=-1).astype(jnp.bfloat16)
    grad_gateup = jnp.einsum(
        "bpd,bpe->de", entry_two, gate_up_grad, preferred_element_type=jnp.float32
    )
    entry_two_grad = jnp.einsum(
        "bpe,de->bpd", gate_up_grad, gateup_weight, preferred_element_type=jnp.float32
    )
    grad_scale_two = jnp.sum(entry_two_grad * normed_two, axis=1)
    grad_shift_two = jnp.sum(entry_two_grad, axis=1)
    middle_grad = upstream + unit_rms_back(middle, entry_two_grad * (1.0 + scale_two))
    grad_gate_one = jnp.sum(middle_grad * attended, axis=1)
    attended_grad = (middle_grad * gate_one).astype(jnp.bfloat16)
    grad_proj = jnp.einsum(
        "bpd,bpe->de", mixed_bf, attended_grad, preferred_element_type=jnp.float32
    )
    mixed_grad = jnp.einsum(
        "bpe,de->bpd", attended_grad, proj_weight, preferred_element_type=jnp.float32
    )
    mixed_grad_bf = mixed_grad.reshape(shape).astype(jnp.bfloat16)
    offsets = jnp.transpose(jnp.sum(mixed_grad_bf.astype(jnp.float32) * mixed, axis=-1), (0, 2, 1))
    key_piece = lax.all_gather(key_bf, "band", axis=1, tiled=True)
    value_piece = lax.all_gather(value_bf, "band", axis=1, tiled=True)
    scores = (
        jnp.einsum("bqhd,bkhd->bhqk", query_bf, key_piece, preferred_element_type=jnp.float32)
        * scaling
    )
    probs = jnp.exp(scores - log_total[..., None])
    prob_grad = jnp.einsum(
        "bqhd,bkhd->bhqk", mixed_grad_bf, value_piece, preferred_element_type=jnp.float32
    )
    score_grad = (probs * (prob_grad - offsets[..., None])).astype(jnp.bfloat16)
    query_grad = (
        jnp.einsum("bhqk,bkhd->bqhd", score_grad, key_piece, preferred_element_type=jnp.float32)
        * scaling
    )
    key_term = (
        jnp.einsum("bhqk,bqhd->bkhd", score_grad, query_bf, preferred_element_type=jnp.float32)
        * scaling
    )
    value_term = jnp.einsum(
        "bhqk,bqhd->bkhd",
        probs.astype(jnp.bfloat16),
        mixed_grad_bf,
        preferred_element_type=jnp.float32,
    )
    key_grads = key_term
    value_grads = value_term
    query_grad, key_grads, value_grads = (query_grad, key_grads, value_grads)
    key_local, value_local = (
        lax.psum_scatter(
            key_grads.astype(jnp.bfloat16), "band", scatter_dimension=1, tiled=True
        ).astype(jnp.float32),
        lax.psum_scatter(
            value_grads.astype(jnp.bfloat16), "band", scatter_dimension=1, tiled=True
        ).astype(jnp.float32),
    )
    query_turned = turned_back(query_grad)
    key_turned = turned_back(key_local)
    local_query_gain = jnp.sum(query_turned * query_unit, axis=(0, 1, 2))
    local_key_gain = jnp.sum(key_turned * key_unit, axis=(0, 1, 2))
    query_raw_grad = unit_rms_back(query_raw, query_turned * query_gain)
    key_raw_grad = unit_rms_back(key_raw, key_turned * key_gain)
    flat = (images, rows, width)
    projected_grad = jnp.concatenate(
        [query_raw_grad.reshape(flat), key_raw_grad.reshape(flat), value_local.reshape(flat)],
        axis=-1,
    ).astype(jnp.bfloat16)
    grad_qkv = jnp.einsum(
        "bpd,bpe->de", entry_one, projected_grad, preferred_element_type=jnp.float32
    )
    entry_one_grad = jnp.einsum(
        "bpe,de->bpd", projected_grad, qkv_weight, preferred_element_type=jnp.float32
    )
    grad_scale_one = jnp.sum(entry_one_grad * normed_one, axis=1)
    grad_shift_one = jnp.sum(entry_one_grad, axis=1)
    source_grad = middle_grad + unit_rms_back(source, entry_one_grad * (1.0 + scale_one))
    grad_latents = source_grad.astype(jnp.bfloat16)
    band_partial = jnp.concatenate(
        [
            grad_shift_one,
            grad_scale_one,
            grad_gate_one,
            grad_shift_two,
            grad_scale_two,
            grad_gate_two,
        ],
        axis=-1,
    )
    modulation_grad, band_query_gain, band_key_gain = (
        lax.psum(band_partial.astype(jnp.bfloat16), "band").astype(jnp.float32),
        lax.psum(local_query_gain[None, :].astype(jnp.bfloat16), "band").astype(jnp.float32),
        lax.psum(local_key_gain[None, :].astype(jnp.bfloat16), "band").astype(jnp.float32),
    )
    condition_grad = jnp.dot(modulation_grad, ada_weight.astype(jnp.float32).T, precision=highest)
    before_grad = condition_grad * silu_slope(before)
    condition_all, features_all, modulation_all, before_all, query_gain_rows, key_gain_rows = (
        lax.all_gather(
            condition.astype(jnp.float32).astype(jnp.bfloat16), "img", axis=0, tiled=True
        ).astype(jnp.float32),
        lax.all_gather(
            features.astype(jnp.float32).astype(jnp.bfloat16), "img", axis=0, tiled=True
        ).astype(jnp.float32),
        lax.all_gather(modulation_grad.astype(jnp.bfloat16), "img", axis=0, tiled=True).astype(
            modulation_grad.dtype
        ),
        lax.all_gather(before_grad.astype(jnp.bfloat16), "img", axis=0, tiled=True).astype(
            before_grad.dtype
        ),
        lax.all_gather(band_query_gain.astype(jnp.bfloat16), "img", axis=0, tiled=True).astype(
            band_query_gain.dtype
        ),
        lax.all_gather(band_key_gain.astype(jnp.bfloat16), "img", axis=0, tiled=True).astype(
            band_key_gain.dtype
        ),
    )
    labels_all = lax.all_gather(labels, "img", axis=0, tiled=True)
    img_index = lax.axis_index("img")
    band_index = lax.axis_index("band")
    ada_rows = width // lax.axis_size("img")
    ada_cols = 6 * width // lax.axis_size("band")
    time_rows = FREQ // lax.axis_size("img")
    time_cols = width // lax.axis_size("band")
    condition_part = lax.dynamic_slice_in_dim(condition_all, img_index * ada_rows, ada_rows, 1)
    modulation_part = lax.dynamic_slice_in_dim(modulation_all, band_index * ada_cols, ada_cols, 1)
    sum_ada = jnp.dot(condition_part.T, modulation_part, precision=highest)
    features_part = lax.dynamic_slice_in_dim(features_all, img_index * time_rows, time_rows, 1)
    before_part = lax.dynamic_slice_in_dim(before_all, band_index * time_cols, time_cols, 1)
    sum_time = jnp.dot(features_part.T, before_part, precision=highest)
    class_all = (labels_all[:, None] == jnp.arange(NCLASS, dtype=jnp.int32)[None, :]).astype(
        jnp.float32
    )
    sum_class = jnp.dot(class_all.T, before_all, precision=highest)
    sum_bias = jnp.sum(modulation_all, axis=0)
    sum_query_gain = jnp.sum(query_gain_rows, axis=0)
    sum_key_gain = jnp.sum(key_gain_rows, axis=0)
    part_qkv, part_proj, part_gateup, part_down = (
        lax.psum_scatter(
            grad_qkv.astype(jnp.bfloat16), "img", scatter_dimension=0, tiled=True
        ).astype(jnp.float32),
        lax.psum_scatter(
            grad_proj.astype(jnp.bfloat16), "img", scatter_dimension=0, tiled=True
        ).astype(jnp.float32),
        lax.psum_scatter(
            grad_gateup.astype(jnp.bfloat16), "img", scatter_dimension=0, tiled=True
        ).astype(jnp.float32),
        lax.psum_scatter(
            grad_down.astype(jnp.bfloat16), "img", scatter_dimension=0, tiled=True
        ).astype(jnp.float32),
    )
    sum_qkv, sum_proj, sum_gateup, sum_down = (
        lax.psum_scatter(
            part_qkv.astype(jnp.bfloat16), "band", scatter_dimension=1, tiled=True
        ).astype(jnp.float32),
        lax.psum_scatter(
            part_proj.astype(jnp.bfloat16), "band", scatter_dimension=1, tiled=True
        ).astype(jnp.float32),
        lax.psum_scatter(
            part_gateup.astype(jnp.bfloat16), "band", scatter_dimension=1, tiled=True
        ).astype(jnp.float32),
        lax.psum_scatter(
            part_down.astype(jnp.bfloat16), "band", scatter_dimension=1, tiled=True
        ).astype(jnp.float32),
    )
    return (
        result,
        grad_latents,
        sum_time,
        sum_class,
        sum_ada,
        sum_bias,
        sum_qkv,
        sum_query_gain,
        sum_key_gain,
        sum_proj,
        sum_gateup,
        sum_down,
    )


HDP = 80
LOG2E = math.log2(math.e)
VMEM_MAX = 62 * 2**20
bf16 = jnp.bfloat16
f32 = jnp.float32


def dot(left, right, left_dim, right_dim):
    return lax.dot_general(
        left, right, (((left_dim,), (right_dim,)), ((), ())), preferred_element_type=f32
    )


def params_of(**extra):
    return pltpu.CompilerParams(vmem_limit_bytes=VMEM_MAX, **extra)


def whole(shape):
    return pl.BlockSpec(shape, lambda *_: (0,) * len(shape), pipeline_mode=pl.Buffered(1))


def cost(flops, bytes_accessed, transcendentals=0):
    return pl.CostEstimate(
        flops=int(flops), bytes_accessed=int(bytes_accessed), transcendentals=int(transcendentals)
    )


def partner_rows(values, low_half):
    quarter = HD // 4
    return jnp.where(
        low_half, pltpu.roll(values, HD - quarter, 0), pltpu.roll(values, quarter, 0)
    )


def low_half_mask(patches):
    row = lax.broadcasted_iota(jnp.int32, (HD, patches), 0)
    quarter = HD // 4
    return (row < quarter) | ((row >= 2 * quarter) & (row < 3 * quarter))


def tail_rows(first, second, patches):
    row = lax.broadcasted_iota(jnp.int32, (HDP - HD, patches), 0)
    return jnp.where(row == 0, first, jnp.where(row == 1, second, 0.0))


def split_two(values):
    high = values.astype(bf16).astype(f32)
    return high, values - high


MESH_ID = pl.DeviceIdType.MESH


def pair_axes():
    bits = lax.axis_size("img").bit_length() - 1
    return ["y"] + [f"b{bit}" for bit in reversed(range(bits))]


def own_places():
    img = lax.axis_index("img")
    places = {"y": lax.axis_index("band")}
    for bit in range(lax.axis_size("img").bit_length() - 1):
        places[f"b{bit}"] = lax.rem(lax.div(img, 2**bit), 2)
    return places


def partner_id(axis, places):
    if axis == "y":
        return {"band": 1 - places["y"]}
    bit = int(axis[1:])
    return {"img": lax.axis_index("img") + (1 - 2 * places[axis]) * 2**bit}


def greet(places):
    barrier = pltpu.get_barrier_semaphore()
    for axis in places:
        pl.semaphore_signal(
            barrier, inc=1, device_id=partner_id(axis, places), device_id_type=MESH_ID
        )
    pl.semaphore_wait(barrier, len(places))


def dispatch(value, cases):
    if not cases:
        return
    keys = sorted(cases)
    if len(keys) == 1:
        pl.when(value == keys[0])(cases[keys[0]])
        return
    middle = keys[len(keys) // 2]
    low = {key: cases[key] for key in keys if key < middle}
    high = {key: cases[key] for key in keys if key >= middle}
    pl.when(value < middle)(functools.partial(dispatch, value, low))
    pl.when(value >= middle)(functools.partial(dispatch, value, high))


class Halving:
    def __init__(self, places, dims, order, held, arrived, send, receive, lead=(), tail=()):
        self.places, self.dims, self.order = places, list(dims), list(order)
        self.held, self.arrived, self.send, self.receive = held, arrived, send, receive
        self.lead, self.tail = tuple(lead), tuple(tail)

    def source_index(self, mine):
        first = self.order[0]
        place = self.places[first] if mine else 1 - self.places[first]
        return [place if name == first else slice(None) for name in self.dims]

    def held_index(self, step, mine):
        picked = []
        for name in self.dims:
            place = self.order.index(name)
            if place == 0:
                continue
            if place < step:
                picked.append(self.places[name])
            elif place == step:
                picked.append(self.places[name] if mine else 1 - self.places[name])
            else:
                picked.append(slice(None))
        return picked

    def settled(self, step):
        picked = []
        for name in self.dims:
            place = self.order.index(name)
            if place > 0:
                picked.append(self.places[name] if place < step else slice(None))
        return self.lead + tuple(picked)

    def copy(self, step, source=None):
        if step == 0:
            block = source.at[tuple(self.source_index(False)) + self.tail]
        else:
            block = self.held.at[self.lead + tuple(self.held_index(step, False))]
        arrived = self.arrived[step]
        return pltpu.make_async_remote_copy(
            src_ref=block,
            dst_ref=arrived.at[self.lead] if self.lead else arrived,
            send_sem=self.send.at[self.lead + (step,)],
            recv_sem=self.receive.at[self.lead + (step,)],
            device_id=partner_id(self.order[step], self.places),
            device_id_type=MESH_ID,
        )

    def own_half(self, source, semaphore):
        return pltpu.make_async_copy(
            source.at[tuple(self.source_index(True)) + self.tail],
            self.held.at[self.lead] if self.lead else self.held,
            semaphore,
        )

    def add(self, step, source=None, put=None):
        picked = self.held_index(step, True)
        spot = self.lead + tuple(picked)
        if source is None:
            old = self.held[spot + (...,)]
        else:
            old = source[tuple(self.source_index(True)) + self.tail + (...,)]
        new = self.arrived[step][self.lead + (...,)]
        if step == len(self.order) - 1:
            put(old.astype(f32) + new.astype(f32))
        else:
            self.held[spot + (...,)] = old + new


class Doubling:
    def __init__(self, places, dims, order, blocks, send, receive):
        self.places, self.dims, self.order = places, list(dims), list(order)
        self.blocks, self.send, self.receive = blocks, send, receive

    def own(self):
        return tuple(self.places[name] for name in self.dims)

    def events(self, point, points):
        for step in range(-1, len(self.order)):
            if points[step + 1] == point:
                if step >= 0:
                    self.copy(step).wait()
                if step + 1 < len(self.order):
                    self.copy(step + 1).start()

    def copy(self, step):
        known = self.order[:step]
        spot = tuple(slice(None) if n in known else self.places[n] for n in self.dims)
        return pltpu.make_async_remote_copy(
            src_ref=self.blocks.at[spot],
            dst_ref=self.blocks.at[spot],
            send_sem=self.send.at[step],
            recv_sem=self.receive.at[step],
            device_id=partner_id(self.order[step], self.places),
            device_id_type=MESH_ID,
        )


def doubling_scratch(dims):
    return [pltpu.SemaphoreType.DMA((len(dims),))] * 2


def halving_scratch(dims, tail, lead=()):
    left = len(dims) - 1
    shapes = [lead + (2,) * left + tail]
    shapes += [lead + (2,) * (left - step) + tail for step in range(len(dims))]
    semaphores = pltpu.SemaphoreType.DMA(lead + (len(dims),))
    return [pltpu.VMEM(shape, bf16) for shape in shapes] + [semaphores, semaphores]


def order_of(dims, *first):
    rest = [name for name in reversed(dims) if name not in first]
    return list(first) + rest


def modes_of(modulation_ref, *members):
    width = modulation_ref.shape[1] // 6
    names = ("shift_one", "scale_one", "gate_one", "shift_two", "scale_two", "gate_two")
    places = [names.index(member) * width for member in members]
    return [modulation_ref[:, place : place + width] for place in places]


def front_kernel(
    own_ref, other_ref, modulation_ref, w_ref, gains_ref, cos_ref, sin_ref,
    entry_ref, heads_ref, unit_ref, factor_ref,
):
    section = pl.program_id(0)
    patches = entry_ref.shape[0]
    half = patches // 2

    @pl.when(section == 0)
    def _():
        shift, scale = modes_of(modulation_ref, "shift_one", "scale_one")
        for number, ref in enumerate((own_ref, other_ref)):
            source = ref[...].astype(f32)
            normed = source * lax.rsqrt(jnp.mean(source * source, axis=1, keepdims=True) + epsilon)
            entry_ref[number * half : (number + 1) * half, :] = (
                normed * (1.0 + scale) + shift
            ).astype(bf16)

    raw = dot(w_ref[...], entry_ref[...], 0, 1)

    @pl.when(section < 2)
    def _():
        mask = low_half_mask(patches)
        extra = tail_rows(*[jnp.where(section == 1, 1.0, 0.0)] * 2, patches)
        gain = gains_ref[0]
        for head in range(HEADS):
            part = raw[head * HD : (head + 1) * HD, :]
            factor = lax.rsqrt(jnp.mean(part * part, axis=0, keepdims=True) + epsilon)
            unit = part * factor
            scaled = unit * gain
            turned = scaled * cos_ref[...] + partner_rows(scaled, mask) * sin_ref[...]
            heads_ref[0, head] = jnp.concatenate([turned, extra], axis=0).astype(bf16)
            unit_ref[0, head] = unit.astype(bf16)
            factor_ref[0, head] = factor

    @pl.when(section == 2)
    def _():
        extra = tail_rows(1.0, 1.0, patches)
        for head in range(HEADS):
            part = raw[head * HD : (head + 1) * HD, :]
            heads_ref[0, head] = jnp.concatenate([part, extra], axis=0).astype(bf16)


def own_image(rows, width, block):
    return pl.BlockSpec((None, rows, width), lambda t: (lax.axis_index("band"), block(t), 0))


def front(images, other, modulation, qkv_weight, gains, cosine, sine):
    half, width = other.shape
    patches = 2 * half
    last = lambda s: jnp.minimum(s, 1)
    return pl.pallas_call(
        front_kernel,
        grid=(3,),
        in_specs=[
            own_image(half, width, lambda s: 0),
            whole((half, width)),
            whole(modulation.shape),
            pl.BlockSpec((width, width), lambda s: (0, s)),
            pl.BlockSpec((1, HD, 1), lambda s: (last(s), 0, 0)),
            whole((HD, patches)),
            whole((HD, patches)),
        ],
        out_specs=[
            pl.BlockSpec((patches, width), lambda s: (0, 0)),
            pl.BlockSpec((1, HEADS, HDP, patches), lambda s: (s, 0, 0, 0)),
            pl.BlockSpec((1, HEADS, HD, patches), lambda s: (last(s), 0, 0, 0)),
            pl.BlockSpec((1, HEADS, 1, patches), lambda s: (last(s), 0, 0, 0)),
        ],
        out_shape=[
            jax.ShapeDtypeStruct((patches, width), bf16),
            jax.ShapeDtypeStruct((3, HEADS, HDP, patches), bf16),
            jax.ShapeDtypeStruct((2, HEADS, HD, patches), bf16),
            jax.ShapeDtypeStruct((2, HEADS, 1, patches), f32),
        ],
        compiler_params=params_of(),
        cost_estimate=cost(6 * patches * width * width, 24e6),
        name="front",
    )(images, other, modulation, qkv_weight, gains, cosine, sine)


def attend_kernel(q_ref, k_ref, v_ref, mixed_ref, lse_ref, qext_ref):
    patches = q_ref.shape[-1]
    step = patches // 2
    key = k_ref[...]
    value = v_ref[...]
    for start in range(0, patches, step):
        columns = slice(start, start + step)
        scores = dot(key, q_ref[:, columns], 0, 0)
        weights = jnp.exp2(scores).astype(bf16)
        summed = dot(value, weights, 1, 0)
        total = summed[HD : HD + 1, :]
        mixed_ref[:, columns] = (summed[:HD, :] / total).astype(bf16)
        high, low = split_two(-jnp.log2(total))
        extra = jnp.concatenate([jnp.zeros((HD, step), f32), tail_rows(high, low, step)], axis=0)
        qext_ref[:, columns] = q_ref[:, columns] + extra.astype(bf16)


def attend(heads):
    patches = heads.shape[-1]
    section = lambda member: pl.BlockSpec(
        (None, None, HDP, patches), lambda h: (member, h, 0, 0)
    )
    return pl.pallas_call(
        lambda q, k, v, mixed, qext: attend_kernel(q, k, v, mixed, None, qext),
        grid=(HEADS,),
        in_specs=[section(0), section(1), section(2)],
        out_specs=[
            pl.BlockSpec((None, HD, patches), lambda h: (h, 0, 0)),
            pl.BlockSpec((None, HDP, patches), lambda h: (h, 0, 0)),
        ],
        out_shape=[
            jax.ShapeDtypeStruct((HEADS, HD, patches), bf16),
            jax.ShapeDtypeStruct((HEADS, HDP, patches), bf16),
        ],
        compiler_params=params_of(),
        cost_estimate=cost(8 * HEADS * patches * patches * HDP, 14e6, HEADS * patches * patches),
        name="attend",
    )(heads, heads, heads)


def middle_kernel(
    mixed_ref, w_ref, own_x_ref, other_x_ref, own_c_ref, other_c_ref, modulation_ref,
    attended_ref, entry_ref, fed_grad_ref,
):
    in_own = pl.program_id(0) < pl.num_programs(0) // 2
    x = jnp.where(in_own, own_x_ref[...].astype(f32), other_x_ref[...].astype(f32))
    c = jnp.where(in_own, own_c_ref[...].astype(f32), other_c_ref[...].astype(f32))
    attended = dot(mixed_ref[...], w_ref[...], 0, 0)
    attended_bf = attended.astype(bf16)
    attended_ref[...] = attended_bf
    gate_one, scale_two, shift_two, gate_two = modes_of(
        modulation_ref, "gate_one", "scale_two", "shift_two", "gate_two"
    )
    middle = x + gate_one * attended_bf.astype(f32)
    normed = middle * lax.rsqrt(jnp.mean(middle * middle, axis=1, keepdims=True) + epsilon)
    entry_ref[...] = (normed * (1.0 + scale_two) + shift_two).astype(bf16)
    fed_grad_ref[...] = (c * gate_two).astype(bf16)


def middle_step(mixed, proj_weight, latents, other_x, cotangent, other_c, modulation):
    half, width = other_x.shape
    patches = 2 * half
    rows = 256
    blocks = half // rows
    block = pl.BlockSpec((rows, width), lambda t: (t, 0))
    own = own_image(rows, width, lambda t: jnp.minimum(t, blocks - 1))
    other = pl.BlockSpec((rows, width), lambda t: (jnp.maximum(t - blocks, 0), 0))
    return pl.pallas_call(
        middle_kernel,
        grid=(patches // rows,),
        in_specs=[
            pl.BlockSpec((width, rows), lambda t: (0, t)),
            whole((width, width)),
            own,
            other,
            own,
            other,
            whole((1, 6 * width)),
        ],
        out_specs=[block] * 3,
        out_shape=[jax.ShapeDtypeStruct((patches, width), bf16)] * 3,
        compiler_params=params_of(),
        cost_estimate=cost(2 * patches * width * width, 17e6),
        name="middle",
    )(mixed, proj_weight, latents, other_x, cotangent, other_c, modulation)


MLP_TILE = 512
MLP_SUB = 256
HOSTED = 5
CARRIED = ((3, 4), (4, 2))


def mlp_kernel(
    dims, entry_ref, fed_grad_ref, wg_ref, wu_ref, wd_ref,
    fed_ref, entry_grad_ref, down_ref, done_ref, left_ref, *rest,
):
    carry_refs, rest = rest[: 2 * len(CARRIED)], rest[2 * len(CARRIED) :]
    hidden_ref, gate_grad_ref, up_grad_ref, source_ref, left_sem, held, *arrived, send, receive = rest
    tile = pl.program_id(0)
    places = own_places()
    orders = mlp_orders(dims)
    steps = len(dims)

    def streams(number):
        slot = lax.rem(number, 2)
        return [
            Halving(places, dims, orders[sub], held, arrived, send, receive, (slot, sub))
            for sub in range(2)
        ]

    def advance(number, step):
        @pl.when((number >= 0) & (number < HOSTED))
        def _():
            for sub, stream in enumerate(streams(number)):
                source = source_ref.at[sub]
                stream.copy(step, source).wait()

                def put(values):
                    done_ref[number, sub] = values.astype(bf16)

                stream.add(step, source if step == 0 else None, put)
                leaves = [place for place, (_, ended) in enumerate(CARRIED) if ended == step + 1]
                for place in leaves:

                    @pl.when(number == CARRIED[place][0])
                    def _():
                        carry_refs[2 * place + sub][...] = held[stream.settled(step + 1)]

                if step + 1 < steps:
                    goes_on = True
                    for place in leaves:
                        goes_on = goes_on & (number != CARRIED[place][0])
                    if leaves:
                        pl.when(goes_on)(stream.copy(step + 1).start)
                    else:
                        stream.copy(step + 1).start()

    @pl.when(tile == 0)
    def _():
        fed_ref[...] = jnp.zeros_like(fed_ref)
        entry_grad_ref[...] = jnp.zeros_like(entry_grad_ref)
        greet(places)

    entry = entry_ref[...]
    fed_grad = fed_grad_ref[...]
    gate = dot(entry, wg_ref[...], 1, 0)
    up = dot(entry, wu_ref[...], 1, 0)
    sigma = jax.nn.sigmoid(gate)
    silu = gate * sigma
    hidden_ref[...] = (silu * up).astype(bf16)
    hidden_grad = dot(fed_grad, wd_ref[...], 1, 1)
    gate_grad_ref[...] = (hidden_grad * up * (sigma * (1.0 + gate * (1.0 - sigma)))).astype(bf16)
    up_grad_ref[...] = (hidden_grad * silu).astype(bf16)
    advance(tile - 3, 4)
    advance(tile - 2, 2)
    advance(tile - 1, 0)
    fed_ref[...] += dot(hidden_ref[...], wd_ref[...], 1, 0)
    entry_grad_ref[...] += dot(gate_grad_ref[...], wg_ref[...], 1, 1) + dot(
        up_grad_ref[...], wu_ref[...], 1, 1
    )
    down = dot(hidden_ref[...], fed_grad, 0, 0).astype(bf16)
    column_half = down.shape[1] // 2
    down_ref[0] = down[:, :column_half]
    down_ref[1] = down[:, column_half:]
    grads = [dot(entry, ref[...], 0, 0) for ref in (gate_grad_ref, up_grad_ref)]
    blocks = 2 ** (steps - 1)
    rows = grads[0].shape[0] // blocks
    for half, grad in enumerate(grads):
        for block in range(blocks):
            spot = tuple(block // 2**bit % 2 for bit in reversed(range(steps - 1)))
            part = grad[block * rows : (block + 1) * rows, :].astype(bf16)
            for sub in range(2):
                source_ref[(sub, half) + spot] = part[:, sub * MLP_SUB : (sub + 1) * MLP_SUB]

    @pl.when(tile < HOSTED)
    def _():
        for sub, stream in enumerate(streams(tile)):
            stream.copy(0, source_ref.at[sub]).start()

    @pl.when(tile == HOSTED)
    def _():
        pltpu.make_async_copy(source_ref, left_ref, left_sem).start()

    advance(tile - 2, 3)
    advance(tile - 1, 1)

    @pl.when(tile == HOSTED)
    def _():
        pltpu.make_async_copy(source_ref, left_ref, left_sem).wait()


def mlp_orders(dims):
    return [order_of(dims, "b0", "y", "b2", "b1"), order_of(dims, "b0", "b1", "y", "b2")]


def carried_orders(dims):
    return [order[ended:] for _, ended in CARRIED for order in mlp_orders(dims)]


def carried_dims(dims):
    return [[name for name in dims if name in order] for order in carried_orders(dims)]


def mlp(entry, fed_grad, gateup_weight, down_weight):
    patches, width = entry.shape
    inner = down_weight.shape[0]
    tile = MLP_TILE
    tiles = inner // tile
    dims = pair_axes()
    rows = width // lax.axis_size("img")
    tail = (rows, MLP_SUB)
    carried = [(2,) * len(names) + tail for names in carried_dims(dims)]
    return pl.pallas_call(
        functools.partial(mlp_kernel, dims),
        grid=(tiles,),
        in_specs=[
            whole((patches, width)),
            whole((patches, width)),
            pl.BlockSpec((width, tile), lambda t: (0, t)),
            pl.BlockSpec((width, tile), lambda t: (0, tiles + t)),
            pl.BlockSpec((tile, width), lambda t: (t, 0)),
        ],
        out_specs=[
            whole((patches, width)),
            whole((patches, width)),
            pl.BlockSpec((2, tile, width // 2), lambda t: (0, t, 0)),
            whole((HOSTED - len(CARRIED), 2) + tail),
            pl.BlockSpec(memory_space=pl.ANY),
        ]
        + [whole(shape) for shape in carried],
        out_shape=[
            jax.ShapeDtypeStruct((patches, width), f32),
            jax.ShapeDtypeStruct((patches, width), f32),
            jax.ShapeDtypeStruct((2, inner, width // 2), bf16),
            jax.ShapeDtypeStruct((HOSTED - len(CARRIED), 2) + tail, bf16),
            jax.ShapeDtypeStruct((2,) + (2,) * len(dims) + tail, bf16),
        ]
        + [jax.ShapeDtypeStruct(shape, bf16) for shape in carried],
        scratch_shapes=[pltpu.VMEM((patches, tile), bf16)] * 3
        + [pltpu.VMEM((2,) + (2,) * len(dims) + tail, bf16), pltpu.SemaphoreType.DMA]
        + halving_scratch(dims, tail, (2, 2)),
        compiler_params=params_of(collective_id=0, has_side_effects=True),
        cost_estimate=cost(18 * patches * width * inner, 56e6),
        name="mlp",
    )(entry, fed_grad, gateup_weight, gateup_weight, down_weight)


ADA_COLUMNS = 384
ADA_PIECES = 3
ADA_EARLY = 4 * ADA_PIECES


def in_blocks(rows):
    return jnp.concatenate(
        [
            row[:, block * ADA_COLUMNS : (block + 1) * ADA_COLUMNS]
            for row in rows
            for block in range(ADA_PIECES)
        ],
        axis=0,
    )


TURN_ROWS = 128


def core_plan(dims):
    return [
        ("down", 0, order_of(dims, "b0", "y", "b1", "b2", "b3"), (2, 9, 25, 31, 35, 40)),
        ("down", 1, order_of(dims, "b0", "b2", "y", "b3", "b1"), (2, 9, 23, 27, 33, 35)),
        ("down", 2, order_of(dims, "b0", "b2", "b3", "b1", "y"), (0, 6, 21, 31, 35, 37)),
        ("down", 3, order_of(dims, "b0", "b1", "b2", "y", "b3"), (2, 9, 23, 31, 35, 40)),
        ("left", 0, order_of(dims, "b0", "b1", "y", "b2", "b3"), (1, 6, 11, 21, 25, 29)),
        ("left", 1, order_of(dims, "b0", "b2", "b1", "b3", "y"), (0, 3, 9, 15, 19, 21)),
        ("proj", 0, order_of(dims, "b0", "b1", "y", "b2", "b3"), (7, 11, 27, 33, 37, 44)),
        ("carry", 0, ["b3"], (0, 3)),
        ("carry", 1, ["b3"], (0, 3)),
        ("carry", 2, ["b2", "b1", "b3"], (0, 4, 6, 9)),
        ("carry", 3, ["y", "b2", "b3"], (0, 7, 11, 15)),
    ]


def core_gather():
    return ["b3", "b2", "y", "b1", "b0"], (7, 17, 23, 29, 35, 39)


def core_kernel(
    dims, fed_ref, entry_grad_ref, own_x_ref, other_x_ref, own_c_ref, other_c_ref, attended_ref,
    all_mixed_ref, w_ref, modulation_ref, codes_ref,
    q_ref, k_ref, v_ref, mixed_ref, unit_ref, factor_ref, gains_ref, cos_ref, sin_ref,
    down_ref, left_ref, *rest,
):
    carry_refs, rest = rest[: 2 * len(CARRIED)], rest[2 * len(CARRIED) :]
    (
        result_ref, middle_grad_ref, out_ref, gain_out_ref,
        down_out_ref, left_out_ref, carry_out_ref, proj_out_ref, modes_out_ref,
        attended_grad_ref, mixed_grad_ref, proj_ref, rows_ref, row_send, row_receive,
        mg_ext_ref, acc_ref, own_sem, modes_ref, doubling_send, doubling_receive, *buffers,
    ) = rest
    step = pl.program_id(0)
    places = own_places()
    patches = q_ref.shape[-1]
    turns = patches // TURN_ROWS
    axes = len(dims)
    carries = carried_dims(dims)
    groups, used = {}, 0
    kinds = [("down", axes), ("left", axes), ("proj", axes)]
    kinds += [(f"carry{part}", len(names)) for part, names in enumerate(carries)]
    for name, count in kinds:
        groups[name] = buffers[used : used + count + 3]
        used += count + 3

    def streams():
        for number, (name, part, order, points) in enumerate(core_plan(dims)):
            names, lead, tail = dims, (), ()
            if name == "down":
                lead = (part,)
                source = down_ref
                rows = source.shape[-2] // 4
                tail = (pl.ds(part * rows, rows), slice(None))
                out, spot = down_out_ref, (part,)
            elif name == "left":
                lead = (part,)
                source = left_ref.at[part]
                out, spot = left_out_ref, (part,)
            elif name == "proj":
                source, out, spot = proj_ref, proj_out_ref, ()
            else:
                names = carries[part]
                source = carry_refs[part]
                out, spot = carry_out_ref, (part,)
            held, *arrived, send, receive = groups[name if name in groups else f"{name}{part}"]
            stream = Halving(places, names, order, held, arrived, send, receive, lead, tail)
            yield number, name, stream, source, points, out, spot

    def events(point):
        doubling.events(point, gather_points)
        for number, name, stream, source, points, out, spot in streams():
            local = name in ("proj", "carry")
            steps = len(points) - 1
            for phase in range(-1, steps):
                if points[phase + 1] != point:
                    continue
                if phase >= 0:
                    stream.copy(phase, source).wait()
                    if phase == 0 and not local:
                        stream.own_half(source, own_sem.at[number]).wait()

                    def put(values):
                        out[spot + (...,)] = values.astype(bf16)

                    stream.add(phase, source if local and phase == 0 else None, put)
                if phase + 1 < steps:
                    stream.copy(phase + 1, source).start()
                    if phase < 0 and not local:
                        stream.own_half(source, own_sem.at[number]).start()

    band = places["y"]

    def away(number):
        return pltpu.make_async_remote_copy(
            src_ref=rows_ref.at[number],
            dst_ref=result_ref.at[band, pl.ds(number * TURN_ROWS, TURN_ROWS)],
            send_sem=row_send.at[number],
            recv_sem=row_receive.at[number],
            device_id=partner_id("y", places),
            device_id_type=MESH_ID,
        )

    def stay(number):
        return pltpu.make_async_copy(
            rows_ref.at[number + turns // 2],
            result_ref.at[band, pl.ds(number * TURN_ROWS, TURN_ROWS)],
            row_send.at[number + turns // 2],
        )

    @pl.when(step == 0)
    def _():
        greet(places)

    gather_order, gather_points = core_gather()
    doubling = Doubling(places, dims, gather_order, modes_ref, doubling_send, doubling_receive)
    width = w_ref.shape[0]
    half = width // 2
    pair = 2 * TURN_ROWS

    def turn(number):
        x_ref, c_ref = (own_x_ref, own_c_ref) if number >= turns // 2 else (other_x_ref, other_c_ref)
        gate_one, scale_two, gate_two = modes_of(modulation_ref, "gate_one", "scale_two", "gate_two")
        attended = attended_ref[...].astype(f32)
        upstream = c_ref[...].astype(f32)
        fed = fed_ref[...]
        middle = x_ref[...].astype(f32) + gate_one * attended
        rows_ref[number] = (middle + gate_two * fed).astype(bf16)
        factor = lax.rsqrt(jnp.mean(middle * middle, axis=1, keepdims=True) + epsilon)
        normed = middle * factor
        entry_grad = entry_grad_ref[...]
        inner = entry_grad * (1.0 + scale_two)
        middle_grad = upstream + factor * (
            inner - normed * jnp.mean(inner * normed, axis=1, keepdims=True)
        )
        middle_grad_ref[...] = middle_grad
        start = (number + turns // 2) % turns * TURN_ROWS
        attended_grad_ref[start : start + TURN_ROWS, :] = (middle_grad * gate_one).astype(bf16)
        add = lambda v: jnp.sum(v, axis=0, keepdims=True)
        sums = in_blocks(
            [
                add(middle_grad * attended),
                add(entry_grad),
                add(entry_grad * normed),
                add(upstream * fed),
            ]
        )
        if number == 0:
            modes_ref[doubling.own() + (slice(0, ADA_EARLY),)] = sums
            modes_ref[doubling.own() + (slice(ADA_EARLY, None),)] = codes_ref[...]
        else:
            modes_ref[doubling.own() + (slice(0, ADA_EARLY),)] += sums
        if number < turns // 2:
            away(number).start()
        else:
            stay(number - turns // 2).start()
        if number % 2 == 1:
            first = start - TURN_ROWS
            grads = dot(w_ref[...], attended_grad_ref[first : first + pair, :], 1, 1)
            for head in range(HEADS):
                mixed_grad_ref[head, :, first : first + pair] = grads[
                    head * HD : (head + 1) * HD, :
                ].astype(bf16)
        if number == turns - 1:
            blocks = 2 ** (axes - 1)
            rows = width // blocks
            grads = dot(all_mixed_ref[...], attended_grad_ref[...], 1, 0)
            for block in range(blocks):
                spot = tuple(block // 2**bit % 2 for bit in reversed(range(axes - 1)))
                part = grads[block * rows : (block + 1) * rows, :].astype(bf16)
                proj_ref[(0,) + spot] = part[:, :half]
                proj_ref[(1,) + spot] = part[:, half:]
        events(number)

    for number in range(turns):

        @pl.when(step == number)
        def _():
            turn(number)

    points = {point for plan in core_plan(dims) for point in plan[3]} | set(gather_points)

    class Events:
        @staticmethod
        def at_head(head, end):
            wanted = [now for now in range(HEADS) if turns + 2 * now + end in points]
            dispatch(
                head,
                {now: functools.partial(events, turns + 2 * now + end) for now in wanted},
            )

    @pl.when(step >= turns)
    def _():
        attend_back(
            step - turns, Events(), mixed_grad_ref,
            q_ref, k_ref, v_ref, mixed_ref, unit_ref, factor_ref, gains_ref, cos_ref, sin_ref,
            out_ref, gain_out_ref, mg_ext_ref, acc_ref,
        )

    @pl.when(step == pl.num_programs(0) - 1)
    def _():
        for point in sorted(points):
            if point >= turns + 2 * HEADS:
                events(point)
        modes_out_ref[...] = modes_ref[...]
        for number in range(turns // 2):
            away(number).wait()
            stay(number).wait()


def attend_back(
    head, events, mixed_grad_ref,
    q_ref, k_ref, v_ref, mixed_ref, unit_ref, factor_ref, gains_ref, cos_ref, sin_ref,
    out_ref, gain_out_ref, mg_ext_ref, acc_ref,
):
    patches = q_ref.shape[-1]
    step = patches // 2
    scaling = HD ** (-0.5)
    mixed_grad = mixed_grad_ref[head].astype(f32)
    offsets = jnp.sum(mixed_grad * mixed_ref[...].astype(f32), axis=0, keepdims=True)
    high, low = split_two(-offsets)
    mg_ext_ref[...] = jnp.concatenate(
        [mixed_grad, tail_rows(high, low, patches)], axis=0
    ).astype(bf16)
    key = k_ref[...]
    value = v_ref[...]
    for start in range(0, patches, step):
        columns = slice(start, start + step)
        query = q_ref[:, columns]
        grads = mg_ext_ref[:, columns]
        probs = jnp.exp2(dot(key, query, 0, 0))
        score_grad = (probs * dot(value, grads, 0, 0)).astype(bf16)
        probs_bf = probs.astype(bf16)
        acc_ref[0, :, columns] = dot(key, score_grad, 1, 0)
        key_term = dot(query, score_grad, 1, 1)
        value_term = dot(grads, probs_bf, 1, 1)
        if start == 0:
            acc_ref[1] = key_term
            acc_ref[2] = value_term
            events.at_head(head, 0)
        else:
            acc_ref[1] += key_term
            acc_ref[2] += value_term
    mask = low_half_mask(patches)
    for member, weight in ((0, scaling), (1, 1.0 / LOG2E)):
        grads = acc_ref[member, :HD, :] * weight
        turned = grads * cos_ref[...] + partner_rows(grads * sin_ref[...], mask)
        unit = unit_ref[member].astype(f32)
        product = turned * unit

        @pl.when(head == 0)
        def _():
            gain_out_ref[member] = product

        @pl.when(head > 0)
        def _():
            gain_out_ref[member] += product

        inner = turned * gains_ref[member]
        raw = factor_ref[member] * (inner - unit * jnp.mean(inner * unit, axis=0, keepdims=True))
        out_ref[member] = raw.astype(bf16)
    out_ref[2] = acc_ref[2, :HD, :].astype(bf16)
    events.at_head(head, 1)


def core_step(
    fed, entry_grad, latents, other_x, cotangent, other_c, attended, mixed, proj_weight, modulation,
    codes, query, heads, unit, factor, gains, cosine, sine, down, left, carries,
):
    half, width = other_x.shape
    patches = 2 * half
    dims = pair_axes()
    turns = patches // TURN_ROWS
    devices = lax.axis_size("img")
    split = (2,) * len(dims)
    down = down.reshape(split + (down.shape[1] // devices, down.shape[2]))
    down_tail = (down.shape[-2] // 4, down.shape[-1])
    left_tail = left.shape[-2:]
    proj_tail = (width // devices, width // 2)
    row_block = lambda t: lax.rem(jnp.minimum(t, turns - 1) + turns // 2, turns)
    block = pl.BlockSpec((TURN_ROWS, width), lambda t: (row_block(t), 0))
    own = own_image(TURN_ROWS, width, lambda t: jnp.clip(t - turns // 2, 0, turns // 2 - 1))
    other = pl.BlockSpec((TURN_ROWS, width), lambda t: (jnp.minimum(t, turns // 2 - 1), 0))
    head_of = lambda t: jnp.maximum(t - turns, 0)
    section = lambda member: pl.BlockSpec(
        (None, None, HDP, patches), lambda t: (member, head_of(t), 0, 0)
    )
    single = lambda rows: pl.BlockSpec((None, rows, patches), lambda t: (head_of(t), 0, 0))
    couple = lambda rows: pl.BlockSpec((2, None, rows, patches), lambda t: (0, head_of(t), 0, 0))
    anywhere = pl.BlockSpec(memory_space=pl.ANY)
    sums = [(4,) + down_tail, (2,) + left_tail, (len(carries),) + left_tail, proj_tail, ()]
    sums[-1] = split + (ADA_EARLY + codes.shape[0], ADA_COLUMNS)
    return pl.pallas_call(
        functools.partial(core_kernel, dims),
        grid=(turns + HEADS,),
        in_specs=[
            block,
            block,
            own,
            other,
            own,
            other,
            block,
            whole((width, patches)),
            whole((width, width)),
            whole((1, 6 * width)),
            whole(codes.shape),
            single(HDP),
            section(1),
            section(2),
            single(HD),
            couple(HD),
            couple(1),
            whole((2, HD, 1)),
            whole((HD, patches)),
            whole((HD, patches)),
            anywhere,
            anywhere,
        ]
        + [whole(carry.shape) for carry in carries],
        out_specs=[
            anywhere,
            block,
            pl.BlockSpec((3, None, HD, patches), lambda t: (0, head_of(t), 0, 0)),
            whole((2, HD, patches)),
        ]
        + [whole(shape) for shape in sums],
        out_shape=[
            jax.ShapeDtypeStruct((2, half, width), bf16),
            jax.ShapeDtypeStruct((patches, width), f32),
            jax.ShapeDtypeStruct((3, HEADS, HD, patches), bf16),
            jax.ShapeDtypeStruct((2, HD, patches), f32),
        ]
        + [jax.ShapeDtypeStruct(shape, bf16) for shape in sums[:-1]]
        + [jax.ShapeDtypeStruct(sums[-1], f32)],
        scratch_shapes=[
            pltpu.VMEM((patches, width), bf16),
            pltpu.VMEM((HEADS, HD, patches), bf16),
            pltpu.VMEM(split + proj_tail, bf16),
            pltpu.VMEM((turns, TURN_ROWS, width), bf16),
            pltpu.SemaphoreType.DMA((turns,)),
            pltpu.SemaphoreType.DMA((turns // 2,)),
            pltpu.VMEM((HDP, patches), bf16),
            pltpu.VMEM((3, HDP, patches), f32),
            pltpu.SemaphoreType.DMA((len(core_plan(dims)),)),
            pltpu.VMEM(sums[-1], f32),
        ]
        + doubling_scratch(dims)
        + halving_scratch(dims, down_tail, (4,))
        + halving_scratch(dims, left_tail, (2,))
        + halving_scratch(dims, proj_tail)
        + [ref for names in carried_dims(dims) for ref in halving_scratch(names, left_tail)],
        compiler_params=params_of(collective_id=1, has_side_effects=True),
        cost_estimate=cost(24 * HEADS * patches * patches * HDP, 70e6, HEADS * patches**2),
        name="core",
    )(
        fed, entry_grad, latents, other_x, cotangent, other_c, attended, mixed, proj_weight,
        modulation, codes, query, heads, heads, mixed.reshape(HEADS, HD, patches), unit, factor,
        gains, cosine, sine, down, left, *carries,
    )


BACK_ROWS = 256


def tail_plan(dims):
    return [
        ("pair", pl.ds(0, 384), order_of(dims, "b0", "b2", "b3", "b1", "y"), (1, 2, 5, 13, 25, 46)),
        ("pair", pl.ds(384, 384), order_of(dims, "b0", "y", "b2", "b1", "b3"), (1, 3, 7, 21, 40, 54)),
        ("pair", pl.ds(768, 384), order_of(dims, "b0", "b2", "b1", "b3", "y"), (1, 4, 15, 35, 49, 61)),
        ("single", None, order_of(dims, "b0", "b1", "b2", "y", "b3"), (2, 5, 20, 40, 54, 66)),
    ]


def tail_gather():
    return ["b3", "b2", "b1", "y", "b0"], (9, 14, 22, 42, 59, 64)


class Ada:
    def __init__(self, places, refs):
        (
            self.weight, self.early, self.table, self.time, self.classes_hbm,
            self.ada_out, self.bias_out, self.time_out, self.class_out, self.gain_out,
            self.classes, self.modes, self.codes, self.total, self.before, self.condition,
            self.features, self.parts, self.sem,
        ) = refs
        self.band = places["y"]

    def fetch(self):
        return pltpu.make_async_copy(self.classes_hbm, self.classes, self.sem.at[0])

    def prepare(self):
        images = self.early.shape[0]

        def one(image, _):
            row = pl.ds(image, 1)
            for block in range(ADA_EARLY):
                self.modes[2 * ADA_PIECES + block, row, :] = self.early[image, block : block + 1, :]
            for part in range(2):
                spot = ADA_EARLY + part
                self.codes[part, row, :] = self.early[image, spot : spot + 1, :128]
            return 0

        lax.fori_loop(0, images, one, 0)
        self.fetch().wait()
        label, group = self.codes[0][:, :1], self.codes[1][:, :1]
        place = lambda shape, axis: lax.broadcasted_iota(jnp.int32, shape, axis)
        group_hot = (group == place((images, GROUPS), 1).astype(f32)).astype(bf16)
        features = dot(group_hot, self.table[...], 1, 0).astype(bf16)
        before = dot(features, self.time[...], 1, 0) + dot(self.class_hot(label), self.classes[...], 1, 0)
        self.before[...] = before
        condition = (before * jax.nn.sigmoid(before)).astype(bf16)
        img = lax.axis_index("img")

        def own_rows(values, rows):
            shape = (rows, values.shape[1])
            picker = (place(shape, 1) == place(shape, 0) + img * rows).astype(bf16)
            return dot(picker, values, 1, 1).astype(bf16)

        self.condition[...] = own_rows(condition, self.condition.shape[0])
        self.features[...] = own_rows(features, self.features.shape[0])
        self.total[...] = jnp.zeros_like(self.total)

    def class_hot(self, label):
        shape = (label.shape[0], self.classes.shape[0])
        return (label == lax.broadcasted_iota(jnp.int32, shape, 1).astype(f32)).astype(bf16)

    def late(self, sums_ref, axes):
        late = 2 * ADA_PIECES

        def one(image, _):
            row = pl.ds(image, 1)
            spot = tuple(lax.rem(lax.div(image, 2**bit), 2) for bit in reversed(range(axes)))
            for block in range(late):
                self.modes[block, row, :] = sums_ref[spot + (slice(block, block + 1),)]
            self.gain_out[...] += sums_ref[spot + (slice(late, late + 1),)]
            return 0

        self.gain_out[...] = jnp.zeros_like(self.gain_out)
        lax.fori_loop(0, self.early.shape[0], one, 0)

    def block(self, number):
        modes = self.modes[number]
        self.bias_out[...] = jnp.sum(modes, axis=0, keepdims=True)
        modes_bf = modes.astype(bf16)
        self.total[...] += dot(modes_bf, self.weight[...], 1, 1)
        blocks = self.parts.shape[0]
        here = number - blocks * self.band

        @pl.when((here >= 0) & (here < blocks))
        def _():
            self.parts[here] = dot(self.condition[...], modes_bf, 1, 0)

    def finish(self, class_ref):
        before = self.before[...]
        sigma = jax.nn.sigmoid(before)
        before_grad = self.total[...] * (sigma * (1.0 + before * (1.0 - sigma)))
        pieces, left = [], before_grad
        for _ in range(3):
            pieces.append(left.astype(bf16))
            left = left - pieces[-1].astype(f32)
        half = before.shape[1] // 2
        times = sum(dot(self.features[...], piece, 1, 0) for piece in pieces)
        self.time_out[...] = jnp.where(self.band == 0, times[:, :half], times[:, half:])
        class_hot = self.class_hot(self.codes[0][:, :1])
        class_ref[...] = sum(dot(class_hot, piece, 0, 0) for piece in pieces)
        for block in range(self.parts.shape[0]):
            columns = slice(block * ADA_COLUMNS, (block + 1) * ADA_COLUMNS)
            self.ada_out[:, columns] = self.parts[block]


def back_kernel(
    dims, pg_ref, w_ref, entry_ref, own_x_ref, other_x_ref, middle_grad_ref, modulation_ref,
    gain_terms_ref, ada_ref, early_ref, table_ref, time_ref, classes_ref,
    latents_out_ref, pair_out_ref, single_out_ref, ada_out_ref, bias_out_ref, time_out_ref,
    class_out_ref, gain_out_ref,
    entry_grad_ref, pair_ref, single_ref, rows_ref, row_send, row_receive,
    classes_copy_ref, modes_ref, codes_ref, total_ref, before_ref, condition_ref, features_ref,
    parts_ref, ada_sem, *buffers,
):
    step = pl.program_id(0)
    places = own_places()
    phases = len(dims)
    size = phases + 3
    *buffers, sums_ref, send, receive = buffers
    streams = []
    for place, (name, columns, order, when) in enumerate(tail_plan(dims)):
        held, *arrived, s, r = buffers[place * size : (place + 1) * size]
        tail = () if columns is None else (slice(None), columns)
        stream = Halving(places, dims, order, held, arrived, s, r, (), tail)
        if name == "pair":
            streams.append((stream, pair_ref, when, pair_out_ref.at[:, columns]))
        else:
            streams.append((stream, single_ref, when, single_out_ref))
    gather_order, gather_points = tail_gather()
    doubling = Doubling(places, dims, gather_order, sums_ref, send, receive)
    ada = Ada(
        places,
        (
            ada_ref, early_ref, table_ref, time_ref, classes_ref,
            ada_out_ref, bias_out_ref, time_out_ref, class_out_ref, gain_out_ref,
            classes_copy_ref, modes_ref, codes_ref, total_ref, before_ref, condition_ref,
            features_ref, parts_ref, ada_sem,
        ),
    )
    width = entry_grad_ref.shape[0]
    patches = entry_ref.shape[0]
    half = width // 2
    blocks = 2 ** (phases - 1)
    rows = width // blocks

    @pl.when(step == 0)
    def _():
        entry_grad_ref[...] = jnp.zeros_like(entry_grad_ref)
        ada.fetch().start()
        greet(places)

    @pl.when(step < 3)
    def _():
        def spot(block):
            return tuple(block // 2**bit % 2 for bit in reversed(range(phases - 1)))

        @pl.when(step < 2)
        def _():
            grad = dot(entry_ref[...], pg_ref[...], 0, 1)
            for block in range(blocks):
                part = grad[block * rows : (block + 1) * rows, :]
                pair_ref[(step,) + spot(block)] = part.astype(bf16)

        @pl.when(step == 2)
        def _():
            grad = dot(entry_ref[...], pg_ref[...], 0, 1)
            for block in range(blocks):
                part = grad[block * rows : (block + 1) * rows, :].astype(bf16)
                single_ref[(0,) + spot(block)] = part[:, :half]
                single_ref[(1,) + spot(block)] = part[:, half:]

    @pl.when((step >= 3) & (step < 6))
    def _():
        entry_grad_ref[:, :patches] += dot(w_ref[...], pg_ref[...], 1, 0)

    band = places["y"]

    def away(number):
        return pltpu.make_async_remote_copy(
            src_ref=rows_ref.at[number],
            dst_ref=latents_out_ref.at[band, pl.ds(number * BACK_ROWS, BACK_ROWS)],
            send_sem=row_send.at[number],
            recv_sem=row_receive.at[number],
            device_id=partner_id("y", places),
            device_id_type=MESH_ID,
        )

    def stay(number):
        return pltpu.make_async_copy(
            rows_ref.at[number + 2],
            latents_out_ref.at[band, pl.ds(number * BACK_ROWS, BACK_ROWS)],
            row_send.at[number + 2],
        )

    for number in range(4):
        block = (number + 2) % 4

        @pl.when(step == 6 + number)
        def _():
            entry_grad = entry_grad_ref[:, block * BACK_ROWS : (block + 1) * BACK_ROWS].T
            source = (other_x_ref if number < 2 else own_x_ref)[...].astype(f32)
            factor = lax.rsqrt(jnp.mean(source * source, axis=1, keepdims=True) + epsilon)
            normed = source * factor
            (scale,) = modes_of(modulation_ref, "scale_one")
            inner = entry_grad * (1.0 + scale)
            grads = middle_grad_ref[...] + factor * (
                inner - normed * jnp.mean(inner * normed, axis=1, keepdims=True)
            )
            rows_ref[number] = grads.astype(bf16)
            add = lambda v: jnp.sum(v, axis=0, keepdims=True)
            sums = in_blocks([add(entry_grad), add(entry_grad * normed)])
            late = 2 * ADA_PIECES
            if number == 0:
                sums_ref[doubling.own() + (slice(0, late),)] = sums
                sums_ref[doubling.own() + (slice(late, None),)] = gain_terms_ref[...]
            else:
                sums_ref[doubling.own() + (slice(0, late),)] += sums
            if number < 2:
                away(number).start()
            else:
                stay(number - 2).start()

    def due(now):
        for stream, source, when, out in streams:
            for phase in range(-1, phases):
                if when[phase + 1] != now:
                    continue
                if phase >= 0:
                    stream.copy(phase, source).wait()

                    def put(values):
                        out[...] = values.astype(bf16)

                    stream.add(phase, source if phase == 0 else None, put)
                if phase + 1 < phases:
                    stream.copy(phase + 1, source).start()

    first_ada = 10
    ada_steps = 6 * ADA_PIECES

    @pl.when(step == first_ada)
    def _():
        ada.prepare()

    points = {when for plan in tail_plan(dims) for when in plan[3]} | set(gather_points)
    hub = first_ada + ADA_EARLY

    def point(now):
        doubling.events(now, gather_points)
        due(now)

    dispatch(step, {now: functools.partial(point, now) for now in points if now < hub})

    @pl.when(step == hub)
    def _():
        for later in sorted(points):
            if hub <= later <= gather_points[-1]:
                point(later)
        ada.late(sums_ref, phases)

    @pl.when(step >= first_ada)
    def _():
        number = step - first_ada
        ada.block(jnp.where(number < ADA_EARLY, number + ada_steps - ADA_EARLY, number - ADA_EARLY))

    class_ref = entry_grad_ref.at[pl.ds(0, class_out_ref.shape[0])]
    class_copy = pltpu.make_async_copy(class_ref, class_out_ref, ada_sem.at[1])
    final = first_ada + ada_steps - 1

    @pl.when(step == final)
    def _():
        ada.finish(class_ref)
        class_copy.start()

    @pl.when(step == final)
    def _():
        for later in sorted(points):
            if later > gather_points[-1]:
                point(later)
        for number in range(2):
            away(number).wait()
            stay(number).wait()
        class_copy.wait()


def back_step(
    projected_grad, qkv_weight, entry, latents, other_x, middle_grad, modulation, gain_rows,
    ada_weight, early, table, time_weight, class_table,
):
    patches, width = entry.shape
    dims = pair_axes()
    rows = width // lax.axis_size("img")
    sections = (0, 2, 1, 0, 1, 2)

    def section_of(step):
        place = jnp.int32(sections[-1])
        for number, section in enumerate(sections[:-1]):
            place = jnp.where(step == number, section, place)
        return place

    weight_section = lambda t: jnp.clip(t - 3, 0, 2)
    row_block = lambda t: lax.rem(jnp.clip(t - 6, 0, 3) + 2, 4)
    block = pl.BlockSpec((BACK_ROWS, width), lambda t: (row_block(t), 0))
    own = own_image(BACK_ROWS, width, lambda t: jnp.clip(t - 8, 0, 1))
    other = pl.BlockSpec((BACK_ROWS, width), lambda t: (jnp.clip(t - 6, 0, 1), 0))
    tails = [(rows, 384)] * 3 + [(rows, width // 2)]
    classes = class_table.shape[0]
    images = early.shape[0]
    time_rows = time_weight.shape[0] // lax.axis_size("img")
    ada_steps = 6 * ADA_PIECES
    half_steps = ada_steps // 2

    def ada_block(t):
        number = jnp.maximum(t - 10, 0)
        return jnp.where(number < ADA_EARLY, number + ada_steps - ADA_EARLY, number - ADA_EARLY)

    wide = (2,) * len(dims)
    scratch = [
        pltpu.VMEM((width, width), f32),
        pltpu.VMEM(wide + (rows, width), bf16),
        pltpu.VMEM(wide + (rows, width // 2), bf16),
        pltpu.VMEM((4, BACK_ROWS, width), bf16),
        pltpu.SemaphoreType.DMA((4,)),
        pltpu.SemaphoreType.DMA((2,)),
        pltpu.VMEM((classes, width), bf16),
        pltpu.VMEM((ada_steps, images, ADA_COLUMNS), f32),
        pltpu.VMEM((2, images, 128), f32),
        pltpu.VMEM((images, width), f32),
        pltpu.VMEM((images, width), f32),
        pltpu.VMEM((rows, images), bf16),
        pltpu.VMEM((time_rows, images), bf16),
        pltpu.VMEM((half_steps, rows, ADA_COLUMNS), f32),
        pltpu.SemaphoreType.DMA((2,)),
    ]
    for tail in tails:
        scratch += halving_scratch(dims, tail)
    return pl.pallas_call(
        functools.partial(back_kernel, dims),
        grid=(10 + ada_steps,),
        in_specs=[
            pl.BlockSpec((None, width, patches), lambda t: (section_of(t), 0, 0)),
            pl.BlockSpec((width, width), lambda t: (0, weight_section(t))),
            whole((patches, width)),
            own,
            other,
            block,
            whole((1, 6 * width)),
            whole((2, ADA_COLUMNS)),
            pl.BlockSpec((width, ADA_COLUMNS), lambda t: (0, ada_block(t))),
            whole(early.shape),
            whole(table.shape),
            whole(time_weight.shape),
            pl.BlockSpec(memory_space=pl.ANY),
        ],
        out_specs=[
            pl.BlockSpec(memory_space=pl.ANY),
            whole((rows, width)),
            whole((rows, width // 2)),
            whole((rows, 3 * width)),
            pl.BlockSpec((1, ADA_COLUMNS), lambda t: (0, ada_block(t))),
            whole((time_rows, width // 2)),
            pl.BlockSpec(memory_space=pl.ANY),
            whole((1, ADA_COLUMNS)),
        ],
        out_shape=[
            jax.ShapeDtypeStruct((2, patches // 2, width), bf16),
            jax.ShapeDtypeStruct((rows, width), bf16),
            jax.ShapeDtypeStruct((rows, width // 2), bf16),
            jax.ShapeDtypeStruct((rows, 3 * width), f32),
            jax.ShapeDtypeStruct((1, 6 * width), f32),
            jax.ShapeDtypeStruct((time_rows, width // 2), f32),
            jax.ShapeDtypeStruct((classes, width), f32),
            jax.ShapeDtypeStruct((1, ADA_COLUMNS), f32),
        ],
        scratch_shapes=scratch
        + [pltpu.VMEM(wide + (2 * ADA_PIECES + 2, ADA_COLUMNS), f32)]
        + doubling_scratch(dims),
        compiler_params=params_of(collective_id=2, has_side_effects=True),
        cost_estimate=cost(12 * patches * width * width, 40e6),
        name="back",
    )(
        projected_grad, qkv_weight, entry, latents, other_x, middle_grad, modulation, gain_rows,
        ada_weight, early, table, time_weight, class_table,
    )


def pick(values, index):
    return lax.dynamic_index_in_dim(values, index, 0, keepdims=False)


def per_device_whole(
    latents,
    cotangent,
    labels,
    group_ids,
    group_logits,
    row_pos,
    col_pos,
    time_weight,
    class_table,
    ada_weight,
    ada_bias,
    qkv_weight,
    query_gain,
    key_gain,
    proj_weight,
    gateup_weight,
    down_weight,
):
    width = latents.shape[-1]
    bands = lax.axis_size("band")
    band_index = lax.axis_index("band")

    def from_other(values):
        return lax.ppermute(values, "band", [(0, 1), (1, 0)])

    other_x = from_other(pick(latents, 1 - band_index))
    away_c, _ = lax.optimization_barrier((pick(cotangent, 1 - band_index), other_x))
    other_c = from_other(away_c)
    places = jnp.stack([row_pos, col_pos], axis=1)
    places = jnp.concatenate([places, from_other(places)], axis=0)

    quarter = HD // 4
    frequency = jnp.exp(-math.log(10000.0) * jnp.arange(quarter, dtype=f32) / quarter)
    angles = frequency[:, None] * places.astype(f32).T[:, None, :]
    cosine, sine = jnp.cos(angles), jnp.sin(angles)
    cosine = jnp.concatenate([cosine[0], cosine[0], cosine[1], cosine[1]], axis=0)
    sine = jnp.concatenate([-sine[0], sine[0], -sine[1], sine[1]], axis=0)

    table = time_features(jax.nn.sigmoid(group_logits), FREQ // 2).astype(bf16)
    own_group = pick(group_ids, band_index)
    own_label = pick(labels, band_index)
    before = jnp.dot(
        pick(table, own_group)[None], time_weight, preferred_element_type=f32
    ) + pick(class_table, own_label)[None].astype(f32)
    condition = jax.nn.silu(before).astype(bf16)
    modulation = jnp.dot(condition, ada_weight, preferred_element_type=f32) + ada_bias
    scaling = HD ** (-0.5)
    gains = jnp.stack([query_gain, key_gain])[:, :, None]
    scaled_gains = gains * jnp.array([scaling * LOG2E, 1.0], f32)[:, None, None]
    entry_one, heads, unit, factor = front(
        latents, other_x, modulation, qkv_weight, scaled_gains, cosine, sine
    )
    mixed, query = attend(heads)
    mixed = mixed.reshape(width, -1)
    attended, entry_two, fed_grad = middle_step(
        mixed, proj_weight, latents, other_x, cotangent, other_c, modulation
    )
    fed, entry_two_grad, grad_down, gateup_done, gateup_left, *carries = mlp(
        entry_two, fed_grad, gateup_weight, down_weight
    )
    codes = jnp.stack([own_label, own_group])[:, None].astype(f32)
    codes = jnp.pad(codes, ((0, 2), (0, ADA_COLUMNS - 1)))
    (
        result, middle_grad, projected_grad, gain_terms,
        sum_down, gateup_last, gateup_carried, sum_proj, modes_early,
    ) = core_step(
        fed, entry_two_grad, latents, other_x, cotangent, other_c, attended, mixed, proj_weight,
        modulation, codes, query, heads, unit, factor, gains, cosine, sine, grad_down, gateup_left,
        carries,
    )
    gain_rows = jnp.pad(jnp.sum(gain_terms, axis=2), ((0, 0), (0, 128 - HD))).reshape(1, -1)
    gain_rows = jnp.pad(gain_rows, ((0, 1), (0, ADA_COLUMNS - gain_rows.shape[1])))
    (
        grad_latents, qkv_pair, qkv_single, sum_ada, sum_bias, sum_time, sum_class, gain_sums,
    ) = back_step(
        projected_grad.reshape(3, width, -1), qkv_weight, entry_one, latents, other_x, middle_grad,
        modulation, gain_rows, ada_weight, modes_early.reshape((-1,) + modes_early.shape[-2:]), table,
        time_weight, class_table,
    )
    sum_bias = sum_bias.reshape(-1)
    sum_query_gain, sum_key_gain = gain_sums[0, :HD], gain_sums[0, 128 : 128 + HD]
    sum_down = sum_down.reshape(-1, sum_down.shape[-1]).astype(f32)
    sum_proj = sum_proj.astype(f32)
    gateup_carried = gateup_carried.reshape((len(CARRIED), 2) + gateup_carried.shape[1:])
    gateup = jnp.concatenate([gateup_done, gateup_carried, gateup_last[None]], axis=0)
    sum_gateup = jnp.transpose(gateup, (2, 0, 1, 3)).reshape(gateup.shape[2], -1).astype(f32)
    sum_qkv = jnp.where(
        band_index == 0,
        jnp.concatenate([qkv_pair, qkv_single], axis=1),
        jnp.concatenate([qkv_single, qkv_pair], axis=1),
    ).astype(f32)
    return (
        result,
        grad_latents,
        sum_time,
        sum_class,
        sum_ada,
        sum_bias,
        sum_qkv,
        sum_query_gain,
        sum_key_gain,
        sum_proj,
        sum_gateup,
        sum_down,
    )


def per_device(latents, *others):
    if latents.shape[0] == lax.axis_size("band") == 2 and lax.axis_size("img") == 16:
        return per_device_whole(latents, *others)
    return per_device_banded(latents, *others)


def solution(mesh):
    return jax.shard_map(
        per_device,
        mesh=mesh,
        in_specs=(
            P("img", "band", None),
            P("img", "band", None),
            P("img"),
            P("img"),
            P(),
            P("band"),
            P("band"),
            P(),
            P(),
            P(),
            P(),
            P(),
            P(),
            P(),
            P(),
            P(),
            P(),
        ),
        out_specs=(
            P("img", "band", None),
            P("img", "band", None),
            P("img", "band"),
            P(),
            P("img", "band"),
            P(),
            P("img", "band"),
            P(),
            P(),
            P("img", "band"),
            P("img", "band"),
            P("img", "band"),
        ),
        check_vma=False,
    )
```

```python
import functools
import math

import jax
import jax.numpy as jnp
from jax import lax
from jax.experimental import pallas as pl
from jax.experimental.pallas import tpu as pltpu
from jax.sharding import PartitionSpec as P

HEADS = 16
HD = 72
FF = 3072
NCLASS = 1000
FREQ = 256
GROUPS = 8


highest = lax.Precision.HIGHEST
epsilon = 1e-06


def unit_rms(values):
    return values * lax.rsqrt(jnp.mean(values * values, axis=-1, keepdims=True) + epsilon)


def unit_rms_back(values, grads):
    factor = lax.rsqrt(jnp.mean(values * values, axis=-1, keepdims=True) + epsilon)
    normed = values * factor
    return factor * (grads - normed * jnp.mean(grads * normed, axis=-1, keepdims=True))


def rope_tables(row_pos, col_pos, quarter):
    frequency = jnp.exp(-math.log(10000.0) * jnp.arange(quarter, dtype=jnp.float32) / quarter)
    row_angle = row_pos.astype(jnp.float32)[:, None] * frequency[None, :]
    col_angle = col_pos.astype(jnp.float32)[:, None] * frequency[None, :]
    cosine = jnp.concatenate(
        [jnp.cos(row_angle), jnp.cos(row_angle), jnp.cos(col_angle), jnp.cos(col_angle)], axis=-1
    )
    sine = jnp.concatenate(
        [-jnp.sin(row_angle), jnp.sin(row_angle), -jnp.sin(col_angle), jnp.sin(col_angle)], axis=-1
    )
    return (cosine, sine)


def partner(values, quarter):
    return jnp.concatenate(
        [
            values[..., quarter : 2 * quarter],
            values[..., :quarter],
            values[..., 3 * quarter :],
            values[..., 2 * quarter : 3 * quarter],
        ],
        axis=-1,
    )


def time_features(times, half):
    frequency = jnp.exp(-math.log(10000.0) * jnp.arange(half, dtype=jnp.float32) / half)
    angles = 1000.0 * times[:, None] * frequency[None, :]
    return jnp.concatenate([jnp.cos(angles), jnp.sin(angles)], axis=-1)


def silu_slope(values):
    sigma = jax.nn.sigmoid(values)
    return sigma * (1.0 + values * (1.0 - sigma))


def per_device_banded(
    latents,
    cotangent,
    labels,
    group_ids,
    group_logits,
    row_pos,
    col_pos,
    time_weight,
    class_table,
    ada_weight,
    ada_bias,
    qkv_weight,
    query_gain,
    key_gain,
    proj_weight,
    gateup_weight,
    down_weight,
):
    images, rows, width = latents.shape
    quarter = HD // 4
    scaling = HD ** (-0.5)
    group_hot = (group_ids[:, None] == jnp.arange(GROUPS, dtype=jnp.int32)[None, :]).astype(
        jnp.float32
    )
    times = jax.nn.sigmoid(jnp.dot(group_hot, group_logits, precision=highest))
    features = time_features(times, FREQ // 2).astype(jnp.bfloat16)
    class_hot = (labels[:, None] == jnp.arange(NCLASS, dtype=jnp.int32)[None, :]).astype(
        jnp.bfloat16
    )
    before = jnp.dot(features, time_weight, preferred_element_type=jnp.float32) + jnp.dot(
        class_hot, class_table, preferred_element_type=jnp.float32
    )
    condition = jax.nn.silu(before).astype(jnp.bfloat16)
    modulation = jnp.dot(condition, ada_weight, preferred_element_type=jnp.float32) + ada_bias
    pieces = [modulation[:, None, member * width : (member + 1) * width] for member in range(6)]
    shift_one, scale_one, gate_one, shift_two, scale_two, gate_two = pieces
    cosine, sine = rope_tables(row_pos, col_pos, quarter)
    cosine = cosine[None, :, None, :]
    sine = sine[None, :, None, :]

    def turned(values):
        return values * cosine + partner(values, quarter) * sine

    def turned_back(grads):
        return grads * cosine + partner(grads * sine, quarter)

    source = latents.astype(jnp.float32)
    normed_one = unit_rms(source)
    entry_one = (normed_one * (1.0 + scale_one) + shift_one).astype(jnp.bfloat16)
    projected = jnp.einsum("bpd,de->bpe", entry_one, qkv_weight, preferred_element_type=jnp.float32)
    shape = (images, rows, HEADS, HD)
    query_raw = projected[..., :width].reshape(shape)
    key_raw = projected[..., width : 2 * width].reshape(shape)
    value_bf = projected[..., 2 * width :].reshape(shape).astype(jnp.bfloat16)
    query_unit = unit_rms(query_raw)
    key_unit = unit_rms(key_raw)
    query_bf = turned(query_unit * query_gain).astype(jnp.bfloat16)
    key_bf = turned(key_unit * key_gain).astype(jnp.bfloat16)
    peak = jnp.full((images, HEADS, rows), -1e30, jnp.float32)
    key_piece = lax.all_gather(key_bf, "band", axis=1, tiled=True)
    value_piece = lax.all_gather(value_bf, "band", axis=1, tiled=True)
    scores = (
        jnp.einsum("bqhd,bkhd->bhqk", query_bf, key_piece, preferred_element_type=jnp.float32)
        * scaling
    )
    new_peak = jnp.maximum(peak, jnp.max(scores, axis=-1))
    weights = jnp.exp(scores - new_peak[..., None])
    total = jnp.sum(weights, axis=-1)
    update = jnp.einsum(
        "bhqk,bkhd->bqhd",
        weights.astype(jnp.bfloat16),
        value_piece,
        preferred_element_type=jnp.float32,
    )
    accum = update
    peak, total, accum = (new_peak, total, accum)
    mixed = accum / jnp.transpose(total, (0, 2, 1))[..., None]
    log_total = peak + jnp.log(total)
    mixed_bf = mixed.reshape(images, rows, width).astype(jnp.bfloat16)
    attended = jnp.einsum("bpd,de->bpe", mixed_bf, proj_weight, preferred_element_type=jnp.float32)
    middle = source + gate_one * attended
    normed_two = unit_rms(middle)
    entry_two = (normed_two * (1.0 + scale_two) + shift_two).astype(jnp.bfloat16)
    gate_up = jnp.einsum(
        "bpd,de->bpe", entry_two, gateup_weight, preferred_element_type=jnp.float32
    )
    gate_part = gate_up[..., :FF]
    up_part = gate_up[..., FF:]
    hidden = (jax.nn.silu(gate_part) * up_part).astype(jnp.bfloat16)
    fed = jnp.einsum("bpf,fd->bpd", hidden, down_weight, preferred_element_type=jnp.float32)
    result = (middle + gate_two * fed).astype(jnp.bfloat16)
    upstream = cotangent.astype(jnp.float32)
    fed_grad = (upstream * gate_two).astype(jnp.bfloat16)
    grad_gate_two = jnp.sum(upstream * fed, axis=1)
    grad_down = jnp.einsum("bpf,bpd->fd", hidden, fed_grad, preferred_element_type=jnp.float32)
    hidden_grad = jnp.einsum(
        "bpd,fd->bpf", fed_grad, down_weight, preferred_element_type=jnp.float32
    )
    gate_grad = hidden_grad * up_part * silu_slope(gate_part)
    up_grad = hidden_grad * jax.nn.silu(gate_part)
    gate_up_grad = jnp.concatenate([gate_grad, up_grad], axis=-1).astype(jnp.bfloat16)
    grad_gateup = jnp.einsum(
        "bpd,bpe->de", entry_two, gate_up_grad, preferred_element_type=jnp.float32
    )
    entry_two_grad = jnp.einsum(
        "bpe,de->bpd", gate_up_grad, gateup_weight, preferred_element_type=jnp.float32
    )
    grad_scale_two = jnp.sum(entry_two_grad * normed_two, axis=1)
    grad_shift_two = jnp.sum(entry_two_grad, axis=1)
    middle_grad = upstream + unit_rms_back(middle, entry_two_grad * (1.0 + scale_two))
    grad_gate_one = jnp.sum(middle_grad * attended, axis=1)
    attended_grad = (middle_grad * gate_one).astype(jnp.bfloat16)
    grad_proj = jnp.einsum(
        "bpd,bpe->de", mixed_bf, attended_grad, preferred_element_type=jnp.float32
    )
    mixed_grad = jnp.einsum(
        "bpe,de->bpd", attended_grad, proj_weight, preferred_element_type=jnp.float32
    )
    mixed_grad_bf = mixed_grad.reshape(shape).astype(jnp.bfloat16)
    offsets = jnp.transpose(jnp.sum(mixed_grad_bf.astype(jnp.float32) * mixed, axis=-1), (0, 2, 1))
    key_piece = lax.all_gather(key_bf, "band", axis=1, tiled=True)
    value_piece = lax.all_gather(value_bf, "band", axis=1, tiled=True)
    scores = (
        jnp.einsum("bqhd,bkhd->bhqk", query_bf, key_piece, preferred_element_type=jnp.float32)
        * scaling
    )
    probs = jnp.exp(scores - log_total[..., None])
    prob_grad = jnp.einsum(
        "bqhd,bkhd->bhqk", mixed_grad_bf, value_piece, preferred_element_type=jnp.float32
    )
    score_grad = (probs * (prob_grad - offsets[..., None])).astype(jnp.bfloat16)
    query_grad = (
        jnp.einsum("bhqk,bkhd->bqhd", score_grad, key_piece, preferred_element_type=jnp.float32)
        * scaling
    )
    key_term = (
        jnp.einsum("bhqk,bqhd->bkhd", score_grad, query_bf, preferred_element_type=jnp.float32)
        * scaling
    )
    value_term = jnp.einsum(
        "bhqk,bqhd->bkhd",
        probs.astype(jnp.bfloat16),
        mixed_grad_bf,
        preferred_element_type=jnp.float32,
    )
    key_grads = key_term
    value_grads = value_term
    query_grad, key_grads, value_grads = (query_grad, key_grads, value_grads)
    key_local, value_local = (
        lax.psum_scatter(
            key_grads.astype(jnp.bfloat16), "band", scatter_dimension=1, tiled=True
        ).astype(jnp.float32),
        lax.psum_scatter(
            value_grads.astype(jnp.bfloat16), "band", scatter_dimension=1, tiled=True
        ).astype(jnp.float32),
    )
    query_turned = turned_back(query_grad)
    key_turned = turned_back(key_local)
    local_query_gain = jnp.sum(query_turned * query_unit, axis=(0, 1, 2))
    local_key_gain = jnp.sum(key_turned * key_unit, axis=(0, 1, 2))
    query_raw_grad = unit_rms_back(query_raw, query_turned * query_gain)
    key_raw_grad = unit_rms_back(key_raw, key_turned * key_gain)
    flat = (images, rows, width)
    projected_grad = jnp.concatenate(
        [query_raw_grad.reshape(flat), key_raw_grad.reshape(flat), value_local.reshape(flat)],
        axis=-1,
    ).astype(jnp.bfloat16)
    grad_qkv = jnp.einsum(
        "bpd,bpe->de", entry_one, projected_grad, preferred_element_type=jnp.float32
    )
    entry_one_grad = jnp.einsum(
        "bpe,de->bpd", projected_grad, qkv_weight, preferred_element_type=jnp.float32
    )
    grad_scale_one = jnp.sum(entry_one_grad * normed_one, axis=1)
    grad_shift_one = jnp.sum(entry_one_grad, axis=1)
    source_grad = middle_grad + unit_rms_back(source, entry_one_grad * (1.0 + scale_one))
    grad_latents = source_grad.astype(jnp.bfloat16)
    band_partial = jnp.concatenate(
        [
            grad_shift_one,
            grad_scale_one,
            grad_gate_one,
            grad_shift_two,
            grad_scale_two,
            grad_gate_two,
        ],
        axis=-1,
    )
    modulation_grad, band_query_gain, band_key_gain = (
        lax.psum(band_partial.astype(jnp.bfloat16), "band").astype(jnp.float32),
        lax.psum(local_query_gain[None, :].astype(jnp.bfloat16), "band").astype(jnp.float32),
        lax.psum(local_key_gain[None, :].astype(jnp.bfloat16), "band").astype(jnp.float32),
    )
    condition_grad = jnp.dot(modulation_grad, ada_weight.astype(jnp.float32).T, precision=highest)
    before_grad = condition_grad * silu_slope(before)
    condition_all, features_all, modulation_all, before_all, query_gain_rows, key_gain_rows = (
        lax.all_gather(
            condition.astype(jnp.float32).astype(jnp.bfloat16), "img", axis=0, tiled=True
        ).astype(jnp.float32),
        lax.all_gather(
            features.astype(jnp.float32).astype(jnp.bfloat16), "img", axis=0, tiled=True
        ).astype(jnp.float32),
        lax.all_gather(modulation_grad.astype(jnp.bfloat16), "img", axis=0, tiled=True).astype(
            modulation_grad.dtype
        ),
        lax.all_gather(before_grad.astype(jnp.bfloat16), "img", axis=0, tiled=True).astype(
            before_grad.dtype
        ),
        lax.all_gather(band_query_gain.astype(jnp.bfloat16), "img", axis=0, tiled=True).astype(
            band_query_gain.dtype
        ),
        lax.all_gather(band_key_gain.astype(jnp.bfloat16), "img", axis=0, tiled=True).astype(
            band_key_gain.dtype
        ),
    )
    labels_all = lax.all_gather(labels, "img", axis=0, tiled=True)
    img_index = lax.axis_index("img")
    band_index = lax.axis_index("band")
    ada_rows = width // lax.axis_size("img")
    ada_cols = 6 * width // lax.axis_size("band")
    time_rows = FREQ // lax.axis_size("img")
    time_cols = width // lax.axis_size("band")
    condition_part = lax.dynamic_slice_in_dim(condition_all, img_index * ada_rows, ada_rows, 1)
    modulation_part = lax.dynamic_slice_in_dim(modulation_all, band_index * ada_cols, ada_cols, 1)
    sum_ada = jnp.dot(condition_part.T, modulation_part, precision=highest)
    features_part = lax.dynamic_slice_in_dim(features_all, img_index * time_rows, time_rows, 1)
    before_part = lax.dynamic_slice_in_dim(before_all, band_index * time_cols, time_cols, 1)
    sum_time = jnp.dot(features_part.T, before_part, precision=highest)
    class_all = (labels_all[:, None] == jnp.arange(NCLASS, dtype=jnp.int32)[None, :]).astype(
        jnp.float32
    )
    sum_class = jnp.dot(class_all.T, before_all, precision=highest)
    sum_bias = jnp.sum(modulation_all, axis=0)
    sum_query_gain = jnp.sum(query_gain_rows, axis=0)
    sum_key_gain = jnp.sum(key_gain_rows, axis=0)
    part_qkv, part_proj, part_gateup, part_down = (
        lax.psum_scatter(
            grad_qkv.astype(jnp.bfloat16), "img", scatter_dimension=0, tiled=True
        ).astype(jnp.float32),
        lax.psum_scatter(
            grad_proj.astype(jnp.bfloat16), "img", scatter_dimension=0, tiled=True
        ).astype(jnp.float32),
        lax.psum_scatter(
            grad_gateup.astype(jnp.bfloat16), "img", scatter_dimension=0, tiled=True
        ).astype(jnp.float32),
        lax.psum_scatter(
            grad_down.astype(jnp.bfloat16), "img", scatter_dimension=0, tiled=True
        ).astype(jnp.float32),
    )
    sum_qkv, sum_proj, sum_gateup, sum_down = (
        lax.psum_scatter(
            part_qkv.astype(jnp.bfloat16), "band", scatter_dimension=1, tiled=True
        ).astype(jnp.float32),
        lax.psum_scatter(
            part_proj.astype(jnp.bfloat16), "band", scatter_dimension=1, tiled=True
        ).astype(jnp.float32),
        lax.psum_scatter(
            part_gateup.astype(jnp.bfloat16), "band", scatter_dimension=1, tiled=True
        ).astype(jnp.float32),
        lax.psum_scatter(
            part_down.astype(jnp.bfloat16), "band", scatter_dimension=1, tiled=True
        ).astype(jnp.float32),
    )
    return (
        result,
        grad_latents,
        sum_time,
        sum_class,
        sum_ada,
        sum_bias,
        sum_qkv,
        sum_query_gain,
        sum_key_gain,
        sum_proj,
        sum_gateup,
        sum_down,
    )


HDP = 80
LOG2E = math.log2(math.e)
VMEM_MAX = 62 * 2**20
bf16 = jnp.bfloat16
f32 = jnp.float32


def dot(left, right, left_dim, right_dim):
    return lax.dot_general(
        left, right, (((left_dim,), (right_dim,)), ((), ())), preferred_element_type=f32
    )


def params_of(**extra):
    return pltpu.CompilerParams(vmem_limit_bytes=VMEM_MAX, **extra)


def whole(shape):
    return pl.BlockSpec(shape, lambda *_: (0,) * len(shape), pipeline_mode=pl.Buffered(1))


def cost(flops, bytes_accessed, transcendentals=0):
    return pl.CostEstimate(
        flops=int(flops), bytes_accessed=int(bytes_accessed), transcendentals=int(transcendentals)
    )


def partner_rows(values, low_half):
    quarter = HD // 4
    return jnp.where(
        low_half, pltpu.roll(values, HD - quarter, 0), pltpu.roll(values, quarter, 0)
    )


def low_half_mask(patches):
    row = lax.broadcasted_iota(jnp.int32, (HD, patches), 0)
    quarter = HD // 4
    return (row < quarter) | ((row >= 2 * quarter) & (row < 3 * quarter))


def tail_rows(first, second, patches):
    row = lax.broadcasted_iota(jnp.int32, (HDP - HD, patches), 0)
    return jnp.where(row == 0, first, jnp.where(row == 1, second, 0.0))


def split_two(values):
    high = values.astype(bf16).astype(f32)
    return high, values - high


MESH_ID = pl.DeviceIdType.MESH


def pair_axes():
    bits = lax.axis_size("img").bit_length() - 1
    return ["y"] + [f"b{bit}" for bit in reversed(range(bits))]


def own_places():
    img = lax.axis_index("img")
    places = {"y": lax.axis_index("band")}
    for bit in range(lax.axis_size("img").bit_length() - 1):
        places[f"b{bit}"] = lax.rem(lax.div(img, 2**bit), 2)
    return places


def partner_id(axis, places):
    if axis == "y":
        return {"band": 1 - places["y"]}
    bit = int(axis[1:])
    return {"img": lax.axis_index("img") + (1 - 2 * places[axis]) * 2**bit}


def greet(places):
    barrier = pltpu.get_barrier_semaphore()
    for axis in places:
        pl.semaphore_signal(
            barrier, inc=1, device_id=partner_id(axis, places), device_id_type=MESH_ID
        )
    pl.semaphore_wait(barrier, len(places))


def dispatch(value, cases):
    if not cases:
        return
    keys = sorted(cases)
    if len(keys) == 1:
        pl.when(value == keys[0])(cases[keys[0]])
        return
    middle = keys[len(keys) // 2]
    low = {key: cases[key] for key in keys if key < middle}
    high = {key: cases[key] for key in keys if key >= middle}
    pl.when(value < middle)(functools.partial(dispatch, value, low))
    pl.when(value >= middle)(functools.partial(dispatch, value, high))


class Halving:
    def __init__(self, places, dims, order, held, arrived, send, receive, lead=(), tail=()):
        self.places, self.dims, self.order = places, list(dims), list(order)
        self.held, self.arrived, self.send, self.receive = held, arrived, send, receive
        self.lead, self.tail = tuple(lead), tuple(tail)

    def source_index(self, mine):
        first = self.order[0]
        place = self.places[first] if mine else 1 - self.places[first]
        return [place if name == first else slice(None) for name in self.dims]

    def held_index(self, step, mine):
        picked = []
        for name in self.dims:
            place = self.order.index(name)
            if place == 0:
                continue
            if place < step:
                picked.append(self.places[name])
            elif place == step:
                picked.append(self.places[name] if mine else 1 - self.places[name])
            else:
                picked.append(slice(None))
        return picked

    def settled(self, step):
        picked = []
        for name in self.dims:
            place = self.order.index(name)
            if place > 0:
                picked.append(self.places[name] if place < step else slice(None))
        return self.lead + tuple(picked)

    def copy(self, step, source=None):
        if step == 0:
            block = source.at[tuple(self.source_index(False)) + self.tail]
        else:
            block = self.held.at[self.lead + tuple(self.held_index(step, False))]
        arrived = self.arrived[step]
        return pltpu.make_async_remote_copy(
            src_ref=block,
            dst_ref=arrived.at[self.lead] if self.lead else arrived,
            send_sem=self.send.at[self.lead + (step,)],
            recv_sem=self.receive.at[self.lead + (step,)],
            device_id=partner_id(self.order[step], self.places),
            device_id_type=MESH_ID,
        )

    def own_half(self, source, semaphore):
        return pltpu.make_async_copy(
            source.at[tuple(self.source_index(True)) + self.tail],
            self.held.at[self.lead] if self.lead else self.held,
            semaphore,
        )

    def add(self, step, source=None, put=None):
        picked = self.held_index(step, True)
        spot = self.lead + tuple(picked)
        if source is None:
            old = self.held[spot + (...,)]
        else:
            old = source[tuple(self.source_index(True)) + self.tail + (...,)]
        new = self.arrived[step][self.lead + (...,)]
        if step == len(self.order) - 1:
            put(old.astype(f32) + new.astype(f32))
        else:
            self.held[spot + (...,)] = old + new


class Doubling:
    def __init__(self, places, dims, order, blocks, send, receive):
        self.places, self.dims, self.order = places, list(dims), list(order)
        self.blocks, self.send, self.receive = blocks, send, receive

    def own(self):
        return tuple(self.places[name] for name in self.dims)

    def events(self, point, points):
        for step in range(-1, len(self.order)):
            if points[step + 1] == point:
                if step >= 0:
                    self.copy(step).wait()
                if step + 1 < len(self.order):
                    self.copy(step + 1).start()

    def copy(self, step):
        known = self.order[:step]
        spot = tuple(slice(None) if n in known else self.places[n] for n in self.dims)
        return pltpu.make_async_remote_copy(
            src_ref=self.blocks.at[spot],
            dst_ref=self.blocks.at[spot],
            send_sem=self.send.at[step],
            recv_sem=self.receive.at[step],
            device_id=partner_id(self.order[step], self.places),
            device_id_type=MESH_ID,
        )


def doubling_scratch(dims):
    return [pltpu.SemaphoreType.DMA((len(dims),))] * 2


def halving_scratch(dims, tail, lead=()):
    left = len(dims) - 1
    shapes = [lead + (2,) * left + tail]
    shapes += [lead + (2,) * (left - step) + tail for step in range(len(dims))]
    semaphores = pltpu.SemaphoreType.DMA(lead + (len(dims),))
    return [pltpu.VMEM(shape, bf16) for shape in shapes] + [semaphores, semaphores]


def order_of(dims, *first):
    rest = [name for name in reversed(dims) if name not in first]
    return list(first) + rest


def modes_of(modulation_ref, *members):
    width = modulation_ref.shape[1] // 6
    names = ("shift_one", "scale_one", "gate_one", "shift_two", "scale_two", "gate_two")
    places = [names.index(member) * width for member in members]
    return [modulation_ref[:, place : place + width] for place in places]


def front_kernel(
    own_ref, other_ref, modulation_ref, w_ref, gains_ref, cos_ref, sin_ref,
    entry_ref, heads_ref, unit_ref, factor_ref,
):
    section = pl.program_id(0)
    patches = entry_ref.shape[0]
    half = patches // 2

    @pl.when(section == 0)
    def _():
        shift, scale = modes_of(modulation_ref, "shift_one", "scale_one")
        for number, ref in enumerate((own_ref, other_ref)):
            source = ref[...].astype(f32)
            normed = source * lax.rsqrt(jnp.mean(source * source, axis=1, keepdims=True) + epsilon)
            entry_ref[number * half : (number + 1) * half, :] = (
                normed * (1.0 + scale) + shift
            ).astype(bf16)

    raw = dot(w_ref[...], entry_ref[...], 0, 1)

    @pl.when(section < 2)
    def _():
        mask = low_half_mask(patches)
        extra = tail_rows(*[jnp.where(section == 1, 1.0, 0.0)] * 2, patches)
        gain = gains_ref[0] * jnp.where(section == 0, HD ** (-0.5) * LOG2E, 1.0)
        for head in range(HEADS):
            part = raw[head * HD : (head + 1) * HD, :]
            factor = lax.rsqrt(jnp.mean(part * part, axis=0, keepdims=True) + epsilon)
            unit = part * factor
            scaled = unit * gain
            turned = scaled * cos_ref[...] + partner_rows(scaled, mask) * sin_ref[...]
            heads_ref[0, head] = jnp.concatenate([turned, extra], axis=0).astype(bf16)
            unit_ref[0, head] = unit.astype(bf16)
            factor_ref[0, head] = factor

    @pl.when(section == 2)
    def _():
        extra = tail_rows(1.0, 1.0, patches)
        for head in range(HEADS):
            part = raw[head * HD : (head + 1) * HD, :]
            heads_ref[0, head] = jnp.concatenate([part, extra], axis=0).astype(bf16)


def own_image(rows, width, block):
    return pl.BlockSpec((None, rows, width), lambda t: (lax.axis_index("band"), block(t), 0))


def front(images, other, modulation, qkv_weight, gains, cosine, sine):
    half, width = other.shape
    patches = 2 * half
    last = lambda s: jnp.minimum(s, 1)
    return pl.pallas_call(
        front_kernel,
        grid=(3,),
        in_specs=[
            own_image(half, width, lambda s: 0),
            whole((half, width)),
            whole(modulation.shape),
            pl.BlockSpec((width, width), lambda s: (0, s)),
            pl.BlockSpec((1, HD, 1), lambda s: (last(s), 0, 0)),
            whole((HD, patches)),
            whole((HD, patches)),
        ],
        out_specs=[
            pl.BlockSpec((patches, width), lambda s: (0, 0)),
            pl.BlockSpec((1, HEADS, HDP, patches), lambda s: (s, 0, 0, 0)),
            pl.BlockSpec((1, HEADS, HD, patches), lambda s: (last(s), 0, 0, 0)),
            pl.BlockSpec((1, HEADS, 1, patches), lambda s: (last(s), 0, 0, 0)),
        ],
        out_shape=[
            jax.ShapeDtypeStruct((patches, width), bf16),
            jax.ShapeDtypeStruct((3, HEADS, HDP, patches), bf16),
            jax.ShapeDtypeStruct((2, HEADS, HD, patches), bf16),
            jax.ShapeDtypeStruct((2, HEADS, 1, patches), f32),
        ],
        compiler_params=params_of(),
        cost_estimate=cost(6 * patches * width * width, 24e6),
        name="front",
    )(images, other, modulation, qkv_weight, gains, cosine, sine)


def attend_kernel(q_ref, k_ref, v_ref, mixed_ref, lse_ref, qext_ref):
    patches = q_ref.shape[-1]
    step = patches // 2
    key = k_ref[...]
    value = v_ref[...]
    for start in range(0, patches, step):
        columns = slice(start, start + step)
        scores = dot(key, q_ref[:, columns], 0, 0)
        weights = jnp.exp2(scores).astype(bf16)
        summed = dot(value, weights, 1, 0)
        total = summed[HD : HD + 1, :]
        mixed_ref[:, columns] = (summed[:HD, :] / total).astype(bf16)
        high, low = split_two(-jnp.log2(total))
        extra = jnp.concatenate([jnp.zeros((HD, step), f32), tail_rows(high, low, step)], axis=0)
        qext_ref[:, columns] = q_ref[:, columns] + extra.astype(bf16)


def attend(heads):
    patches = heads.shape[-1]
    section = lambda member: pl.BlockSpec(
        (None, None, HDP, patches), lambda h: (member, h, 0, 0)
    )
    return pl.pallas_call(
        lambda q, k, v, mixed, qext: attend_kernel(q, k, v, mixed, None, qext),
        grid=(HEADS,),
        in_specs=[section(0), section(1), section(2)],
        out_specs=[
            pl.BlockSpec((None, HD, patches), lambda h: (h, 0, 0)),
            pl.BlockSpec((None, HDP, patches), lambda h: (h, 0, 0)),
        ],
        out_shape=[
            jax.ShapeDtypeStruct((HEADS, HD, patches), bf16),
            jax.ShapeDtypeStruct((HEADS, HDP, patches), bf16),
        ],
        compiler_params=params_of(),
        cost_estimate=cost(8 * HEADS * patches * patches * HDP, 14e6, HEADS * patches * patches),
        name="attend",
    )(heads, heads, heads)


def middle_kernel(
    mixed_ref, w_ref, own_x_ref, other_x_ref, own_c_ref, other_c_ref, modulation_ref,
    attended_ref, entry_ref, fed_grad_ref,
):
    in_own = pl.program_id(0) < pl.num_programs(0) // 2
    x = jnp.where(in_own, own_x_ref[...].astype(f32), other_x_ref[...].astype(f32))
    c = jnp.where(in_own, own_c_ref[...].astype(f32), other_c_ref[...].astype(f32))
    attended = dot(mixed_ref[...], w_ref[...], 0, 0)
    attended_bf = attended.astype(bf16)
    attended_ref[...] = attended_bf
    gate_one, scale_two, shift_two, gate_two = modes_of(
        modulation_ref, "gate_one", "scale_two", "shift_two", "gate_two"
    )
    middle = x + gate_one * attended_bf.astype(f32)
    normed = middle * lax.rsqrt(jnp.mean(middle * middle, axis=1, keepdims=True) + epsilon)
    entry_ref[...] = (normed * (1.0 + scale_two) + shift_two).astype(bf16)
    fed_grad_ref[...] = (c * gate_two).astype(bf16)


def middle_step(mixed, proj_weight, latents, other_x, cotangent, other_c, modulation):
    half, width = other_x.shape
    patches = 2 * half
    rows = 256
    blocks = half // rows
    block = pl.BlockSpec((rows, width), lambda t: (t, 0))
    own = own_image(rows, width, lambda t: jnp.minimum(t, blocks - 1))
    other = pl.BlockSpec((rows, width), lambda t: (jnp.maximum(t - blocks, 0), 0))
    return pl.pallas_call(
        middle_kernel,
        grid=(patches // rows,),
        in_specs=[
            pl.BlockSpec((width, rows), lambda t: (0, t)),
            whole((width, width)),
            own,
            other,
            own,
            other,
            whole((1, 6 * width)),
        ],
        out_specs=[block] * 3,
        out_shape=[jax.ShapeDtypeStruct((patches, width), bf16)] * 3,
        compiler_params=params_of(),
        cost_estimate=cost(2 * patches * width * width, 17e6),
        name="middle",
    )(mixed, proj_weight, latents, other_x, cotangent, other_c, modulation)


MLP_TILE = 512
MLP_SUB = 256
HOSTED = 5
CARRIED = ((3, 4), (4, 2))


def mlp_kernel(
    dims, entry_ref, fed_grad_ref, wg_ref, wu_ref, wd_ref,
    fed_ref, entry_grad_ref, down_ref, done_ref, left_ref, *rest,
):
    carry_refs, rest = rest[: 2 * len(CARRIED)], rest[2 * len(CARRIED) :]
    hidden_ref, gate_grad_ref, up_grad_ref, source_ref, left_sem, held, *arrived, send, receive = rest
    tile = pl.program_id(0)
    places = own_places()
    orders = mlp_orders(dims)
    steps = len(dims)

    def streams(number):
        slot = lax.rem(number, 2)
        return [
            Halving(places, dims, orders[sub], held, arrived, send, receive, (slot, sub))
            for sub in range(2)
        ]

    def advance(number, step):
        @pl.when((number >= 0) & (number < HOSTED))
        def _():
            for sub, stream in enumerate(streams(number)):
                source = source_ref.at[sub]
                stream.copy(step, source).wait()

                def put(values):
                    done_ref[number, sub] = values.astype(bf16)

                stream.add(step, source if step == 0 else None, put)
                leaves = [place for place, (_, ended) in enumerate(CARRIED) if ended == step + 1]
                for place in leaves:

                    @pl.when(number == CARRIED[place][0])
                    def _():
                        carry_refs[2 * place + sub][...] = held[stream.settled(step + 1)]

                if step + 1 < steps:
                    goes_on = True
                    for place in leaves:
                        goes_on = goes_on & (number != CARRIED[place][0])
                    if leaves:
                        pl.when(goes_on)(stream.copy(step + 1).start)
                    else:
                        stream.copy(step + 1).start()

    @pl.when(tile == 0)
    def _():
        fed_ref[...] = jnp.zeros_like(fed_ref)
        entry_grad_ref[...] = jnp.zeros_like(entry_grad_ref)
        greet(places)

    entry = entry_ref[...]
    fed_grad = fed_grad_ref[...]
    gate = dot(entry, wg_ref[...], 1, 0)
    up = dot(entry, wu_ref[...], 1, 0)
    sigma = jax.nn.sigmoid(gate)
    silu = gate * sigma
    hidden_ref[...] = (silu * up).astype(bf16)
    hidden_grad = dot(fed_grad, wd_ref[...], 1, 1)
    gate_grad_ref[...] = (hidden_grad * up * (sigma * (1.0 + gate * (1.0 - sigma)))).astype(bf16)
    up_grad_ref[...] = (hidden_grad * silu).astype(bf16)
    advance(tile - 3, 4)
    advance(tile - 2, 2)
    advance(tile - 1, 0)
    fed_ref[...] += dot(hidden_ref[...], wd_ref[...], 1, 0)
    entry_grad_ref[...] += dot(gate_grad_ref[...], wg_ref[...], 1, 1) + dot(
        up_grad_ref[...], wu_ref[...], 1, 1
    )
    down = dot(hidden_ref[...], fed_grad, 0, 0).astype(bf16)
    column_half = down.shape[1] // 2
    down_ref[0] = down[:, :column_half]
    down_ref[1] = down[:, column_half:]
    grads = [dot(entry, ref[...], 0, 0) for ref in (gate_grad_ref, up_grad_ref)]
    blocks = 2 ** (steps - 1)
    rows = grads[0].shape[0] // blocks
    for half, grad in enumerate(grads):
        for block in range(blocks):
            spot = tuple(block // 2**bit % 2 for bit in reversed(range(steps - 1)))
            part = grad[block * rows : (block + 1) * rows, :].astype(bf16)
            for sub in range(2):
                source_ref[(sub, half) + spot] = part[:, sub * MLP_SUB : (sub + 1) * MLP_SUB]

    @pl.when(tile < HOSTED)
    def _():
        for sub, stream in enumerate(streams(tile)):
            stream.copy(0, source_ref.at[sub]).start()

    @pl.when(tile == HOSTED)
    def _():
        pltpu.make_async_copy(source_ref, left_ref, left_sem).start()

    advance(tile - 2, 3)
    advance(tile - 1, 1)

    @pl.when(tile == HOSTED)
    def _():
        pltpu.make_async_copy(source_ref, left_ref, left_sem).wait()


def mlp_orders(dims):
    return [order_of(dims, "b0", "y", "b2", "b1"), order_of(dims, "b0", "b1", "y", "b2")]


def carried_orders(dims):
    return [order[ended:] for _, ended in CARRIED for order in mlp_orders(dims)]


def carried_dims(dims):
    return [[name for name in dims if name in order] for order in carried_orders(dims)]


def mlp(entry, fed_grad, gateup_weight, down_weight):
    patches, width = entry.shape
    inner = down_weight.shape[0]
    tile = MLP_TILE
    tiles = inner // tile
    dims = pair_axes()
    rows = width // lax.axis_size("img")
    tail = (rows, MLP_SUB)
    carried = [(2,) * len(names) + tail for names in carried_dims(dims)]
    return pl.pallas_call(
        functools.partial(mlp_kernel, dims),
        grid=(tiles,),
        in_specs=[
            whole((patches, width)),
            whole((patches, width)),
            pl.BlockSpec((width, tile), lambda t: (0, t)),
            pl.BlockSpec((width, tile), lambda t: (0, tiles + t)),
            pl.BlockSpec((tile, width), lambda t: (t, 0)),
        ],
        out_specs=[
            whole((patches, width)),
            whole((patches, width)),
            pl.BlockSpec((2, tile, width // 2), lambda t: (0, t, 0)),
            whole((HOSTED - len(CARRIED), 2) + tail),
            pl.BlockSpec(memory_space=pl.ANY),
        ]
        + [whole(shape) for shape in carried],
        out_shape=[
            jax.ShapeDtypeStruct((patches, width), f32),
            jax.ShapeDtypeStruct((patches, width), f32),
            jax.ShapeDtypeStruct((2, inner, width // 2), bf16),
            jax.ShapeDtypeStruct((HOSTED - len(CARRIED), 2) + tail, bf16),
            jax.ShapeDtypeStruct((2,) + (2,) * len(dims) + tail, bf16),
        ]
        + [jax.ShapeDtypeStruct(shape, bf16) for shape in carried],
        scratch_shapes=[pltpu.VMEM((patches, tile), bf16)] * 3
        + [pltpu.VMEM((2,) + (2,) * len(dims) + tail, bf16), pltpu.SemaphoreType.DMA]
        + halving_scratch(dims, tail, (2, 2)),
        compiler_params=params_of(collective_id=0, has_side_effects=True),
        cost_estimate=cost(18 * patches * width * inner, 56e6),
        name="mlp",
    )(entry, fed_grad, gateup_weight, gateup_weight, down_weight)


ADA_COLUMNS = 384
ADA_PIECES = 3
ADA_EARLY = 4 * ADA_PIECES


def in_blocks(rows):
    return jnp.concatenate(
        [
            row[:, block * ADA_COLUMNS : (block + 1) * ADA_COLUMNS]
            for row in rows
            for block in range(ADA_PIECES)
        ],
        axis=0,
    )


TURN_ROWS = 128


def core_plan(dims):
    return [
        ("down", 0, order_of(dims, "b0", "y", "b1", "b2", "b3"), (2, 9, 25, 31, 35, 40)),
        ("down", 1, order_of(dims, "b0", "b2", "y", "b3", "b1"), (2, 9, 23, 27, 33, 35)),
        ("down", 2, order_of(dims, "b0", "b2", "b3", "b1", "y"), (0, 6, 21, 31, 35, 37)),
        ("down", 3, order_of(dims, "b0", "b1", "b2", "y", "b3"), (2, 9, 23, 31, 35, 40)),
        ("left", 0, order_of(dims, "b0", "b1", "y", "b2", "b3"), (1, 6, 11, 21, 25, 29)),
        ("left", 1, order_of(dims, "b0", "b2", "b1", "b3", "y"), (0, 3, 9, 15, 19, 21)),
        ("proj", 0, order_of(dims, "b0", "b1", "y", "b2", "b3"), (7, 11, 27, 33, 37, 44)),
        ("carry", 0, ["b3"], (0, 3)),
        ("carry", 1, ["b3"], (0, 3)),
        ("carry", 2, ["b2", "b1", "b3"], (0, 4, 6, 9)),
        ("carry", 3, ["y", "b2", "b3"], (0, 7, 11, 15)),
    ]


def core_gather():
    return ["b3", "b2", "y", "b1", "b0"], (7, 17, 23, 29, 35, 39)


def core_kernel(
    dims, fed_ref, entry_grad_ref, own_x_ref, other_x_ref, own_c_ref, other_c_ref, attended_ref,
    all_mixed_ref, w_ref, modulation_ref, codes_ref,
    q_ref, k_ref, v_ref, mixed_ref, unit_ref, factor_ref, gains_ref, cos_ref, sin_ref,
    down_ref, left_ref, *rest,
):
    carry_refs, rest = rest[: 2 * len(CARRIED)], rest[2 * len(CARRIED) :]
    (
        result_ref, middle_grad_ref, out_ref, gain_out_ref,
        down_out_ref, left_out_ref, carry_out_ref, proj_out_ref, modes_out_ref,
        attended_grad_ref, mixed_grad_ref, proj_ref, rows_ref, row_send, row_receive,
        mg_ext_ref, acc_ref, own_sem, modes_ref, doubling_send, doubling_receive, *buffers,
    ) = rest
    step = pl.program_id(0)
    places = own_places()
    patches = q_ref.shape[-1]
    turns = patches // TURN_ROWS
    axes = len(dims)
    carries = carried_dims(dims)
    groups, used = {}, 0
    kinds = [("down", axes), ("left", axes), ("proj", axes)]
    kinds += [(f"carry{part}", len(names)) for part, names in enumerate(carries)]
    for name, count in kinds:
        groups[name] = buffers[used : used + count + 3]
        used += count + 3

    def streams():
        for number, (name, part, order, points) in enumerate(core_plan(dims)):
            names, lead, tail = dims, (), ()
            if name == "down":
                lead = (part,)
                source = down_ref
                rows = source.shape[-2] // 4
                tail = (pl.ds(part * rows, rows), slice(None))
                out, spot = down_out_ref, (part,)
            elif name == "left":
                lead = (part,)
                source = left_ref.at[part]
                out, spot = left_out_ref, (part,)
            elif name == "proj":
                source, out, spot = proj_ref, proj_out_ref, ()
            else:
                names = carries[part]
                source = carry_refs[part]
                out, spot = carry_out_ref, (part,)
            held, *arrived, send, receive = groups[name if name in groups else f"{name}{part}"]
            stream = Halving(places, names, order, held, arrived, send, receive, lead, tail)
            yield number, name, stream, source, points, out, spot

    def events(point):
        doubling.events(point, gather_points)
        for number, name, stream, source, points, out, spot in streams():
            local = name in ("proj", "carry")
            steps = len(points) - 1
            for phase in range(-1, steps):
                if points[phase + 1] != point:
                    continue
                if phase >= 0:
                    stream.copy(phase, source).wait()
                    if phase == 0 and not local:
                        stream.own_half(source, own_sem.at[number]).wait()

                    def put(values):
                        out[spot + (...,)] = values.astype(bf16)

                    stream.add(phase, source if local and phase == 0 else None, put)
                if phase + 1 < steps:
                    stream.copy(phase + 1, source).start()
                    if phase < 0 and not local:
                        stream.own_half(source, own_sem.at[number]).start()

    band = places["y"]

    def away(number):
        return pltpu.make_async_remote_copy(
            src_ref=rows_ref.at[number],
            dst_ref=result_ref.at[band, pl.ds(number * TURN_ROWS, TURN_ROWS)],
            send_sem=row_send.at[number],
            recv_sem=row_receive.at[number],
            device_id=partner_id("y", places),
            device_id_type=MESH_ID,
        )

    def stay(number):
        return pltpu.make_async_copy(
            rows_ref.at[number + turns // 2],
            result_ref.at[band, pl.ds(number * TURN_ROWS, TURN_ROWS)],
            row_send.at[number + turns // 2],
        )

    @pl.when(step == 0)
    def _():
        greet(places)

    gather_order, gather_points = core_gather()
    doubling = Doubling(places, dims, gather_order, modes_ref, doubling_send, doubling_receive)
    width = w_ref.shape[0]
    half = width // 2
    pair = 2 * TURN_ROWS

    def turn(number):
        x_ref, c_ref = (own_x_ref, own_c_ref) if number >= turns // 2 else (other_x_ref, other_c_ref)
        gate_one, scale_two, gate_two = modes_of(modulation_ref, "gate_one", "scale_two", "gate_two")
        attended = attended_ref[...].astype(f32)
        upstream = c_ref[...].astype(f32)
        fed = fed_ref[...]
        middle = x_ref[...].astype(f32) + gate_one * attended
        rows_ref[number] = (middle + gate_two * fed).astype(bf16)
        factor = lax.rsqrt(jnp.mean(middle * middle, axis=1, keepdims=True) + epsilon)
        normed = middle * factor
        entry_grad = entry_grad_ref[...]
        inner = entry_grad * (1.0 + scale_two)
        middle_grad = upstream + factor * (
            inner - normed * jnp.mean(inner * normed, axis=1, keepdims=True)
        )
        middle_grad_ref[...] = middle_grad
        start = (number + turns // 2) % turns * TURN_ROWS
        attended_grad_ref[start : start + TURN_ROWS, :] = (middle_grad * gate_one).astype(bf16)
        add = lambda v: jnp.sum(v, axis=0, keepdims=True)
        sums = in_blocks(
            [
                add(middle_grad * attended),
                add(entry_grad),
                add(entry_grad * normed),
                add(upstream * fed),
            ]
        )
        if number == 0:
            modes_ref[doubling.own() + (slice(0, ADA_EARLY),)] = sums
            modes_ref[doubling.own() + (slice(ADA_EARLY, None),)] = codes_ref[...]
        else:
            modes_ref[doubling.own() + (slice(0, ADA_EARLY),)] += sums
        if number < turns // 2:
            away(number).start()
        else:
            stay(number - turns // 2).start()
        if number % 2 == 1:
            first = start - TURN_ROWS
            grads = dot(w_ref[...], attended_grad_ref[first : first + pair, :], 1, 1)
            for head in range(HEADS):
                mixed_grad_ref[head, :, first : first + pair] = grads[
                    head * HD : (head + 1) * HD, :
                ].astype(bf16)
        if number == turns - 1:
            blocks = 2 ** (axes - 1)
            rows = width // blocks
            grads = dot(all_mixed_ref[...], attended_grad_ref[...], 1, 0)
            for block in range(blocks):
                spot = tuple(block // 2**bit % 2 for bit in reversed(range(axes - 1)))
                part = grads[block * rows : (block + 1) * rows, :].astype(bf16)
                proj_ref[(0,) + spot] = part[:, :half]
                proj_ref[(1,) + spot] = part[:, half:]
        events(number)

    for number in range(turns):

        @pl.when(step == number)
        def _():
            turn(number)

    points = {point for plan in core_plan(dims) for point in plan[3]} | set(gather_points)

    class Events:
        @staticmethod
        def at_head(head, end):
            wanted = [now for now in range(HEADS) if turns + 2 * now + end in points]
            dispatch(
                head,
                {now: functools.partial(events, turns + 2 * now + end) for now in wanted},
            )

    @pl.when(step >= turns)
    def _():
        attend_back(
            step - turns, Events(), mixed_grad_ref,
            q_ref, k_ref, v_ref, mixed_ref, unit_ref, factor_ref, gains_ref, cos_ref, sin_ref,
            out_ref, gain_out_ref, mg_ext_ref, acc_ref,
        )

    @pl.when(step == pl.num_programs(0) - 1)
    def _():
        for point in sorted(points):
            if point >= turns + 2 * HEADS:
                events(point)
        modes_out_ref[...] = modes_ref[...]
        for number in range(turns // 2):
            away(number).wait()
            stay(number).wait()


def attend_back(
    head, events, mixed_grad_ref,
    q_ref, k_ref, v_ref, mixed_ref, unit_ref, factor_ref, gains_ref, cos_ref, sin_ref,
    out_ref, gain_out_ref, mg_ext_ref, acc_ref,
):
    patches = q_ref.shape[-1]
    step = patches // 2
    scaling = HD ** (-0.5)
    mixed_grad = mixed_grad_ref[head].astype(f32)
    offsets = jnp.sum(mixed_grad * mixed_ref[...].astype(f32), axis=0, keepdims=True)
    high, low = split_two(-offsets)
    mg_ext_ref[...] = jnp.concatenate(
        [mixed_grad, tail_rows(high, low, patches)], axis=0
    ).astype(bf16)
    key = k_ref[...]
    value = v_ref[...]
    for start in range(0, patches, step):
        columns = slice(start, start + step)
        query = q_ref[:, columns]
        grads = mg_ext_ref[:, columns]
        probs = jnp.exp2(dot(key, query, 0, 0))
        score_grad = (probs * dot(value, grads, 0, 0)).astype(bf16)
        probs_bf = probs.astype(bf16)
        acc_ref[0, :, columns] = dot(key, score_grad, 1, 0)
        key_term = dot(query, score_grad, 1, 1)
        value_term = dot(grads, probs_bf, 1, 1)
        if start == 0:
            acc_ref[1] = key_term
            acc_ref[2] = value_term
            events.at_head(head, 0)
        else:
            acc_ref[1] += key_term
            acc_ref[2] += value_term
    mask = low_half_mask(patches)
    for member, weight in ((0, scaling), (1, 1.0 / LOG2E)):
        grads = acc_ref[member, :HD, :] * weight
        turned = grads * cos_ref[...] + partner_rows(grads * sin_ref[...], mask)
        unit = unit_ref[member].astype(f32)
        product = turned * unit

        @pl.when(head == 0)
        def _():
            gain_out_ref[member] = product

        @pl.when(head > 0)
        def _():
            gain_out_ref[member] += product

        inner = turned * gains_ref[member]
        raw = factor_ref[member] * (inner - unit * jnp.mean(inner * unit, axis=0, keepdims=True))
        out_ref[member] = raw.astype(bf16)
    out_ref[2] = acc_ref[2, :HD, :].astype(bf16)
    events.at_head(head, 1)


def core_step(
    fed, entry_grad, latents, other_x, cotangent, other_c, attended, mixed, proj_weight, modulation,
    codes, query, heads, unit, factor, gains, cosine, sine, down, left, carries,
):
    half, width = other_x.shape
    patches = 2 * half
    dims = pair_axes()
    turns = patches // TURN_ROWS
    devices = lax.axis_size("img")
    split = (2,) * len(dims)
    down = down.reshape(split + (down.shape[1] // devices, down.shape[2]))
    down_tail = (down.shape[-2] // 4, down.shape[-1])
    left_tail = left.shape[-2:]
    proj_tail = (width // devices, width // 2)
    row_block = lambda t: lax.rem(jnp.minimum(t, turns - 1) + turns // 2, turns)
    block = pl.BlockSpec((TURN_ROWS, width), lambda t: (row_block(t), 0))
    own = own_image(TURN_ROWS, width, lambda t: jnp.clip(t - turns // 2, 0, turns // 2 - 1))
    other = pl.BlockSpec((TURN_ROWS, width), lambda t: (jnp.minimum(t, turns // 2 - 1), 0))
    head_of = lambda t: jnp.maximum(t - turns, 0)
    section = lambda member: pl.BlockSpec(
        (None, None, HDP, patches), lambda t: (member, head_of(t), 0, 0)
    )
    single = lambda rows: pl.BlockSpec((None, rows, patches), lambda t: (head_of(t), 0, 0))
    couple = lambda rows: pl.BlockSpec((2, None, rows, patches), lambda t: (0, head_of(t), 0, 0))
    anywhere = pl.BlockSpec(memory_space=pl.ANY)
    sums = [(4,) + down_tail, (2,) + left_tail, (len(carries),) + left_tail, proj_tail, ()]
    sums[-1] = split + (ADA_EARLY + codes.shape[0], ADA_COLUMNS)
    return pl.pallas_call(
        functools.partial(core_kernel, dims),
        grid=(turns + HEADS,),
        in_specs=[
            block,
            block,
            own,
            other,
            own,
            other,
            block,
            whole((width, patches)),
            whole((width, width)),
            whole((1, 6 * width)),
            whole(codes.shape),
            single(HDP),
            section(1),
            section(2),
            single(HD),
            couple(HD),
            couple(1),
            whole((2, HD, 1)),
            whole((HD, patches)),
            whole((HD, patches)),
            anywhere,
            anywhere,
        ]
        + [whole(carry.shape) for carry in carries],
        out_specs=[
            anywhere,
            block,
            pl.BlockSpec((3, None, HD, patches), lambda t: (0, head_of(t), 0, 0)),
            whole((2, HD, patches)),
        ]
        + [whole(shape) for shape in sums],
        out_shape=[
            jax.ShapeDtypeStruct((2, half, width), bf16),
            jax.ShapeDtypeStruct((patches, width), f32),
            jax.ShapeDtypeStruct((3, HEADS, HD, patches), bf16),
            jax.ShapeDtypeStruct((2, HD, patches), f32),
        ]
        + [jax.ShapeDtypeStruct(shape, bf16) for shape in sums[:-1]]
        + [jax.ShapeDtypeStruct(sums[-1], f32)],
        scratch_shapes=[
            pltpu.VMEM((patches, width), bf16),
            pltpu.VMEM((HEADS, HD, patches), bf16),
            pltpu.VMEM(split + proj_tail, bf16),
            pltpu.VMEM((turns, TURN_ROWS, width), bf16),
            pltpu.SemaphoreType.DMA((turns,)),
            pltpu.SemaphoreType.DMA((turns // 2,)),
            pltpu.VMEM((HDP, patches), bf16),
            pltpu.VMEM((3, HDP, patches), f32),
            pltpu.SemaphoreType.DMA((len(core_plan(dims)),)),
            pltpu.VMEM(sums[-1], f32),
        ]
        + doubling_scratch(dims)
        + halving_scratch(dims, down_tail, (4,))
        + halving_scratch(dims, left_tail, (2,))
        + halving_scratch(dims, proj_tail)
        + [ref for names in carried_dims(dims) for ref in halving_scratch(names, left_tail)],
        compiler_params=params_of(collective_id=1, has_side_effects=True),
        cost_estimate=cost(24 * HEADS * patches * patches * HDP, 70e6, HEADS * patches**2),
        name="core",
    )(
        fed, entry_grad, latents, other_x, cotangent, other_c, attended, mixed, proj_weight,
        modulation, codes, query, heads, heads, mixed.reshape(HEADS, HD, patches), unit, factor,
        gains, cosine, sine, down, left, *carries,
    )


BACK_ROWS = 256


def tail_plan(dims):
    return [
        ("pair", pl.ds(0, 384), order_of(dims, "b0", "b1", "b3", "b2", "y"), (1, 2, 5, 13, 19, 46)),
        ("pair", pl.ds(384, 384), order_of(dims, "b0", "y", "b1", "b2", "b3"), (1, 3, 7, 30, 46, 59)),
        ("pair", pl.ds(768, 384), order_of(dims, "b0", "b2", "b1", "b3", "y"), (1, 4, 14, 40, 54, 61)),
        ("single", None, order_of(dims, "b0", "b1", "b2", "y", "b3"), (2, 5, 20, 40, 54, 67)),
    ]


def tail_gather():
    return ["b2", "b3", "b1", "y", "b0"], (9, 14, 18, 42, 59, 64)


class Ada:
    def __init__(self, places, refs):
        (
            self.weight, self.early, self.table, self.time, self.classes_hbm,
            self.ada_out, self.bias_out, self.time_out, self.class_out, self.gain_out,
            self.classes, self.modes, self.codes, self.total, self.before, self.condition,
            self.features, self.parts, self.sem,
        ) = refs
        self.band = places["y"]

    def fetch(self):
        return pltpu.make_async_copy(self.classes_hbm, self.classes, self.sem.at[0])

    def prepare(self):
        images = self.early.shape[0]

        def one(image, _):
            row = pl.ds(image, 1)
            for block in range(ADA_EARLY):
                self.modes[2 * ADA_PIECES + block, row, :] = self.early[image, block : block + 1, :]
            for part in range(2):
                spot = ADA_EARLY + part
                self.codes[part, row, :] = self.early[image, spot : spot + 1, :128]
            return 0

        lax.fori_loop(0, images, one, 0)
        self.fetch().wait()
        label, group = self.codes[0][:, :1], self.codes[1][:, :1]
        place = lambda shape, axis: lax.broadcasted_iota(jnp.int32, shape, axis)
        group_hot = (group == place((images, GROUPS), 1).astype(f32)).astype(bf16)
        features = dot(group_hot, self.table[...], 1, 0).astype(bf16)
        before = dot(features, self.time[...], 1, 0) + dot(self.class_hot(label), self.classes[...], 1, 0)
        self.before[...] = before
        condition = (before * jax.nn.sigmoid(before)).astype(bf16)
        img = lax.axis_index("img")

        def own_rows(values, rows):
            shape = (rows, values.shape[1])
            picker = (place(shape, 1) == place(shape, 0) + img * rows).astype(bf16)
            return dot(picker, values, 1, 1).astype(bf16)

        self.condition[...] = own_rows(condition, self.condition.shape[0])
        self.features[...] = own_rows(features, self.features.shape[0])
        self.total[...] = jnp.zeros_like(self.total)

    def class_hot(self, label):
        shape = (label.shape[0], self.classes.shape[0])
        return (label == lax.broadcasted_iota(jnp.int32, shape, 1).astype(f32)).astype(bf16)

    def late(self, sums_ref, axes):
        late = 2 * ADA_PIECES

        def one(image, _):
            row = pl.ds(image, 1)
            spot = tuple(lax.rem(lax.div(image, 2**bit), 2) for bit in reversed(range(axes)))
            for block in range(late):
                self.modes[block, row, :] = sums_ref[spot + (slice(block, block + 1),)]
            self.gain_out[...] += sums_ref[spot + (slice(late, late + 1),)]
            return 0

        self.gain_out[...] = jnp.zeros_like(self.gain_out)
        lax.fori_loop(0, self.early.shape[0], one, 0)

    def block(self, number):
        modes = self.modes[number]
        self.bias_out[...] = jnp.sum(modes, axis=0, keepdims=True)
        modes_bf = modes.astype(bf16)
        self.total[...] += dot(modes_bf, self.weight[...], 1, 1)
        blocks = self.parts.shape[0]
        here = number - blocks * self.band

        @pl.when((here >= 0) & (here < blocks))
        def _():
            self.parts[here] = dot(self.condition[...], modes_bf, 1, 0)

    def finish(self):
        before = self.before[...]
        sigma = jax.nn.sigmoid(before)
        before_grad = self.total[...] * (sigma * (1.0 + before * (1.0 - sigma)))
        pieces, left = [], before_grad
        for _ in range(3):
            pieces.append(left.astype(bf16))
            left = left - pieces[-1].astype(f32)
        half = before.shape[1] // 2
        times = sum(dot(self.features[...], piece, 1, 0) for piece in pieces)
        self.time_out[...] = jnp.where(self.band == 0, times[:, :half], times[:, half:])
        self.class_out[0] = before_grad
        self.class_out[1, :, :128] = self.codes[0]
        for block in range(self.parts.shape[0]):
            columns = slice(block * ADA_COLUMNS, (block + 1) * ADA_COLUMNS)
            self.ada_out[:, columns] = self.parts[block]


def back_kernel(
    dims, pg_ref, w_ref, entry_ref, own_x_ref, other_x_ref, middle_grad_ref, modulation_ref,
    gain_terms_ref, ada_ref, early_ref, table_ref, time_ref, classes_ref,
    latents_out_ref, pair_out_ref, single_out_ref, ada_out_ref, bias_out_ref, time_out_ref,
    class_out_ref, gain_out_ref,
    entry_grad_ref, pair_ref, single_ref, rows_ref, row_send, row_receive,
    classes_copy_ref, modes_ref, codes_ref, total_ref, before_ref, condition_ref, features_ref,
    parts_ref, ada_sem, *buffers,
):
    step = pl.program_id(0)
    places = own_places()
    phases = len(dims)
    size = phases + 3
    *buffers, sums_ref, send, receive = buffers
    streams = []
    for place, (name, columns, order, when) in enumerate(tail_plan(dims)):
        held, *arrived, s, r = buffers[place * size : (place + 1) * size]
        tail = () if columns is None else (slice(None), columns)
        stream = Halving(places, dims, order, held, arrived, s, r, (), tail)
        if name == "pair":
            streams.append((stream, pair_ref, when, pair_out_ref.at[:, columns]))
        else:
            streams.append((stream, single_ref, when, single_out_ref))
    gather_order, gather_points = tail_gather()
    doubling = Doubling(places, dims, gather_order, sums_ref, send, receive)
    ada = Ada(
        places,
        (
            ada_ref, early_ref, table_ref, time_ref, classes_ref,
            ada_out_ref, bias_out_ref, time_out_ref, class_out_ref, gain_out_ref,
            classes_copy_ref, modes_ref, codes_ref, total_ref, before_ref, condition_ref,
            features_ref, parts_ref, ada_sem,
        ),
    )
    width = entry_grad_ref.shape[0]
    patches = entry_ref.shape[0]
    half = width // 2
    blocks = 2 ** (phases - 1)
    rows = width // blocks

    @pl.when(step == 0)
    def _():
        entry_grad_ref[...] = jnp.zeros_like(entry_grad_ref)
        ada.fetch().start()
        greet(places)

    @pl.when(step < 3)
    def _():
        def spot(block):
            return tuple(block // 2**bit % 2 for bit in reversed(range(phases - 1)))

        @pl.when(step < 2)
        def _():
            grad = dot(entry_ref[...], pg_ref[...], 0, 1)
            for block in range(blocks):
                part = grad[block * rows : (block + 1) * rows, :]
                pair_ref[(step,) + spot(block)] = part.astype(bf16)

        @pl.when(step == 2)
        def _():
            grad = dot(entry_ref[...], pg_ref[...], 0, 1)
            for block in range(blocks):
                part = grad[block * rows : (block + 1) * rows, :].astype(bf16)
                single_ref[(0,) + spot(block)] = part[:, :half]
                single_ref[(1,) + spot(block)] = part[:, half:]

    @pl.when((step >= 3) & (step < 6))
    def _():
        entry_grad_ref[:, :patches] += dot(w_ref[...], pg_ref[...], 1, 0)

    band = places["y"]

    def away(number):
        return pltpu.make_async_remote_copy(
            src_ref=rows_ref.at[number],
            dst_ref=latents_out_ref.at[band, pl.ds(number * BACK_ROWS, BACK_ROWS)],
            send_sem=row_send.at[number],
            recv_sem=row_receive.at[number],
            device_id=partner_id("y", places),
            device_id_type=MESH_ID,
        )

    def stay(number):
        return pltpu.make_async_copy(
            rows_ref.at[number + 2],
            latents_out_ref.at[band, pl.ds(number * BACK_ROWS, BACK_ROWS)],
            row_send.at[number + 2],
        )

    for number in range(4):
        block = (number + 2) % 4

        @pl.when(step == 6 + number)
        def _():
            entry_grad = entry_grad_ref[:, block * BACK_ROWS : (block + 1) * BACK_ROWS].T
            source = (other_x_ref if number < 2 else own_x_ref)[...].astype(f32)
            factor = lax.rsqrt(jnp.mean(source * source, axis=1, keepdims=True) + epsilon)
            normed = source * factor
            (scale,) = modes_of(modulation_ref, "scale_one")
            inner = entry_grad * (1.0 + scale)
            grads = middle_grad_ref[...] + factor * (
                inner - normed * jnp.mean(inner * normed, axis=1, keepdims=True)
            )
            rows_ref[number] = grads.astype(bf16)
            add = lambda v: jnp.sum(v, axis=0, keepdims=True)
            sums = in_blocks([add(entry_grad), add(entry_grad * normed)])
            late = 2 * ADA_PIECES
            if number == 0:
                sums_ref[doubling.own() + (slice(0, late),)] = sums
                sums_ref[doubling.own() + (slice(late, None),)] = gain_terms_ref[...]
            else:
                sums_ref[doubling.own() + (slice(0, late),)] += sums
            if number < 2:
                away(number).start()
            else:
                stay(number - 2).start()

    def due(now):
        for stream, source, when, out in streams:
            for phase in range(-1, phases):
                if when[phase + 1] != now:
                    continue
                if phase >= 0:
                    stream.copy(phase, source).wait()

                    def put(values):
                        out[...] = values.astype(bf16)

                    stream.add(phase, source if phase == 0 else None, put)
                if phase + 1 < phases:
                    stream.copy(phase + 1, source).start()

    first_ada = 10
    ada_steps = 6 * ADA_PIECES

    @pl.when(step == first_ada)
    def _():
        ada.prepare()

    points = {when for plan in tail_plan(dims) for when in plan[3]} | set(gather_points)
    hub = first_ada + ADA_EARLY

    def point(now):
        doubling.events(now, gather_points)
        due(now)

    dispatch(step, {now: functools.partial(point, now) for now in points if now < hub})

    @pl.when(step == hub)
    def _():
        for later in sorted(points):
            if hub <= later <= gather_points[-1]:
                point(later)
        ada.late(sums_ref, phases)

    @pl.when(step >= first_ada)
    def _():
        number = step - first_ada
        ada.block(jnp.where(number < ADA_EARLY, number + ada_steps - ADA_EARLY, number - ADA_EARLY))

    final = first_ada + ada_steps - 1

    @pl.when(step == final)
    def _():
        ada.finish()

    @pl.when(step == final)
    def _():
        for later in sorted(points):
            if later > gather_points[-1]:
                point(later)
        for number in range(2):
            away(number).wait()
            stay(number).wait()


def back_step(
    projected_grad, qkv_weight, entry, latents, other_x, middle_grad, modulation, gain_rows,
    ada_weight, early, table, time_weight, class_table,
):
    patches, width = entry.shape
    dims = pair_axes()
    rows = width // lax.axis_size("img")
    sections = (0, 2, 1, 0, 1, 2)

    def section_of(step):
        place = jnp.int32(sections[-1])
        for number, section in enumerate(sections[:-1]):
            place = jnp.where(step == number, section, place)
        return place

    weight_section = lambda t: jnp.clip(t - 3, 0, 2)
    row_block = lambda t: lax.rem(jnp.clip(t - 6, 0, 3) + 2, 4)
    block = pl.BlockSpec((BACK_ROWS, width), lambda t: (row_block(t), 0))
    own = own_image(BACK_ROWS, width, lambda t: jnp.clip(t - 8, 0, 1))
    other = pl.BlockSpec((BACK_ROWS, width), lambda t: (jnp.clip(t - 6, 0, 1), 0))
    tails = [(rows, 384)] * 3 + [(rows, width // 2)]
    classes = class_table.shape[0]
    images = early.shape[0]
    time_rows = time_weight.shape[0] // lax.axis_size("img")
    ada_steps = 6 * ADA_PIECES
    half_steps = ada_steps // 2

    def ada_block(t):
        number = jnp.maximum(t - 10, 0)
        return jnp.where(number < ADA_EARLY, number + ada_steps - ADA_EARLY, number - ADA_EARLY)

    wide = (2,) * len(dims)
    scratch = [
        pltpu.VMEM((width, width), f32),
        pltpu.VMEM(wide + (rows, width), bf16),
        pltpu.VMEM(wide + (rows, width // 2), bf16),
        pltpu.VMEM((4, BACK_ROWS, width), bf16),
        pltpu.SemaphoreType.DMA((4,)),
        pltpu.SemaphoreType.DMA((2,)),
        pltpu.VMEM((classes, width), bf16),
        pltpu.VMEM((ada_steps, images, ADA_COLUMNS), f32),
        pltpu.VMEM((2, images, 128), f32),
        pltpu.VMEM((images, width), f32),
        pltpu.VMEM((images, width), f32),
        pltpu.VMEM((rows, images), bf16),
        pltpu.VMEM((time_rows, images), bf16),
        pltpu.VMEM((half_steps, rows, ADA_COLUMNS), f32),
        pltpu.SemaphoreType.DMA((2,)),
    ]
    for tail in tails:
        scratch += halving_scratch(dims, tail)
    return pl.pallas_call(
        functools.partial(back_kernel, dims),
        grid=(10 + ada_steps,),
        in_specs=[
            pl.BlockSpec((None, width, patches), lambda t: (section_of(t), 0, 0)),
            pl.BlockSpec((width, width), lambda t: (0, weight_section(t))),
            whole((patches, width)),
            own,
            other,
            block,
            whole((1, 6 * width)),
            whole((2, ADA_COLUMNS)),
            pl.BlockSpec((width, ADA_COLUMNS), lambda t: (0, ada_block(t))),
            whole(early.shape),
            whole(table.shape),
            whole(time_weight.shape),
            pl.BlockSpec(memory_space=pl.ANY),
        ],
        out_specs=[
            pl.BlockSpec(memory_space=pl.ANY),
            whole((rows, width)),
            whole((rows, width // 2)),
            whole((rows, 3 * width)),
            pl.BlockSpec((1, ADA_COLUMNS), lambda t: (0, ada_block(t))),
            whole((time_rows, width // 2)),
            whole((2, images, width)),
            whole((1, ADA_COLUMNS)),
        ],
        out_shape=[
            jax.ShapeDtypeStruct((2, patches // 2, width), bf16),
            jax.ShapeDtypeStruct((rows, width), bf16),
            jax.ShapeDtypeStruct((rows, width // 2), bf16),
            jax.ShapeDtypeStruct((rows, 3 * width), f32),
            jax.ShapeDtypeStruct((1, 6 * width), f32),
            jax.ShapeDtypeStruct((time_rows, width // 2), f32),
            jax.ShapeDtypeStruct((2, images, width), f32),
            jax.ShapeDtypeStruct((1, ADA_COLUMNS), f32),
        ],
        scratch_shapes=scratch
        + [pltpu.VMEM(wide + (2 * ADA_PIECES + 2, ADA_COLUMNS), f32)]
        + doubling_scratch(dims),
        compiler_params=params_of(collective_id=2, has_side_effects=True),
        cost_estimate=cost(12 * patches * width * width, 40e6),
        name="back",
    )(
        projected_grad, qkv_weight, entry, latents, other_x, middle_grad, modulation, gain_rows,
        ada_weight, early, table, time_weight, class_table,
    )


def last_kernel(rows_ref, result_ref, latents_ref, class_ref, result_out, latents_out):
    label = rows_ref[1, :, :1]
    first = pl.program_id(0) * class_ref.shape[0]
    place = lax.broadcasted_iota(jnp.int32, (label.shape[0], class_ref.shape[0]), 1) + first
    class_hot = (label == place.astype(f32)).astype(bf16)
    parts, left = [], rows_ref[0]
    for _ in range(3):
        parts.append(left.astype(bf16))
        left = left - parts[-1].astype(f32)
    class_ref[...] = dot(
        jnp.concatenate([class_hot] * 3, axis=0), jnp.concatenate(parts, axis=0), 0, 0
    )
    result_out[...] = result_ref[...]
    latents_out[...] = latents_ref[...]


def last_step(rows, classes, result, latents):
    width = rows.shape[2]
    block = 256
    steps = pl.cdiv(classes, block)
    images, half, _ = result.shape
    part = pl.BlockSpec((images, half // steps, width), lambda t: (0, t, 0))
    return pl.pallas_call(
        last_kernel,
        grid=(steps,),
        in_specs=[whole(rows.shape), part, part],
        out_specs=[pl.BlockSpec((block, width), lambda t: (t, 0)), part, part],
        out_shape=[
            jax.ShapeDtypeStruct((classes, width), f32),
            jax.ShapeDtypeStruct(result.shape, result.dtype),
            jax.ShapeDtypeStruct(latents.shape, latents.dtype),
        ],
        compiler_params=params_of(),
        cost_estimate=cost(6 * rows.shape[1] * classes * width, 14e6),
        name="last",
    )(rows, result, latents)


def pick(values, index):
    return lax.dynamic_index_in_dim(values, index, 0, keepdims=False)


def per_device_whole(
    latents,
    cotangent,
    labels,
    group_ids,
    group_logits,
    row_pos,
    col_pos,
    time_weight,
    class_table,
    ada_weight,
    ada_bias,
    qkv_weight,
    query_gain,
    key_gain,
    proj_weight,
    gateup_weight,
    down_weight,
):
    width = latents.shape[-1]
    bands = lax.axis_size("band")
    band_index = lax.axis_index("band")

    def from_other(values):
        return lax.ppermute(values, "band", [(0, 1), (1, 0)])

    other_x = from_other(pick(latents, 1 - band_index))
    away_c, _ = lax.optimization_barrier((pick(cotangent, 1 - band_index), other_x))
    other_c = from_other(away_c)
    places = jnp.stack([row_pos, col_pos], axis=1)
    places = jnp.concatenate([places, from_other(places)], axis=0)

    quarter = HD // 4
    frequency = jnp.exp(-math.log(10000.0) * jnp.arange(quarter, dtype=f32) / quarter)
    angles = frequency[:, None] * places.astype(f32).T[:, None, :]
    cosine, sine = jnp.cos(angles), jnp.sin(angles)
    cosine = jnp.concatenate([cosine[0], cosine[0], cosine[1], cosine[1]], axis=0)
    sine = jnp.concatenate([-sine[0], sine[0], -sine[1], sine[1]], axis=0)

    table = time_features(jax.nn.sigmoid(group_logits), FREQ // 2).astype(bf16)
    own_group = pick(group_ids, band_index)
    own_label = pick(labels, band_index)
    before = jnp.dot(
        pick(table, own_group)[None], time_weight, preferred_element_type=f32
    ) + pick(class_table, own_label)[None].astype(f32)
    condition = jax.nn.silu(before).astype(bf16)
    modulation = jnp.dot(condition, ada_weight, preferred_element_type=f32) + ada_bias
    gains = jnp.stack([query_gain, key_gain])[:, :, None]
    entry_one, heads, unit, factor = front(
        latents, other_x, modulation, qkv_weight, gains, cosine, sine
    )
    mixed, query = attend(heads)
    mixed = mixed.reshape(width, -1)
    attended, entry_two, fed_grad = middle_step(
        mixed, proj_weight, latents, other_x, cotangent, other_c, modulation
    )
    fed, entry_two_grad, grad_down, gateup_done, gateup_left, *carries = mlp(
        entry_two, fed_grad, gateup_weight, down_weight
    )
    codes = jnp.stack([own_label, own_group])[:, None].astype(f32)
    codes = jnp.pad(codes, ((0, 2), (0, ADA_COLUMNS - 1)))
    (
        result, middle_grad, projected_grad, gain_terms,
        sum_down, gateup_last, gateup_carried, sum_proj, modes_early,
    ) = core_step(
        fed, entry_two_grad, latents, other_x, cotangent, other_c, attended, mixed, proj_weight,
        modulation, codes, query, heads, unit, factor, gains, cosine, sine, grad_down, gateup_left,
        carries,
    )
    gain_rows = jnp.pad(jnp.sum(gain_terms, axis=2), ((0, 0), (0, 128 - HD))).reshape(1, -1)
    gain_rows = jnp.pad(gain_rows, ((0, 1), (0, ADA_COLUMNS - gain_rows.shape[1])))
    (
        grad_latents, qkv_pair, qkv_single, sum_ada, sum_bias, sum_time, before_rows, gain_sums,
    ) = back_step(
        projected_grad.reshape(3, width, -1), qkv_weight, entry_one, latents, other_x, middle_grad,
        modulation, gain_rows, ada_weight, modes_early.reshape((-1,) + modes_early.shape[-2:]), table,
        time_weight, class_table,
    )
    sum_bias = sum_bias.reshape(-1)
    sum_class, result, grad_latents = last_step(
        before_rows, class_table.shape[0], result, grad_latents
    )
    sum_query_gain, sum_key_gain = gain_sums[0, :HD], gain_sums[0, 128 : 128 + HD]
    sum_down = sum_down.reshape(-1, sum_down.shape[-1]).astype(f32)
    sum_proj = sum_proj.astype(f32)
    gateup_carried = gateup_carried.reshape((len(CARRIED), 2) + gateup_carried.shape[1:])
    gateup = jnp.concatenate([gateup_done, gateup_carried, gateup_last[None]], axis=0)
    sum_gateup = jnp.transpose(gateup, (2, 0, 1, 3)).reshape(gateup.shape[2], -1).astype(f32)
    sum_qkv = jnp.where(
        band_index == 0,
        jnp.concatenate([qkv_pair, qkv_single], axis=1),
        jnp.concatenate([qkv_single, qkv_pair], axis=1),
    ).astype(f32)
    return (
        result,
        grad_latents,
        sum_time,
        sum_class,
        sum_ada,
        sum_bias,
        sum_qkv,
        sum_query_gain,
        sum_key_gain,
        sum_proj,
        sum_gateup,
        sum_down,
    )


def per_device(latents, *others):
    if latents.shape[0] == lax.axis_size("band") == 2 and lax.axis_size("img") == 16:
        return per_device_whole(latents, *others)
    return per_device_banded(latents, *others)


def solution(mesh):
    return jax.shard_map(
        per_device,
        mesh=mesh,
        in_specs=(
            P("img", "band", None),
            P("img", "band", None),
            P("img"),
            P("img"),
            P(),
            P("band"),
            P("band"),
            P(),
            P(),
            P(),
            P(),
            P(),
            P(),
            P(),
            P(),
            P(),
            P(),
        ),
        out_specs=(
            P("img", "band", None),
            P("img", "band", None),
            P("img", "band"),
            P(),
            P("img", "band"),
            P(),
            P("img", "band"),
            P(),
            P(),
            P("img", "band"),
            P("img", "band"),
            P("img", "band"),
        ),
        check_vma=False,
    )
```
